32 devices in a mesh: grp: 8 (over z, x), dom: 4 (over y, core).
Axes of the slice: x: 2, y: 2, z: 4, core: 2. Of those that a mesh axis runs over, the one named last changes fastest.
Arguments:
- density: float32 [8, 256, 2048], P('grp', 'dom'), may hold values from -6 to 6
- diffusion: float32 [8, 256, 2048], P('grp', 'dom'), may hold values from 0.05 to 0.22
- drift_speed: float32 [8, 256, 2048], P('grp', 'dom'), may hold values from -0.3 to 0.3
- levels: int32 [8], P('grp'), may hold values from 5 to 8
- coefficient: int32 [8], P('grp'), may hold values from -2 to 2
Outputs:
- combined_field: float32 [8, 256, 2048], P('grp', 'dom')
The draws below stay inside these ranges and needn't reach their ends.
All inputs are finite; a program needn't handle non-finite values.
Results may differ from the reference program's by a relative error of at most 0.0003.
Values sent between devices are 32-bit elements; how exact they have to be, the bound alone decides.
No kernel may reach another device: no remote copies, remote signals or barrier semaphores. Data moves between devices by JAX's collectives and lax.ppermute only.
A program may use at most 64 MiB of HBM per device.

```python
import math
import jax
import jax.numpy as jnp
import numpy as np
from jax import lax

S = 256
STEPS = 4
R = 2048
G = 8


def set_ends(entries, stream_key, least, top_value):
    index_at = [jax.random.randint(jax.random.fold_in(stream_key, axis), (), 0, length) for axis, length in enumerate(entries.shape)]
    longest = entries.shape.index(max(entries.shape))
    next_to = index_at[:longest] + [(index_at[longest] + 1) % entries.shape[longest]] + index_at[longest + 1:]
    return entries.at[tuple(index_at)].set(least).at[tuple(next_to)].set(top_value)


def shard_levels(rng, dims, split, low, top_value):
    def one(dim, blocks):
        heights = jax.random.uniform(jax.random.fold_in(jax.random.fold_in(rng, 6), dim), (blocks,), jnp.float32, low / len(split), top_value / len(split))
        return jnp.repeat(jnp.exp(heights), dims[dim] // blocks).reshape((-1,) + (1,) * (len(dims) - dim - 1))

    factor_of = one(*split[0])
    for cut in split[1:]:
        factor_of = factor_of * one(*cut)
    return factor_of


def gaussian(rng, dims, spread, bound, pieces=(), kind=jnp.bfloat16):
    gain = shard_levels(rng, dims, pieces, -0.22, 0.18) if pieces else 1.0
    entries = jax.random.normal(rng, dims, jnp.float32) * spread * gain
    return jnp.minimum(jnp.maximum(entries, -bound), bound).astype(kind)


def setup_inputs(seed: int = 0) -> dict:
    seeds = jax.random.split(jax.random.key(seed), 6)
    density = gaussian(seeds[0], (G, S, R), 1.0, 6.0, ((0, 8), (1, 4)), jnp.float32)
    diffusion = jnp.clip(jnp.exp(math.log(0.22) - 1.48160452 * jax.random.uniform(seeds[1], (G, S, R), jnp.float32) ** shard_levels(seeds[1], (G, S, R), ((0, 8), (1, 4)), -0.2, 0.2)), 0.05, 0.22)
    drift_speed = jnp.clip(jax.random.uniform(seeds[2], (G, S, R), jnp.float32, -0.3, 0.3) * shard_levels(seeds[2], (G, S, R), ((0, 8), (1, 4)), -0.4, 0.0), -0.3, 0.3)
    levels = set_ends(jax.random.randint(seeds[3], (G,), 5, 9), jax.random.fold_in(seeds[3], 1), 5, 8).astype(jnp.int32)
    coefficient = set_ends(jax.random.randint(seeds[4], (G,), -2, 3), jax.random.fold_in(seeds[4], 1), -2, 2).astype(jnp.int32)
    return {"density": density, "diffusion": diffusion, "drift_speed": drift_speed, "levels": levels, "coefficient": coefficient}


def hier_tables(size):
    to_surplus = np.zeros((size, size), dtype=np.float32)
    to_nodal = np.zeros((size, size), dtype=np.float32)
    node_level = np.zeros((size,), dtype=np.int32)
    depth = size.bit_length() - 1
    spots = np.arange(1, size + 1, dtype=np.float32)
    for index in range(size):
        position = index + 1
        to_surplus[index, index] = 1.0
        if position == size:
            node_level[index] = 0
            to_nodal[:, index] = spots / size
            continue
        stride = 1
        zeros_count = 0
        while position % (2 * stride) == 0:
            stride = stride * 2
            zeros_count = zeros_count + 1
        node_level[index] = depth - zeros_count
        to_nodal[:, index] = np.maximum(0.0, 1.0 - np.abs(spots - position) / stride)
        if position - stride > 0:
            to_surplus[index, position - stride - 1] -= 0.5
        if position + stride <= size:
            to_surplus[index, position + stride - 1] -= 0.5
    return to_surplus, to_nodal, node_level


def advance(state, diffuse, drifts):
    padded = jnp.pad(state, 1)
    above_cell = padded[2:, 1:-1]
    below_cell = padded[:-2, 1:-1]
    right_cell = padded[1:-1, 2:]
    left_cell = padded[1:-1, :-2]
    return state + diffuse * (above_cell + below_cell + right_cell + left_cell - 4.0 * state) - 0.5 * drifts * (above_cell - below_cell)


def reference(density, diffusion, drift_speed, levels, coefficient):
    to_surplus, to_nodal, node_level = hier_tables(S)
    to_surplus = jnp.asarray(to_surplus)
    to_nodal = jnp.asarray(to_nodal)
    node_level = jnp.asarray(node_level)

    def one_grid(items):
        state, diffuse, drifts, level_one, coef_one = items
        for sweep in range(STEPS):
            state = advance(state, diffuse, drifts)
        surplus = jnp.dot(to_surplus, state, precision=lax.Precision.HIGHEST, preferred_element_type=jnp.float32)
        member_mask = (node_level <= level_one).astype(jnp.float32)
        return surplus * (member_mask * coef_one.astype(jnp.float32))[:, None]

    weighted = lax.map(one_grid, (density, diffusion, drift_speed, levels, coefficient))
    total = jnp.sum(weighted, axis=0)

    def back_grid(level_one):
        member_mask = (node_level <= level_one).astype(jnp.float32)
        return jnp.dot(to_nodal, total * member_mask[:, None], precision=lax.Precision.HIGHEST, preferred_element_type=jnp.float32)

    return lax.map(back_grid, levels)
```

```python
import functools

import jax
import jax.numpy as jnp
from jax import lax
from jax.experimental import pallas as pl
from jax.experimental.pallas import tpu as pltpu
from jax.sharding import PartitionSpec as P

STEPS = 4
LANES = 128
TILE = 8
VMEM_LIMIT = 40 * 1024 * 1024


def lane_ids(shape):
    return lax.broadcasted_iota(jnp.int32, shape, 1)


def row_in_tile(shape):
    return lax.broadcasted_iota(jnp.int32, shape, 0) % TILE


def run_kernel(
    rows, strips, per_chunk, level_ref, coef_ref, dens_ref, diff_ref, drift_ref, up_ref, dn_ref,
    out_ref, state_a, state_b, center, above_c, below_c, side
):
    tall = rows + 2 * TILE
    lanes = lane_ids((tall, LANES))
    zeros = jnp.zeros((tall, LANES), jnp.float32)
    for buf in (state_a, state_b):
        buf[0] = zeros
        buf[strips + 1] = zeros

    def columns(j):
        return pl.ds(pl.multiple_of(j * LANES, LANES), LANES)

    def first_state(j):
        at = columns(j)
        return jnp.concatenate([up_ref[0:TILE, at], dens_ref[:, at], dn_ref[0:TILE, at]], axis=0)

    def coefficients(j):
        at = columns(j)
        up, dn = up_ref[TILE:, at], dn_ref[TILE:, at]
        diffuse = jnp.concatenate([up, diff_ref[:, at], dn], axis=0)
        drifts = jnp.concatenate(
            [pltpu.roll(up, 4, 0), drift_ref[:, at], pltpu.roll(dn, 4, 0)], axis=0
        )
        half = 0.5 * drifts
        return 1.0 - 4.0 * diffuse, diffuse - half, diffuse + half, diffuse

    def sweep(load, coefs, emit):
        def body(j, carry):
            cur, right_prev, left_cur = carry
            nxt = load(j + 1)
            left_next = pltpu.roll(nxt, LANES - 1, 1)
            right_cur = pltpu.roll(cur, 1, 1)
            left = jnp.where(lanes == 0, right_prev, right_cur)
            right = jnp.where(lanes == LANES - 1, left_next, left_cur)
            above = pltpu.roll(cur, tall - 1, 0)
            below = pltpu.roll(cur, 1, 0)
            c0, ca, cb, cs = coefs(j)
            emit(j, c0 * cur + ca * above + cb * below + cs * (left + right))
            return nxt, right_cur, left_next

        cur = load(0)
        lax.fori_loop(0, strips, body, (cur, zeros, pltpu.roll(cur, LANES - 1, 1)), unroll=2)

    def load_first(j):
        strip = first_state(jnp.minimum(j, strips - 1))
        return jnp.where(j < strips, strip, zeros)

    def coefs_first(j):
        c0, ca, cb, cs = coefficients(j)
        center[j], above_c[j], below_c[j], side[j] = c0, ca, cb, cs
        return c0, ca, cb, cs

    def coefs_kept(j):
        return center[j], above_c[j], below_c[j], side[j]

    def to(buf):
        def emit(j, value):
            buf[j + 1] = value

        return emit

    coef = coef_ref[0].astype(jnp.float32)
    weight = [jnp.where(level_ref[0] >= level, coef, 0.0) for level in (6, 7, 8)]
    row = row_in_tile((tall, LANES))
    is8, is7, is6 = row % 2 == 0, row % 4 == 1, row == 3
    scale = jnp.where(is8, weight[2], jnp.where(is7, weight[1], jnp.where(is6, weight[0], coef)))
    halves = jnp.where(row == 7, 0.0, 0.5)

    def surplus(j, value):
        def both(shift):
            return pltpu.roll(value, shift, 0) + pltpu.roll(value, tall - shift, 0)

        ends = jnp.where(is8, both(1), jnp.where(is7, both(2), both(4)))
        weighted = scale * (value - halves * ends)
        chunk, part = j // per_chunk, lax.rem(j, per_chunk)
        out_ref[chunk, pl.ds(pl.multiple_of(part * rows, TILE), rows), :] = weighted[
            TILE : TILE + rows
        ]
        out_ref[chunk, pl.ds(per_chunk * rows + part, 1), :] = coef * value[TILE - 1 : TILE]

    sweep(load_first, coefs_first, to(state_a))
    src, dst = state_a, state_b
    for step in range(1, STEPS):
        emit = to(dst) if step < STEPS - 1 else surplus
        sweep(lambda j, src=src: src[j + 1], coefs_kept, emit)
        src, dst = dst, src


def sum_kernel(parts_ref, out_ref):
    total = parts_ref[0]
    for g in range(1, parts_ref.shape[0]):
        total = total + parts_ref[g]
    for g in range(out_ref.shape[0]):
        out_ref[g] = total


def nodal_kernel(rows, strips, per_chunk, level_ref, total_ref, out_ref):
    level = level_ref[0]
    keep = [jnp.where(level >= at, 1.0, 0.0) for at in (6, 7, 8)]
    row = row_in_tile((TILE, LANES))
    place = (row + 1).astype(jnp.float32)
    from_next = place / TILE
    from_prev = 1.0 - from_next
    hat6 = keep[0] * jnp.minimum(place, TILE - place) * 0.25
    fine = jnp.where(row >= 4, place - 4, place)
    hat7 = keep[1] * jnp.minimum(fine, 4.0 - fine) * 0.5
    hat8 = jnp.where(row % 2 == 0, keep[2], 0.0)

    def body(j, _):
        chunk, part = j // per_chunk, lax.rem(j, per_chunk)
        top = pl.multiple_of(part * rows, TILE)
        prev = total_ref[chunk, pl.ds(per_chunk * rows + part, 1), :]
        strip = total_ref[chunk, pl.ds(top, rows), :]
        tiles = []
        for t in range(rows // TILE):
            tile = strip[t * TILE : (t + 1) * TILE]
            last = tile[7:8]
            mid = jnp.where(row < 4, tile[1:2], tile[5:6])
            tiles.append(
                from_prev * prev + from_next * last + hat6 * tile[3:4] + hat7 * mid + hat8 * tile
            )
            prev = last
        at = pl.ds(pl.multiple_of(j * LANES, LANES), LANES)
        out_ref[:, at] = jnp.concatenate(tiles, axis=0)
        return 0

    lax.fori_loop(0, strips, body, 0, unroll=2)


def call(kernel, out_shape, operands, in_smem, scratch=()):
    specs = [
        pl.BlockSpec(memory_space=pltpu.SMEM if k < in_smem else pltpu.VMEM)
        for k in range(len(operands))
    ]
    return pl.pallas_call(
        kernel,
        out_shape=jax.ShapeDtypeStruct(out_shape, jnp.float32),
        in_specs=specs,
        out_specs=pl.BlockSpec(memory_space=pltpu.VMEM),
        scratch_shapes=list(scratch),
        compiler_params=pltpu.CompilerParams(vmem_limit_bytes=VMEM_LIMIT),
    )(*operands)


def on_device(density, diffusion, drift_speed, levels, coefficient):
    state, diffuse, drifts = density[0], diffusion[0], drift_speed[0]
    rows, cols = state.shape
    doms, grids = lax.axis_size("dom"), lax.axis_size("grp")
    strips = cols // LANES
    per_chunk = strips // grids
    tall = rows + 2 * TILE
    chunk_rows = per_chunk * rows + -(-per_chunk // TILE) * TILE

    up = [(i, i + 1) for i in range(doms - 1)]
    down = [(j, i) for i, j in up]
    to_next = jnp.concatenate([state[-8:], drifts[-4:], diffuse[-4:]], axis=0)
    to_prev = jnp.concatenate([state[:8], diffuse[:4], drifts[:4]], axis=0)
    before = lax.ppermute(to_next, "dom", up)
    after = lax.ppermute(to_prev, "dom", down)

    packed = (grids, chunk_rows, LANES)
    weighted = call(
        functools.partial(run_kernel, rows, strips, per_chunk),
        packed,
        (levels, coefficient, state, diffuse, drifts, before, after),
        2,
        [pltpu.VMEM((strips + 2, tall, LANES), jnp.float32)] * 2
        + [pltpu.VMEM((strips, tall, LANES), jnp.float32)] * 4,
    )
    parts = lax.all_to_all(weighted, "grp", split_axis=0, concat_axis=0, tiled=True)
    spread = call(sum_kernel, packed, (parts,), 0)
    total = lax.all_to_all(spread, "grp", split_axis=0, concat_axis=0, tiled=True)
    nodal = call(
        functools.partial(nodal_kernel, rows, strips, per_chunk), (rows, cols), (levels, total), 1
    )
    return nodal[None]


def solution(mesh):
    return jax.shard_map(
        on_device,
        mesh=mesh,
        in_specs=(
            P("grp", "dom", None),
            P("grp", "dom", None),
            P("grp", "dom", None),
            P("grp"),
            P("grp"),
        ),
        out_specs=P("grp", "dom", None),
        check_vma=False,
    )
```

```python
import functools

import jax
import jax.numpy as jnp
from jax import lax
from jax.experimental import pallas as pl
from jax.experimental.pallas import tpu as pltpu
from jax.sharding import PartitionSpec as P

STEPS = 4
LANES = 128
SQUARE = 4
TILE = 8
VMEM_LIMIT = 40 * 1024 * 1024


def lane_ids(shape):
    return lax.broadcasted_iota(jnp.int32, shape, 1)


def row_in_tile(shape):
    return lax.broadcasted_iota(jnp.int32, shape, 0) % TILE


def run_kernel(
    rows, strips, per_chunk, level_ref, coef_ref, dens_ref, diff_ref, drift_ref, up_ref, dn_ref,
    out_ref, state_a, state_b, center, above_c, below_c, side
):
    tall = rows + 2 * TILE
    lanes = lane_ids((tall, LANES))
    zeros = jnp.zeros((tall, LANES), jnp.float32)
    for buf in (state_a, state_b):
        buf[0] = zeros
        buf[strips + 1] = zeros

    def columns(j):
        return pl.ds(pl.multiple_of(j * LANES, LANES), LANES)

    def first_state(j):
        at = columns(j)
        return jnp.concatenate([up_ref[0:TILE, at], dens_ref[:, at], dn_ref[0:TILE, at]], axis=0)

    def coefficients(j):
        at = columns(j)
        up, dn = up_ref[TILE:, at], dn_ref[TILE:, at]
        diffuse = jnp.concatenate([up, diff_ref[:, at], dn], axis=0)
        drifts = jnp.concatenate(
            [pltpu.roll(up, 4, 0), drift_ref[:, at], pltpu.roll(dn, 4, 0)], axis=0
        )
        half = 0.5 * drifts
        return 1.0 - 4.0 * diffuse, diffuse - half, diffuse + half, diffuse

    def sweep(load, coefs, emit):
        def body(j, carry):
            cur, right_prev, left_cur = carry
            nxt = load(j + 1)
            left_next = pltpu.roll(nxt, LANES - 1, 1)
            right_cur = pltpu.roll(cur, 1, 1)
            left = jnp.where(lanes == 0, right_prev, right_cur)
            right = jnp.where(lanes == LANES - 1, left_next, left_cur)
            above = pltpu.roll(cur, tall - 1, 0)
            below = pltpu.roll(cur, 1, 0)
            c0, ca, cb, cs = coefs(j)
            emit(j, c0 * cur + ca * above + cb * below + cs * (left + right))
            return nxt, right_cur, left_next

        cur = load(0)
        lax.fori_loop(0, strips, body, (cur, zeros, pltpu.roll(cur, LANES - 1, 1)), unroll=2)

    def load_first(j):
        strip = first_state(jnp.minimum(j, strips - 1))
        return jnp.where(j < strips, strip, zeros)

    def coefs_first(j):
        c0, ca, cb, cs = coefficients(j)
        center[j], above_c[j], below_c[j], side[j] = c0, ca, cb, cs
        return c0, ca, cb, cs

    def coefs_kept(j):
        return center[j], above_c[j], below_c[j], side[j]

    def to(buf):
        def emit(j, value):
            buf[j + 1] = value

        return emit

    coef = coef_ref[0].astype(jnp.float32)
    weight = [jnp.where(level_ref[0] >= level, coef, 0.0) for level in (6, 7, 8)]
    row = row_in_tile((tall, LANES))
    is8, is7, is6 = row % 2 == 0, row % 4 == 1, row == 3
    scale = jnp.where(is8, weight[2], jnp.where(is7, weight[1], jnp.where(is6, weight[0], coef)))
    halves = jnp.where(row == 7, 0.0, 0.5)

    def surplus(j, value):
        def both(shift):
            return pltpu.roll(value, shift, 0) + pltpu.roll(value, tall - shift, 0)

        ends = jnp.where(is8, both(1), jnp.where(is7, both(2), both(4)))
        weighted = scale * (value - halves * ends)
        chunk, part = j // per_chunk, lax.rem(j, per_chunk)
        out_ref[chunk, pl.ds(pl.multiple_of(part * rows, TILE), rows), :] = weighted[
            TILE : TILE + rows
        ]
        out_ref[chunk, pl.ds(per_chunk * rows + part, 1), :] = coef * value[TILE - 1 : TILE]

    sweep(load_first, coefs_first, to(state_a))
    src, dst = state_a, state_b
    for step in range(1, STEPS):
        emit = to(dst) if step < STEPS - 1 else surplus
        sweep(lambda j, src=src: src[j + 1], coefs_kept, emit)
        src, dst = dst, src


def sum_kernel(parts_ref, out_ref):
    total = parts_ref[0]
    for g in range(1, parts_ref.shape[0]):
        total = total + parts_ref[g]
    out_ref[...] = total


def spread_kernel(mine_ref, theirs_ref, out_ref):
    total = mine_ref[...] + theirs_ref[...]
    for g in range(out_ref.shape[0]):
        out_ref[g] = total


def nodal_kernel(rows, strips, per_chunk, level_ref, total_ref, out_ref):
    level = level_ref[0]
    keep = [jnp.where(level >= at, 1.0, 0.0) for at in (6, 7, 8)]
    row = row_in_tile((TILE, LANES))
    place = (row + 1).astype(jnp.float32)
    from_next = place / TILE
    from_prev = 1.0 - from_next
    hat6 = keep[0] * jnp.minimum(place, TILE - place) * 0.25
    fine = jnp.where(row >= 4, place - 4, place)
    hat7 = keep[1] * jnp.minimum(fine, 4.0 - fine) * 0.5
    hat8 = jnp.where(row % 2 == 0, keep[2], 0.0)

    def body(j, _):
        chunk, part = j // per_chunk, lax.rem(j, per_chunk)
        top = pl.multiple_of(part * rows, TILE)
        prev = total_ref[chunk, pl.ds(per_chunk * rows + part, 1), :]
        strip = total_ref[chunk, pl.ds(top, rows), :]
        tiles = []
        for t in range(rows // TILE):
            tile = strip[t * TILE : (t + 1) * TILE]
            last = tile[7:8]
            mid = jnp.where(row < 4, tile[1:2], tile[5:6])
            tiles.append(
                from_prev * prev + from_next * last + hat6 * tile[3:4] + hat7 * mid + hat8 * tile
            )
            prev = last
        at = pl.ds(pl.multiple_of(j * LANES, LANES), LANES)
        out_ref[:, at] = jnp.concatenate(tiles, axis=0)
        return 0

    lax.fori_loop(0, strips, body, 0, unroll=2)


def call(kernel, out_shape, operands, in_smem, scratch=()):
    specs = [
        pl.BlockSpec(memory_space=pltpu.SMEM if k < in_smem else pltpu.VMEM)
        for k in range(len(operands))
    ]
    return pl.pallas_call(
        kernel,
        out_shape=jax.ShapeDtypeStruct(out_shape, jnp.float32),
        in_specs=specs,
        out_specs=pl.BlockSpec(memory_space=pltpu.VMEM),
        scratch_shapes=list(scratch),
        compiler_params=pltpu.CompilerParams(vmem_limit_bytes=VMEM_LIMIT),
    )(*operands)


def on_device(density, diffusion, drift_speed, levels, coefficient):
    state, diffuse, drifts = density[0], diffusion[0], drift_speed[0]
    rows, cols = state.shape
    doms, grids = lax.axis_size("dom"), lax.axis_size("grp")
    strips = cols // LANES
    squares = [list(range(q, q + SQUARE)) for q in range(0, grids, SQUARE)]
    per_chunk = strips // SQUARE
    tall = rows + 2 * TILE
    chunk_rows = per_chunk * rows + -(-per_chunk // TILE) * TILE

    up = [(i, i + 1) for i in range(doms - 1)]
    down = [(j, i) for i, j in up]
    to_next = jnp.concatenate([state[-8:], drifts[-4:], diffuse[-4:]], axis=0)
    to_prev = jnp.concatenate([state[:8], diffuse[:4], drifts[:4]], axis=0)
    before = lax.ppermute(to_next, "dom", up)
    after = lax.ppermute(to_prev, "dom", down)

    packed = (SQUARE, chunk_rows, LANES)
    weighted = call(
        functools.partial(run_kernel, rows, strips, per_chunk),
        packed,
        (levels, coefficient, state, diffuse, drifts, before, after),
        2,
        [pltpu.VMEM((strips + 2, tall, LANES), jnp.float32)] * 2
        + [pltpu.VMEM((strips, tall, LANES), jnp.float32)] * 4,
    )
    exchange = functools.partial(
        lax.all_to_all,
        axis_name="grp",
        split_axis=0,
        concat_axis=0,
        axis_index_groups=squares,
        tiled=True,
    )
    total = call(sum_kernel, packed[1:], (exchange(weighted),), 0)
    apart = SQUARE
    while apart < grids:
        swap = [(g, g ^ apart) for g in range(grids)]
        other = lax.ppermute(total, "grp", swap)
        apart *= 2
        if apart < grids:
            total = total + other
    spread = call(spread_kernel, packed, (total, other), 0)
    total = exchange(spread)
    nodal = call(
        functools.partial(nodal_kernel, rows, strips, per_chunk), (rows, cols), (levels, total), 1
    )
    return nodal[None]


def solution(mesh):
    return jax.shard_map(
        on_device,
        mesh=mesh,
        in_specs=(
            P("grp", "dom", None),
            P("grp", "dom", None),
            P("grp", "dom", None),
            P("grp"),
            P("grp"),
        ),
        out_specs=P("grp", "dom", None),
        check_vma=False,
    )
```

```python
import functools

import jax
import jax.numpy as jnp
from jax import lax
from jax.experimental import pallas as pl
from jax.experimental.pallas import tpu as pltpu
from jax.sharding import PartitionSpec as P

STEPS = 4
LANES = 128
SQUARE = 4
TILE = 8
VMEM_LIMIT = 40 * 1024 * 1024


def lane_ids(shape):
    return lax.broadcasted_iota(jnp.int32, shape, 1)


def row_in_tile(shape):
    return lax.broadcasted_iota(jnp.int32, shape, 0) % TILE


def run_kernel(
    rows, strips, per_chunk, me_ref, level_ref, coef_ref, dens_ref, diff_ref, drift_ref, up_ref,
    dn_ref, own_ref, one_ref, two_ref, three_ref, state_a, state_b, center, above_c, below_c, side
):
    tall = rows + 2 * TILE
    lanes = lane_ids((tall, LANES))
    zeros = jnp.zeros((tall, LANES), jnp.float32)
    for buf in (state_a, state_b):
        buf[0] = zeros
        buf[strips + 1] = zeros

    def columns(j):
        return pl.ds(pl.multiple_of(j * LANES, LANES), LANES)

    def first_state(j):
        at = columns(j)
        return jnp.concatenate([up_ref[0:TILE, at], dens_ref[:, at], dn_ref[0:TILE, at]], axis=0)

    def coefficients(j):
        at = columns(j)
        up, dn = up_ref[TILE:, at], dn_ref[TILE:, at]
        diffuse = jnp.concatenate([up, diff_ref[:, at], dn], axis=0)
        drifts = jnp.concatenate(
            [pltpu.roll(up, 4, 0), drift_ref[:, at], pltpu.roll(dn, 4, 0)], axis=0
        )
        half = 0.5 * drifts
        return 1.0 - 4.0 * diffuse, diffuse - half, diffuse + half, diffuse

    def sweep(load, coefs, emit):
        def body(j, carry):
            cur, right_prev, left_cur = carry
            nxt = load(j + 1)
            left_next = pltpu.roll(nxt, LANES - 1, 1)
            right_cur = pltpu.roll(cur, 1, 1)
            left = jnp.where(lanes == 0, right_prev, right_cur)
            right = jnp.where(lanes == LANES - 1, left_next, left_cur)
            above = pltpu.roll(cur, tall - 1, 0)
            below = pltpu.roll(cur, 1, 0)
            c0, ca, cb, cs = coefs(j)
            emit(j, c0 * cur + ca * above + cb * below + cs * (left + right))
            return nxt, right_cur, left_next

        cur = load(0)
        lax.fori_loop(0, strips, body, (cur, zeros, pltpu.roll(cur, LANES - 1, 1)), unroll=2)

    def load_first(j):
        strip = first_state(jnp.minimum(j, strips - 1))
        return jnp.where(j < strips, strip, zeros)

    def coefs_first(j):
        c0, ca, cb, cs = coefficients(j)
        center[j], above_c[j], below_c[j], side[j] = c0, ca, cb, cs
        return c0, ca, cb, cs

    def coefs_kept(j):
        return center[j], above_c[j], below_c[j], side[j]

    def to(buf):
        def emit(j, value):
            buf[j + 1] = value

        return emit

    coef = coef_ref[0].astype(jnp.float32)
    weight = [jnp.where(level_ref[0] >= level, coef, 0.0) for level in (6, 7, 8)]
    row = row_in_tile((tall, LANES))
    is8, is7, is6 = row % 2 == 0, row % 4 == 1, row == 3
    scale = jnp.where(is8, weight[2], jnp.where(is7, weight[1], jnp.where(is6, weight[0], coef)))
    halves = jnp.where(row == 7, 0.0, 0.5)

    def surplus(j, value):
        def both(shift):
            return pltpu.roll(value, shift, 0) + pltpu.roll(value, tall - shift, 0)

        ends = jnp.where(is8, both(1), jnp.where(is7, both(2), both(4)))
        weighted = scale * (value - halves * ends)
        away = (j // per_chunk) ^ me_ref[0]
        part = lax.rem(j, per_chunk)
        for k, ref in enumerate((own_ref, one_ref, two_ref, three_ref)):

            @pl.when(away == k)
            def _(ref=ref):
                at = pl.ds(pl.multiple_of(part * rows, TILE), rows)
                ref[at, :] = weighted[TILE : TILE + rows]
                ref[pl.ds(per_chunk * rows + part, 1), :] = coef * value[TILE - 1 : TILE]

    sweep(load_first, coefs_first, to(state_a))
    src, dst = state_a, state_b
    for step in range(1, STEPS):
        emit = to(dst) if step < STEPS - 1 else surplus
        sweep(lambda j, src=src: src[j + 1], coefs_kept, emit)
        src, dst = dst, src


def sum_kernel(*refs):
    *parts, out_ref = refs
    total = parts[0][...]
    for part in parts[1:]:
        total = total + part[...]
    out_ref[...] = total


def nodal_kernel(rows, per_chunk, me_ref, level_ref, *refs):
    *totals, out_ref = refs
    level = level_ref[0]
    keep = [jnp.where(level >= at, 1.0, 0.0) for at in (6, 7, 8)]
    row = row_in_tile((TILE, LANES))
    place = (row + 1).astype(jnp.float32)
    from_next = place / TILE
    from_prev = 1.0 - from_next
    hat6 = keep[0] * jnp.minimum(place, TILE - place) * 0.25
    fine = jnp.where(row >= 4, place - 4, place)
    hat7 = keep[1] * jnp.minimum(fine, 4.0 - fine) * 0.5
    hat8 = jnp.where(row % 2 == 0, keep[2], 0.0)

    for away, total_ref in enumerate(totals):
        first = (me_ref[0] ^ away) * per_chunk

        def body(part, _, total_ref=total_ref, first=first):
            prev = total_ref[pl.ds(per_chunk * rows + part, 1), :]
            strip = total_ref[pl.ds(pl.multiple_of(part * rows, TILE), rows), :]
            tiles = []
            for t in range(rows // TILE):
                tile = strip[t * TILE : (t + 1) * TILE]
                last = tile[7:8]
                mid = jnp.where(row < 4, tile[1:2], tile[5:6])
                spans = from_prev * prev + from_next * last
                tiles.append(spans + hat6 * tile[3:4] + hat7 * mid + hat8 * tile)
                prev = last
            at = pl.ds(pl.multiple_of((first + part) * LANES, LANES), LANES)
            out_ref[:, at] = jnp.concatenate(tiles, axis=0)
            return 0

        lax.fori_loop(0, per_chunk, body, 0, unroll=2)


def call(kernel, out_shapes, operands, in_smem, scratch=()):
    specs = [
        pl.BlockSpec(memory_space=pltpu.SMEM if k < in_smem else pltpu.VMEM)
        for k in range(len(operands))
    ]
    return pl.pallas_call(
        kernel,
        out_shape=[jax.ShapeDtypeStruct(shape, jnp.float32) for shape in out_shapes],
        in_specs=specs,
        out_specs=[pl.BlockSpec(memory_space=pltpu.VMEM) for _ in out_shapes],
        scratch_shapes=list(scratch),
        compiler_params=pltpu.CompilerParams(vmem_limit_bytes=VMEM_LIMIT),
    )(*operands)


def on_device(density, diffusion, drift_speed, levels, coefficient):
    state, diffuse, drifts = density[0], diffusion[0], drift_speed[0]
    rows, cols = state.shape
    doms, grids = lax.axis_size("dom"), lax.axis_size("grp")
    strips = cols // LANES
    me = lax.rem(lax.axis_index("grp"), SQUARE).astype(jnp.int32)[None]
    per_chunk = strips // SQUARE
    tall = rows + 2 * TILE
    chunk_rows = per_chunk * rows + -(-per_chunk // TILE) * TILE

    up = [(i, i + 1) for i in range(doms - 1)]
    down = [(j, i) for i, j in up]
    to_next = jnp.concatenate([state[-8:], drifts[-4:], diffuse[-4:]], axis=0)
    to_prev = jnp.concatenate([state[:8], diffuse[:4], drifts[:4]], axis=0)
    before = lax.ppermute(to_next, "dom", up)
    after = lax.ppermute(to_prev, "dom", down)

    packed = (chunk_rows, LANES)
    own, *others = call(
        functools.partial(run_kernel, rows, strips, per_chunk),
        [packed] * SQUARE,
        (me, levels, coefficient, state, diffuse, drifts, before, after),
        3,
        [pltpu.VMEM((strips + 2, tall, LANES), jnp.float32)] * 2
        + [pltpu.VMEM((strips, tall, LANES), jnp.float32)] * 4,
    )

    def swap(array, apart):
        return lax.ppermute(array, "grp", [(g, g ^ apart) for g in range(grids)])

    theirs = [swap(array, apart) for apart, array in enumerate(others, 1)]
    (total,) = call(sum_kernel, [packed], (own, *theirs), 0)
    apart = SQUARE
    while apart < grids:
        (total,) = call(sum_kernel, [packed], (total, swap(total, apart)), 0)
        apart *= 2
    totals = [total] + [swap(total, apart) for apart in range(1, SQUARE)]
    (nodal,) = call(
        functools.partial(nodal_kernel, rows, per_chunk), [(rows, cols)], (me, levels, *totals), 2
    )
    return nodal[None]


def solution(mesh):
    return jax.shard_map(
        on_device,
        mesh=mesh,
        in_specs=(
            P("grp", "dom", None),
            P("grp", "dom", None),
            P("grp", "dom", None),
            P("grp"),
            P("grp"),
        ),
        out_specs=P("grp", "dom", None),
        check_vma=False,
    )
```

```python
import functools

import jax
import jax.numpy as jnp
from jax import lax
from jax.experimental import pallas as pl
from jax.experimental.pallas import tpu as pltpu
from jax.sharding import PartitionSpec as P

STEPS = 4
LANES = 128
TILE = 8
HALF = TILE // 2
SLAB = 4 * TILE
SQUARE = 4
VMEM_LIMIT = 40 * 1024 * 1024


def tiles_of(block):
    rows, cols = block.shape
    return block.reshape(rows // TILE, TILE, cols // LANES, LANES).transpose(0, 2, 1, 3)


def block_of(tiles):
    many, strips = tiles.shape[:2]
    return tiles.transpose(0, 2, 1, 3).reshape(many * TILE, strips * LANES)


def flat(ref):
    return ref.reshape(ref.size // LANES, LANES)


def spaced(first, count, stride):
    return pl.ds(first, count, stride=stride) if count > 1 else pl.ds(first, 1)


def roll_rows(value, shift):
    count = value.shape[0]
    return pltpu.roll(value, shift % count, 0) if count > 1 else value


def per_strip(strips, body, unroll):
    def step(j, carry):
        body(j)
        return carry

    lax.fori_loop(0, strips, step, 0, unroll=unroll)


def advance(strips, classes, source, coefs, emit, unroll):
    shape = source.shape[2:]
    lanes = lax.broadcasted_iota(jnp.int32, shape, 1)
    center, above_c, below_c, side = coefs

    def body(j, carry):
        cur, right_prev, left_cur = carry
        nxt = [source[j + 2, t] for t in range(classes)]
        left_next = [pltpu.roll(x, LANES - 1, 1) for x in nxt]
        right_cur = [pltpu.roll(x, 1, 1) for x in cur]
        above = cur[1:] + [roll_rows(cur[0], -1)]
        below = [roll_rows(cur[-1], 1)] + cur[:-1]
        new = []
        for t in range(classes):
            left = jnp.where(lanes == 0, right_prev[t], right_cur[t])
            right = jnp.where(lanes == LANES - 1, left_next[t], left_cur[t])
            new.append(
                center[j, t] * cur[t]
                + above_c[j, t] * above[t]
                + below_c[j, t] * below[t]
                + side[j, t] * (left + right)
            )
        emit(j, new)
        return nxt, right_cur, left_next

    cur = [source[1, t] for t in range(classes)]
    zeros = [jnp.zeros(shape, jnp.float32)] * classes
    first = (cur, zeros, [pltpu.roll(x, LANES - 1, 1) for x in cur])
    lax.fori_loop(0, strips, body, first, unroll=unroll)


def run_steps(strips, classes, load, buffers, coefs, finish, unroll):
    center, above_c, below_c, side = coefs
    for buf in buffers:
        for edge in (0, strips + 1):
            buf[edge] = jnp.zeros(buf.shape[1:], jnp.float32)

    def begin(j):
        for t in range(classes):
            state, diffuse, drifts = load(j, t)
            half = 0.5 * drifts
            buffers[0][j + 1, t] = state
            center[j, t] = 1.0 - 4.0 * diffuse
            above_c[j, t] = diffuse - half
            below_c[j, t] = diffuse + half
            side[j, t] = diffuse

    per_strip(strips, begin, unroll)
    for step in range(STEPS):
        source, target = buffers[step % 2], buffers[1 - step % 2]

        def keep(j, new, target=target):
            for t in range(classes):
                target[j + 1, t] = new[t]

        emit = keep if step < STEPS - 1 else finish
        advance(strips, classes, source, coefs, emit, unroll)


def pack_kernel(parity_ref, dens_ref, diff_ref, drift_ref, far_ref, near_ref, ends_ref):
    many, strips = dens_ref.shape[:2]
    odd = parity_ref[0] == 1
    upper = lax.broadcasted_iota(jnp.int32, (TILE, LANES), 0) < HALF

    def body(j):
        refs = (dens_ref, diff_ref, drift_ref)
        heads, tails = ([ref[at, j] for ref in refs] for at in (0, many - 1))
        for k in range(3):
            ends_ref[k, 0, j], ends_ref[k, 1, j] = heads[k], tails[k]
        mix_next = jnp.where(upper, pltpu.roll(tails[2], HALF, 0), tails[1])
        mix_prev = jnp.where(upper, heads[1], pltpu.roll(heads[2], HALF, 0))
        to_next, to_prev = (tails[0], mix_next), (heads[0], mix_prev)
        for k in range(2):
            at = pl.ds(k * TILE, TILE)
            far_ref[j, at] = jnp.where(odd, to_next[k], to_prev[k])
            near_ref[j, at] = jnp.where(odd, to_prev[k], to_next[k])

    per_strip(strips, body, 4)


def inner_kernel(dens_ref, diff_ref, drift_ref, out_ref, state_a, state_b, *coefs):
    many, strips = dens_ref.shape[:2]
    refs = [flat(ref) for ref in (dens_ref, diff_ref, drift_ref)]

    def load(j, t):
        at = spaced(j * TILE + t, many, strips * TILE)
        return [ref[at, :] for ref in refs]

    def finish(j, new):
        for t in range(TILE):
            out_ref[j, t] = new[t]

    run_steps(strips, TILE, load, (state_a, state_b), coefs, finish, 2)


def edge_kernel(
    per_chunk, depth, parity_ref, me_ref, level_ref, coef_ref, ends_ref, inner_ref, far_ref,
    near_ref, own_ref, one_ref, two_ref, three_ref, slab, state_a, state_b, *coefs
):
    strips, _, many = inner_ref.shape[:3]
    odd = parity_ref[0] == 1

    def stage(j):
        far, near = far_ref[j], near_ref[j]
        up, dn = jnp.where(odd, near, far), jnp.where(odd, far, near)
        up_mix, dn_mix = up[TILE:], dn[TILE:]
        outer = (
            (up[:TILE], dn[:TILE]),
            (up_mix, dn_mix),
            (pltpu.roll(up_mix, HALF, 0), pltpu.roll(dn_mix, HALF, 0)),
        )
        for k, (before, after) in enumerate(outer):
            for e, tile in enumerate((before, ends_ref[k, 0, j], ends_ref[k, 1, j], after)):
                slab[k, j, e * TILE : (e + 1) * TILE] = tile

    per_strip(strips, stage, 4)
    slabs = flat(slab)

    def load(j, t):
        return [
            slabs[pl.ds((k * strips + j) * SLAB + t, TILE, stride=HALF), :] for k in range(3)
        ]

    coef = coef_ref[0].astype(jnp.float32)
    fine, mid, low = (
        jnp.where(level_ref[0] >= depth - down, coef, 0.0) for down in range(3)
    )
    place = lax.broadcasted_iota(jnp.int32, (many, LANES), 0)
    out_refs = (own_ref, one_ref, two_ref, three_ref)

    def finish(j, new):
        s = [inner_ref[j, t] for t in range(TILE)]
        for t in range(HALF):
            s[t] = jnp.where(place == 0, new[t][2:3], s[t])
        for t in range(HALF):
            s[HALF + t] = jnp.where(place == many - 1, new[t][5:6], s[HALF + t])
        before = new[HALF - 1][1:2]
        prev = jnp.where(place == 0, before, roll_rows(s[7], 1))
        weighted = [
            fine * (s[0] - 0.5 * (prev + s[1])),
            mid * (s[1] - 0.5 * (prev + s[3])),
            fine * (s[2] - 0.5 * (s[1] + s[3])),
            low * (s[3] - 0.5 * (prev + s[7])),
            fine * (s[4] - 0.5 * (s[3] + s[5])),
            mid * (s[5] - 0.5 * (s[3] + s[7])),
            fine * (s[6] - 0.5 * (s[5] + s[7])),
            coef * s[7],
        ]
        away = (j // per_chunk) ^ me_ref[0]
        part = lax.rem(j, per_chunk)
        for k, ref in enumerate(out_refs):

            @pl.when(away == k)
            def _(ref=ref):
                for t in range(TILE):
                    ref[part * TILE + t] = weighted[t]
                ref[per_chunk * TILE + part // many, pl.ds(lax.rem(part, many), 1), :] = (
                    coef * before
                )

    run_steps(strips, HALF, load, (state_a, state_b), coefs, finish, 2)


def sum_kernel(*refs):
    *parts, out_ref = refs
    total = parts[0][...]
    for part in parts[1:]:
        total = total + part[...]
    out_ref[...] = total


def nodal_kernel(per_chunk, depth, me_ref, level_ref, *refs):
    *totals, out_ref = refs
    many, strips = out_ref.shape[:2]
    out = flat(out_ref)
    fine, mid, low = (jnp.where(level_ref[0] >= depth - down, 1.0, 0.0) for down in range(3))
    place = lax.broadcasted_iota(jnp.int32, (many, LANES), 0)
    for away, ref in enumerate(totals):
        first = (me_ref[0] ^ away) * per_chunk

        def body(part, ref=ref, first=first):
            w = [ref[part * TILE + t] for t in range(TILE)]
            before = ref[per_chunk * TILE + part // many, pl.ds(lax.rem(part, many), 1), :]
            prev = jnp.where(place == 0, before, roll_rows(w[7], 1))
            v3 = 0.5 * (prev + w[7]) + low * w[3]
            v1 = 0.5 * (prev + v3) + mid * w[1]
            v5 = 0.5 * (v3 + w[7]) + mid * w[5]
            values = (
                0.5 * (prev + v1) + fine * w[0],
                v1,
                0.5 * (v1 + v3) + fine * w[2],
                v3,
                0.5 * (v3 + v5) + fine * w[4],
                v5,
                0.5 * (v5 + w[7]) + fine * w[6],
                w[7],
            )
            for t in range(TILE):
                out[spaced((first + part) * TILE + t, many, strips * TILE), :] = values[t]

        per_strip(per_chunk, body, 2)


def call(kernel, out_shapes, operands, in_smem=0, scratch=(), flops=0):
    specs = [
        pl.BlockSpec(memory_space=pltpu.SMEM if k < in_smem else pltpu.VMEM)
        for k in range(len(operands))
    ]
    moved = 4 * sum(x.size for x in operands)
    return pl.pallas_call(
        kernel,
        out_shape=[jax.ShapeDtypeStruct(shape, jnp.float32) for shape in out_shapes],
        in_specs=specs,
        out_specs=[pl.BlockSpec(memory_space=pltpu.VMEM) for _ in out_shapes],
        scratch_shapes=list(scratch),
        compiler_params=pltpu.CompilerParams(vmem_limit_bytes=VMEM_LIMIT),
        cost_estimate=pl.CostEstimate(flops=flops, bytes_accessed=moved, transcendentals=0),
    )(*operands)


def on_device(density, diffusion, drift_speed, levels, coefficient):
    rows, cols = density.shape[1:]
    doms, grids = lax.axis_size("dom"), lax.axis_size("grp")
    many, strips = rows // TILE, cols // LANES
    per_chunk = strips // SQUARE
    depth = (rows * doms).bit_length() - 1
    tiles = [tiles_of(x[0]) for x in (density, diffusion, drift_speed)]
    me = (lax.axis_index("grp") % SQUARE).astype(jnp.int32)[None]
    parity = (lax.axis_index("dom") % 2).astype(jnp.int32)[None]

    def vmem(*shape):
        return pltpu.VMEM(shape, jnp.float32)

    far, near, ends = call(
        pack_kernel,
        [(strips, 2 * TILE, LANES)] * 2 + [(3, 2, strips, TILE, LANES)],
        (parity, *tiles),
        1,
    )
    far_pairs = [(d, d + 1) for d in range(1, doms - 1, 2)]
    near_pairs = [(d, d + 1) for d in range(0, doms, 2)]
    far, near = (
        lax.ppermute(array, "dom", pairs + [(b, a) for a, b in pairs])
        for array, pairs in ((far, far_pairs), (near, near_pairs))
    )
    (inner,) = call(
        inner_kernel,
        [(strips, TILE, many, LANES)],
        tiles,
        0,
        [vmem(strips + 2, TILE, many, LANES)] * 2 + [vmem(strips, TILE, many, LANES)] * 4,
        flops=40 * rows * cols,
    )

    chunk = (per_chunk * TILE + -(-per_chunk // many), many, LANES)
    own, *others = call(
        functools.partial(edge_kernel, per_chunk, depth),
        [chunk] * SQUARE,
        (parity, me, levels, coefficient, ends, inner, far, near),
        4,
        [vmem(3, strips, SLAB, LANES)]
        + [vmem(strips + 2, HALF, TILE, LANES)] * 2
        + [vmem(strips, HALF, TILE, LANES)] * 4,
        flops=40 * SLAB * cols,
    )

    def swap(array, apart):
        return lax.ppermute(array, "grp", [(g, g ^ apart) for g in range(grids)])

    theirs = [swap(array, apart) for apart, array in enumerate(others, 1)]
    (total,) = call(sum_kernel, [chunk], (own, *theirs))
    apart = SQUARE
    while apart < grids:
        (total,) = call(sum_kernel, [chunk], (total, swap(total, apart)))
        apart *= 2
    totals = [total] + [swap(total, apart) for apart in range(1, SQUARE)]
    (nodal,) = call(
        functools.partial(nodal_kernel, per_chunk, depth),
        [(many, strips, TILE, LANES)],
        (me, levels, *totals),
        2,
    )
    return block_of(nodal)[None]


def solution(mesh):
    return jax.shard_map(
        on_device,
        mesh=mesh,
        in_specs=(
            P("grp", "dom", None),
            P("grp", "dom", None),
            P("grp", "dom", None),
            P("grp"),
            P("grp"),
        ),
        out_specs=P("grp", "dom", None),
        check_vma=False,
    )
```

```python
import functools

import jax
import jax.numpy as jnp
from jax import lax
from jax.experimental import pallas as pl
from jax.experimental.pallas import tpu as pltpu
from jax.sharding import PartitionSpec as P

STEPS = 4
LANES = 128
TILE = 8
HALF = TILE // 2
SLAB = 4 * TILE
SQUARE = 4
UNROLL = 16
VMEM_LIMIT = 40 * 1024 * 1024


def tiles_of(block):
    rows, cols = block.shape
    return block.reshape(rows // TILE, TILE, cols // LANES, LANES).transpose(0, 2, 1, 3)


def block_of(tiles):
    many, strips = tiles.shape[:2]
    return tiles.transpose(0, 2, 1, 3).reshape(many * TILE, strips * LANES)


def flat(ref):
    return ref.reshape(ref.size // LANES, LANES)


def spaced(first, count, stride):
    return pl.ds(first, count, stride=stride) if count > 1 else pl.ds(first, 1)


def roll_rows(value, shift):
    count = value.shape[0]
    return pltpu.roll(value, shift % count, 0) if count > 1 else value


def per_strip(strips, body, unroll):
    def step(j, carry):
        body(j)
        return carry

    lax.fori_loop(0, strips, step, 0, unroll=unroll)


def advance(strips, classes, source, coefs, emit, unroll):
    shape = source.shape[2:]
    lanes = lax.broadcasted_iota(jnp.int32, shape, 1)
    center, above_c, below_c, side = coefs

    def body(j, carry):
        cur, right_prev, left_cur = carry
        nxt = [source[j + 2, t] for t in range(classes)]
        left_next = [pltpu.roll(x, LANES - 1, 1) for x in nxt]
        right_cur = [pltpu.roll(x, 1, 1) for x in cur]
        above = cur[1:] + [roll_rows(cur[0], -1)]
        below = [roll_rows(cur[-1], 1)] + cur[:-1]
        new = []
        for t in range(classes):
            left = jnp.where(lanes == 0, right_prev[t], right_cur[t])
            right = jnp.where(lanes == LANES - 1, left_next[t], left_cur[t])
            new.append(
                center[j, t] * cur[t]
                + above_c[j, t] * above[t]
                + below_c[j, t] * below[t]
                + side[j, t] * (left + right)
            )
        emit(j, new)
        return nxt, right_cur, left_next

    cur = [source[1, t] for t in range(classes)]
    zeros = [jnp.zeros(shape, jnp.float32)] * classes
    first = (cur, zeros, [pltpu.roll(x, LANES - 1, 1) for x in cur])
    lax.fori_loop(0, strips, body, first, unroll=unroll)


def run_steps(strips, classes, load, buffers, coefs, finish, unroll):
    center, above_c, below_c, side = coefs
    for buf in buffers:
        for edge in (0, strips + 1):
            buf[edge] = jnp.zeros(buf.shape[1:], jnp.float32)

    def begin(j):
        for t in range(classes):
            state, diffuse, drifts = load(j, t)
            half = 0.5 * drifts
            buffers[0][j + 1, t] = state
            center[j, t] = 1.0 - 4.0 * diffuse
            above_c[j, t] = diffuse - half
            below_c[j, t] = diffuse + half
            side[j, t] = diffuse

    per_strip(strips, begin, unroll)
    for step in range(STEPS):
        source, target = buffers[step % 2], buffers[1 - step % 2]

        def keep(j, new, target=target):
            for t in range(classes):
                target[j + 1, t] = new[t]

        emit = keep if step < STEPS - 1 else finish
        advance(strips, classes, source, coefs, emit, unroll)


def pack_kernel(parity_ref, *refs):
    *ends, far_ref, near_ref = refs
    strips = far_ref.shape[0]
    odd = parity_ref[0] == 1
    upper = lax.broadcasted_iota(jnp.int32, (TILE, LANES), 0) < HALF

    def body(j):
        heads, tails = ([ref[j] for ref in ends[e::2]] for e in range(2))
        mix_next = jnp.where(upper, pltpu.roll(tails[2], HALF, 0), tails[1])
        mix_prev = jnp.where(upper, heads[1], pltpu.roll(heads[2], HALF, 0))
        to_next, to_prev = (tails[0], mix_next), (heads[0], mix_prev)
        for k in range(2):
            at = pl.ds(k * TILE, TILE)
            far_ref[j, at] = jnp.where(odd, to_next[k], to_prev[k])
            near_ref[j, at] = jnp.where(odd, to_prev[k], to_next[k])

    per_strip(strips, body, 4)


def inner_kernel(
    depth, level_ref, coef_ref, dens_ref, diff_ref, drift_ref, out_ref, keep_ref, weight_ref,
    state_a, state_b, *coefs
):
    many, strips = dens_ref.shape[:2]
    refs = [flat(ref) for ref in (dens_ref, diff_ref, drift_ref)]

    def load(j, t):
        at = spaced(j * TILE + t, many, strips * TILE)
        return [ref[at, :] for ref in refs]

    def finish(j, new):
        for t in range(TILE):
            out_ref[j, t] = new[t]

    run_steps(strips, TILE, load, (state_a, state_b), coefs, finish, min(strips, UNROLL))
    coef = coef_ref[0].astype(jnp.float32)
    for down in range(3):
        keep = jnp.where(level_ref[0] >= depth - down, 1.0, 0.0)
        keep_ref[down] = jnp.full((many, LANES), keep)
        weight_ref[down] = jnp.full((many, LANES), keep * coef)
    weight_ref[3] = jnp.full((many, LANES), coef)


def edge_kernel(
    per_chunk, parity_ref, me_ref, weight_ref, *refs
):
    ends, (inner_ref, far_ref, near_ref), out_refs = refs[:6], refs[6:9], refs[9:13]
    slab, state_a, state_b, *coefs = refs[13:]
    strips, _, many = inner_ref.shape[:3]
    odd = parity_ref[0] == 1

    def stage(j):
        far, near = far_ref[j], near_ref[j]
        up, dn = jnp.where(odd, near, far), jnp.where(odd, far, near)
        up_mix, dn_mix = up[TILE:], dn[TILE:]
        outer = (
            (up[:TILE], dn[:TILE]),
            (up_mix, dn_mix),
            (pltpu.roll(up_mix, HALF, 0), pltpu.roll(dn_mix, HALF, 0)),
        )
        for k, (before, after) in enumerate(outer):
            for e, tile in enumerate((before, ends[2 * k][j], ends[2 * k + 1][j], after)):
                slab[k, j, e * TILE : (e + 1) * TILE] = tile

    per_strip(strips, stage, 4)
    slabs = flat(slab)

    def load(j, t):
        return [
            slabs[pl.ds((k * strips + j) * SLAB + t, TILE, stride=HALF), :] for k in range(3)
        ]

    fine, mid, low, coef = (weight_ref[k] for k in range(4))
    place = lax.broadcasted_iota(jnp.int32, (many, LANES), 0)

    def finish(j, new):
        s = [inner_ref[j, t] for t in range(TILE)]
        for t in range(HALF):
            s[t] = jnp.where(place == 0, new[t][2:3], s[t])
        for t in range(HALF):
            s[HALF + t] = jnp.where(place == many - 1, new[t][5:6], s[HALF + t])
        before = new[HALF - 1][1:2]
        prev = jnp.where(place == 0, before, roll_rows(s[7], 1))
        weighted = [
            fine * (s[0] - 0.5 * (prev + s[1])),
            mid * (s[1] - 0.5 * (prev + s[3])),
            fine * (s[2] - 0.5 * (s[1] + s[3])),
            low * (s[3] - 0.5 * (prev + s[7])),
            fine * (s[4] - 0.5 * (s[3] + s[5])),
            mid * (s[5] - 0.5 * (s[3] + s[7])),
            fine * (s[6] - 0.5 * (s[5] + s[7])),
            coef * s[7],
        ]
        away = (j // per_chunk) ^ me_ref[0]
        part = lax.rem(j, per_chunk)
        for k, ref in enumerate(out_refs):

            @pl.when(away == k)
            def _(ref=ref):
                for t in range(TILE):
                    ref[part * TILE + t] = weighted[t]
                ref[per_chunk * TILE + part // many, pl.ds(lax.rem(part, many), 1), :] = (
                    coef[0:1] * before
                )

    run_steps(strips, HALF, load, (state_a, state_b), coefs, finish, min(strips, UNROLL))


def sum_kernel(*refs):
    *parts, out_ref = refs
    total = parts[0][...]
    for part in parts[1:]:
        total = total + part[...]
    out_ref[...] = total


def nodal_kernel(per_chunk, me_ref, keep_ref, *refs):
    *totals, out_ref = refs
    many, strips = out_ref.shape[:2]
    out = flat(out_ref)
    fine, mid, low = (keep_ref[k] for k in range(3))
    place = lax.broadcasted_iota(jnp.int32, (many, LANES), 0)
    for away, ref in enumerate(totals):
        first = (me_ref[0] ^ away) * per_chunk

        def body(part, ref=ref, first=first):
            w = [ref[part * TILE + t] for t in range(TILE)]
            before = ref[per_chunk * TILE + part // many, pl.ds(lax.rem(part, many), 1), :]
            prev = jnp.where(place == 0, before, roll_rows(w[7], 1))
            v3 = 0.5 * (prev + w[7]) + low * w[3]
            v1 = 0.5 * (prev + v3) + mid * w[1]
            v5 = 0.5 * (v3 + w[7]) + mid * w[5]
            values = (
                0.5 * (prev + v1) + fine * w[0],
                v1,
                0.5 * (v1 + v3) + fine * w[2],
                v3,
                0.5 * (v3 + v5) + fine * w[4],
                v5,
                0.5 * (v5 + w[7]) + fine * w[6],
                w[7],
            )
            for t in range(TILE):
                out[spaced((first + part) * TILE + t, many, strips * TILE), :] = values[t]

        per_strip(per_chunk, body, min(per_chunk, 4))


def call(kernel, out_shapes, operands, in_smem=0, scratch=(), flops=0):
    spaces = [pltpu.SMEM] * in_smem + [pltpu.VMEM] * (len(operands) - in_smem)
    specs = [pl.BlockSpec(memory_space=space) for space in spaces]
    moved = 4 * sum(x.size for x in operands)
    return pl.pallas_call(
        kernel,
        out_shape=[jax.ShapeDtypeStruct(shape, jnp.float32) for shape in out_shapes],
        in_specs=specs,
        out_specs=[pl.BlockSpec(memory_space=pltpu.VMEM) for _ in out_shapes],
        scratch_shapes=list(scratch),
        compiler_params=pltpu.CompilerParams(vmem_limit_bytes=VMEM_LIMIT),
        cost_estimate=pl.CostEstimate(flops=flops, bytes_accessed=moved, transcendentals=0),
    )(*operands)


def on_device(density, diffusion, drift_speed, levels, coefficient):
    rows, cols = density.shape[1:]
    doms, grids = lax.axis_size("dom"), lax.axis_size("grp")
    many, strips = rows // TILE, cols // LANES
    per_chunk = strips // SQUARE
    depth = (rows * doms).bit_length() - 1
    tiles = [tiles_of(x[0]) for x in (density, diffusion, drift_speed)]
    me = (lax.axis_index("grp") % SQUARE).astype(jnp.int32)[None]
    parity = (lax.axis_index("dom") % 2).astype(jnp.int32)[None]

    def vmem(*shape):
        return pltpu.VMEM(shape, jnp.float32)

    ends = [x[at] for x in tiles for at in (0, many - 1)]
    far, near = call(
        pack_kernel,
        [(strips, 2 * TILE, LANES)] * 2,
        (parity, *ends),
        1,
    )
    far_pairs = [(d, d + 1) for d in range(1, doms - 1, 2)]
    near_pairs = [(d, d + 1) for d in range(0, doms, 2)]
    far, near = (
        lax.ppermute(array, "dom", pairs + [(b, a) for a, b in pairs])
        for array, pairs in ((far, far_pairs), (near, near_pairs))
    )
    inner, keep, weight = call(
        functools.partial(inner_kernel, depth),
        [(strips, TILE, many, LANES), (3, many, LANES), (4, many, LANES)],
        (levels, coefficient, *tiles),
        2,
        [vmem(strips + 2, TILE, many, LANES)] * 2 + [vmem(strips, TILE, many, LANES)] * 4,
        flops=40 * rows * cols,
    )

    chunk = (per_chunk * TILE + -(-per_chunk // many), many, LANES)
    own, *others = call(
        functools.partial(edge_kernel, per_chunk),
        [chunk] * SQUARE,
        (parity, me, weight, *ends, inner, far, near),
        2,
        [vmem(3, strips, SLAB, LANES)]
        + [vmem(strips + 2, HALF, TILE, LANES)] * 2
        + [vmem(strips, HALF, TILE, LANES)] * 4,
        flops=40 * SLAB * cols,
    )

    def swap(array, apart):
        return lax.ppermute(array, "grp", [(g, g ^ apart) for g in range(grids)])

    theirs = [swap(array, apart) for apart, array in enumerate(others, 1)]
    (total,) = call(sum_kernel, [chunk], (own, *theirs))
    apart = SQUARE
    while apart < grids:
        (total,) = call(sum_kernel, [chunk], (total, swap(total, apart)))
        apart *= 2
    totals = [total] + [swap(total, apart) for apart in range(1, SQUARE)]
    (nodal,) = call(
        functools.partial(nodal_kernel, per_chunk),
        [(many, strips, TILE, LANES)],
        (me, keep, *totals),
        1,
    )
    return block_of(nodal)[None]


def solution(mesh):
    return jax.shard_map(
        on_device,
        mesh=mesh,
        in_specs=(
            P("grp", "dom", None),
            P("grp", "dom", None),
            P("grp", "dom", None),
            P("grp"),
            P("grp"),
        ),
        out_specs=P("grp", "dom", None),
        check_vma=False,
    )
```

```python
import functools

import jax
import jax.numpy as jnp
from jax import lax
from jax.experimental import pallas as pl
from jax.experimental.pallas import tpu as pltpu
from jax.sharding import PartitionSpec as P

STEPS = 4
LANES = 128
TILE = 8
HALF = TILE // 2
SLAB = 4 * TILE
SQUARE = 4
UNROLL = 16
VMEM_LIMIT = 40 * 1024 * 1024


def tiles_of(block):
    rows, cols = block.shape
    return block.reshape(rows // TILE, TILE, cols // LANES, LANES).transpose(0, 2, 1, 3)


def block_of(tiles):
    many, strips = tiles.shape[:2]
    return tiles.transpose(0, 2, 1, 3).reshape(many * TILE, strips * LANES)


def flat(ref):
    return ref.reshape(ref.size // LANES, LANES)


def spaced(first, count, stride):
    return pl.ds(first, count, stride=stride) if count > 1 else pl.ds(first, 1)


def roll_rows(value, shift):
    count = value.shape[0]
    return pltpu.roll(value, shift % count, 0) if count > 1 else value


def per_strip(strips, body, unroll):
    def step(j, carry):
        body(j)
        return carry

    lax.fori_loop(0, strips, step, 0, unroll=unroll)


def advance(first, count, classes, source, coefs, emit):
    shape = source.shape[2:]
    lanes = lax.broadcasted_iota(jnp.int32, shape, 1)
    center, above_c, below_c, side = coefs

    def body(k, carry):
        j = first + k
        cur, right_prev, left_cur = carry
        nxt = [source[j + 2, t] for t in range(classes)]
        left_next = [pltpu.roll(x, LANES - 1, 1) for x in nxt]
        right_cur = [pltpu.roll(x, 1, 1) for x in cur]
        above = cur[1:] + [roll_rows(cur[0], -1)]
        below = [roll_rows(cur[-1], 1)] + cur[:-1]
        new = []
        for t in range(classes):
            left = jnp.where(lanes == 0, right_prev[t], right_cur[t])
            right = jnp.where(lanes == LANES - 1, left_next[t], left_cur[t])
            new.append(
                center[j, t] * cur[t]
                + above_c[j, t] * above[t]
                + below_c[j, t] * below[t]
                + side[j, t] * (left + right)
            )
        emit(j, k, new)
        return nxt, right_cur, left_next

    prev, cur = ([source[first + at, t] for t in range(classes)] for at in range(2))
    ends = [pltpu.roll(x, 1, 1) for x in prev], [pltpu.roll(x, LANES - 1, 1) for x in cur]
    lax.fori_loop(0, count, body, (cur, *ends), unroll=min(count, UNROLL))


def run_steps(strips, per_chunk, me, classes, load, buffers, coefs, finish):
    center, above_c, below_c, side = coefs
    for buf in buffers:
        for edge in (0, strips + 1):
            buf[edge] = jnp.zeros(buf.shape[1:], jnp.float32)

    def begin(j):
        for t in range(classes):
            state, diffuse, drifts = load(j, t)
            half = 0.5 * drifts
            buffers[0][j + 1, t] = state
            center[j, t] = 1.0 - 4.0 * diffuse
            above_c[j, t] = diffuse - half
            below_c[j, t] = diffuse + half
            side[j, t] = diffuse

    per_strip(strips, begin, min(strips, UNROLL))
    for step in range(STEPS - 1):
        source, target = buffers[step % 2], buffers[1 - step % 2]

        def keep(j, _, new, target=target):
            for t in range(classes):
                target[j + 1, t] = new[t]

        advance(0, strips, classes, source, coefs, keep)
    source = buffers[(STEPS - 1) % 2]
    for away in range(SQUARE):
        emit = functools.partial(finish, away)
        advance((me ^ away) * per_chunk, per_chunk, classes, source, coefs, emit)


def surpluses(s, prev, weight_ref):
    fine, mid, low, coef = (weight_ref[k] for k in range(4))
    return (
        fine * (s[0] - 0.5 * (prev + s[1])),
        mid * (s[1] - 0.5 * (prev + s[3])),
        fine * (s[2] - 0.5 * (s[1] + s[3])),
        low * (s[3] - 0.5 * (prev + s[7])),
        fine * (s[4] - 0.5 * (s[3] + s[5])),
        mid * (s[5] - 0.5 * (s[3] + s[7])),
        fine * (s[6] - 0.5 * (s[5] + s[7])),
        coef * s[7],
    )


def pack(odd, refs, far_ref, near_ref):
    many, strips = refs[0].shape[:2]
    upper = lax.broadcasted_iota(jnp.int32, (TILE, LANES), 0) < HALF

    def body(j):
        heads, tails = ([ref[at, j] for ref in refs] for at in (0, many - 1))
        mix_next = jnp.where(upper, pltpu.roll(tails[2], HALF, 0), tails[1])
        mix_prev = jnp.where(upper, heads[1], pltpu.roll(heads[2], HALF, 0))
        to_next, to_prev = (tails[0], mix_next), (heads[0], mix_prev)
        for k in range(2):
            at = pl.ds(k * TILE, TILE)
            far_ref[j, at] = jnp.where(odd, to_next[k], to_prev[k])
            near_ref[j, at] = jnp.where(odd, to_prev[k], to_next[k])

    per_strip(strips, body, 4)


def inner_kernel(
    per_chunk, depth, parity_ref, me_ref, level_ref, coef_ref, dens_ref, diff_ref, drift_ref,
    far_ref, near_ref, state_ref, keep_ref, weight_ref, *refs
):
    many, strips = dens_ref.shape[:2]
    *out_refs, scratch, state_a, state_b = refs[:-4]
    fields = (dens_ref, diff_ref, drift_ref)
    pack(parity_ref[0] == 1, fields, far_ref, near_ref)
    coef = coef_ref[0].astype(jnp.float32)
    for down in range(3):
        keep = jnp.where(level_ref[0] >= depth - down, 1.0, 0.0)
        keep_ref[down] = jnp.full((many, LANES), keep)
        weight_ref[down] = jnp.full((many, LANES), keep * coef)
    weight_ref[3] = jnp.full((many, LANES), coef)
    rows = [flat(ref) for ref in fields]
    by_row = flat(scratch)
    inside = many - 2

    def load(j, t):
        at = spaced(j * TILE + t, many, strips * TILE)
        return [ref[at, :] for ref in rows]

    def finish(away, j, part, new):
        for t in range(TILE):
            state_ref[j, t] = new[t]
        if inside <= 0:
            return
        weighted = surpluses(new, roll_rows(new[7], 1), weight_ref)
        for t in range(TILE):
            by_row[spaced(j * many * TILE + t, many, TILE), :] = weighted[t]
        for m in range(inside):
            out_refs[away][part * inside + m] = scratch[j, 1 + m]

    run_steps(strips, per_chunk, me_ref[0], TILE, load, (state_a, state_b), refs[-4:], finish)


def edge_kernel(
    per_chunk, parity_ref, me_ref, dens_ref, diff_ref, drift_ref, state_ref, weight_ref, far_ref,
    near_ref, *refs
):
    many, strips = dens_ref.shape[:2]
    odd = parity_ref[0] == 1
    *out_refs, scratch, slab, state_a, state_b = refs[:-4]

    def stage(j):
        far, near = far_ref[j], near_ref[j]
        up, dn = jnp.where(odd, near, far), jnp.where(odd, far, near)
        up_mix, dn_mix = up[TILE:], dn[TILE:]
        tiles = (
            (up[:TILE], dens_ref, dn[:TILE]),
            (up_mix, diff_ref, dn_mix),
            (pltpu.roll(up_mix, HALF, 0), drift_ref, pltpu.roll(dn_mix, HALF, 0)),
        )
        for k, (before, ref, after) in enumerate(tiles):
            for e, tile in enumerate((before, ref[0, j], ref[many - 1, j], after)):
                slab[k, j, e * TILE : (e + 1) * TILE] = tile

    per_strip(strips, stage, 4)
    slabs = flat(slab)

    def load(j, t):
        return [
            slabs[pl.ds((k * strips + j) * SLAB + t, TILE, stride=HALF), :] for k in range(3)
        ]

    place = lax.broadcasted_iota(jnp.int32, (many, LANES), 0)
    by_row = flat(scratch)
    edges = sorted({0, many - 1})

    def finish(away, j, part, new):
        s = [state_ref[j, t] for t in range(TILE)]
        for t in range(HALF):
            s[t] = jnp.where(place == 0, new[t][2:3], s[t])
            s[HALF + t] = jnp.where(place == many - 1, new[t][5:6], s[HALF + t])
        before = new[HALF - 1][1:2]
        weighted = surpluses(s, jnp.where(place == 0, before, roll_rows(s[7], 1)), weight_ref)
        for t in range(TILE):
            by_row[spaced(j * many * TILE + t, many, TILE), :] = weighted[t]
        for e, m in enumerate(edges):
            out_refs[away][part * len(edges) + e] = scratch[j, m]
        last = per_chunk * len(edges) + part // TILE
        out_refs[away][last, pl.ds(lax.rem(part, TILE), 1), :] = weight_ref[3][0:1] * before

    run_steps(strips, per_chunk, me_ref[0], HALF, load, (state_a, state_b), refs[-4:], finish)


def sum_kernel(*refs):
    *parts, out_ref = refs
    total = parts[0][...]
    for part in parts[1:]:
        total = total + part[...]
    out_ref[...] = total


def nodal_kernel(per_chunk, me_ref, keep_ref, *refs):
    *totals, out_ref, scratch = refs
    many, strips = out_ref.shape[:2]
    out, by_row = flat(out_ref), flat(scratch)
    fine, mid, low = (keep_ref[k] for k in range(3))
    place = lax.broadcasted_iota(jnp.int32, (many, LANES), 0)
    edges, inside = sorted({0, many - 1}), many - 2
    for away in range(SQUARE):
        first = (me_ref[0] ^ away) * per_chunk
        outer_ref = totals[away]
        inner_ref = totals[SQUARE + away] if inside > 0 else None

        def body(part, outer_ref=outer_ref, inner_ref=inner_ref, first=first):
            j = first + part
            for e, m in enumerate(edges):
                scratch[j, m] = outer_ref[part * len(edges) + e]
            for m in range(inside):
                scratch[j, 1 + m] = inner_ref[part * inside + m]
            w = [by_row[spaced(j * many * TILE + t, many, TILE), :] for t in range(TILE)]
            last = per_chunk * len(edges) + part // TILE
            before = outer_ref[last, pl.ds(lax.rem(part, TILE), 1), :]
            prev = jnp.where(place == 0, before, roll_rows(w[7], 1))
            v3 = 0.5 * (prev + w[7]) + low * w[3]
            v1 = 0.5 * (prev + v3) + mid * w[1]
            v5 = 0.5 * (v3 + w[7]) + mid * w[5]
            values = (
                0.5 * (prev + v1) + fine * w[0],
                v1,
                0.5 * (v1 + v3) + fine * w[2],
                v3,
                0.5 * (v3 + v5) + fine * w[4],
                v5,
                0.5 * (v5 + w[7]) + fine * w[6],
                w[7],
            )
            for t in range(TILE):
                out[spaced(j * TILE + t, many, strips * TILE), :] = values[t]

        per_strip(per_chunk, body, min(per_chunk, 4))


def call(kernel, out_shapes, operands, in_smem=0, scratch=(), flops=0):
    spaces = [pltpu.SMEM] * in_smem + [pltpu.VMEM] * (len(operands) - in_smem)
    specs = [pl.BlockSpec(memory_space=space) for space in spaces]
    moved = 4 * sum(x.size for x in operands)
    return pl.pallas_call(
        kernel,
        out_shape=[jax.ShapeDtypeStruct(shape, jnp.float32) for shape in out_shapes],
        in_specs=specs,
        out_specs=[pl.BlockSpec(memory_space=pltpu.VMEM) for _ in out_shapes],
        scratch_shapes=list(scratch),
        compiler_params=pltpu.CompilerParams(vmem_limit_bytes=VMEM_LIMIT),
        cost_estimate=pl.CostEstimate(flops=flops, bytes_accessed=moved, transcendentals=0),
    )(*operands)


def on_device(density, diffusion, drift_speed, levels, coefficient):
    rows, cols = density.shape[1:]
    doms, grids = lax.axis_size("dom"), lax.axis_size("grp")
    many, strips = rows // TILE, cols // LANES
    per_chunk = strips // SQUARE
    depth = (rows * doms).bit_length() - 1
    tiles = [tiles_of(x[0]) for x in (density, diffusion, drift_speed)]
    me = (lax.axis_index("grp") % SQUARE).astype(jnp.int32)[None]
    parity = (lax.axis_index("dom") % 2).astype(jnp.int32)[None]

    def vmem(*shape):
        return pltpu.VMEM(shape, jnp.float32)

    place = (strips, TILE, many, LANES)
    pieces = (strips, many, TILE, LANES)
    far, near, state, keep, weight, *inside = call(
        functools.partial(inner_kernel, per_chunk, depth),
        [(strips, 2 * TILE, LANES)] * 2
        + [place, (3, many, LANES), (4, many, LANES)]
        + [(per_chunk * (many - 2), TILE, LANES)] * (SQUARE if many > 2 else 0),
        (parity, me, levels, coefficient, *tiles),
        4,
        [vmem(*pieces)] + [vmem(strips + 2, *place[1:])] * 2 + [vmem(*place)] * 4,
        flops=40 * rows * cols,
    )
    far_pairs = [(d, d + 1) for d in range(1, doms - 1, 2)]
    near_pairs = [(d, d + 1) for d in range(0, doms, 2)]
    far, near = (
        lax.ppermute(array, "dom", pairs + [(b, a) for a, b in pairs])
        for array, pairs in ((far, far_pairs), (near, near_pairs))
    )
    outside = call(
        functools.partial(edge_kernel, per_chunk),
        [(per_chunk * min(many, 2) + -(-per_chunk // TILE), TILE, LANES)] * SQUARE,
        (parity, me, *tiles, state, weight, far, near),
        2,
        [vmem(*pieces), vmem(3, strips, SLAB, LANES)]
        + [vmem(strips + 2, HALF, TILE, LANES)] * 2
        + [vmem(strips, HALF, TILE, LANES)] * 4,
        flops=40 * SLAB * cols,
    )

    def swap(array, apart):
        return lax.ppermute(array, "grp", [(g, g ^ apart) for g in range(grids)])

    def over_grids(own, *others):
        theirs = [swap(array, apart) for apart, array in enumerate(others, 1)]
        (total,) = call(sum_kernel, [own.shape], (own, *theirs))
        apart = SQUARE
        while apart < grids:
            (total,) = call(sum_kernel, [own.shape], (total, swap(total, apart)))
            apart *= 2
        return [total] + [swap(total, apart) for apart in range(1, SQUARE)]

    totals = over_grids(*outside) + (over_grids(*inside) if inside else [])
    (nodal,) = call(
        functools.partial(nodal_kernel, per_chunk),
        [(many, strips, TILE, LANES)],
        (me, keep, *totals),
        1,
        [vmem(*pieces)],
    )
    return block_of(nodal)[None]


def solution(mesh):
    return jax.shard_map(
        on_device,
        mesh=mesh,
        in_specs=(
            P("grp", "dom", None),
            P("grp", "dom", None),
            P("grp", "dom", None),
            P("grp"),
            P("grp"),
        ),
        out_specs=P("grp", "dom", None),
        check_vma=False,
    )
```

```python
import functools

import jax
import jax.numpy as jnp
from jax import lax
from jax.experimental import pallas as pl
from jax.experimental.pallas import tpu as pltpu
from jax.sharding import PartitionSpec as P

STEPS = 4
LANES = 128
TILE = 8
HALF = TILE // 2
SLAB = 4 * TILE
SQUARE = 4
UNROLL = 16
VMEM_LIMIT = 40 * 1024 * 1024


def tiles_of(block):
    rows, cols = block.shape
    return block.reshape(rows // TILE, TILE, cols // LANES, LANES).transpose(0, 2, 1, 3)


def block_of(tiles):
    many, strips = tiles.shape[:2]
    return tiles.transpose(0, 2, 1, 3).reshape(many * TILE, strips * LANES)


def flat(ref):
    return ref.reshape(ref.size // LANES, LANES)


def spaced(first, count, stride):
    return pl.ds(first, count, stride=stride) if count > 1 else pl.ds(first, 1)


def roll_rows(value, shift):
    count = value.shape[0]
    return pltpu.roll(value, shift % count, 0) if count > 1 else value


def per_strip(strips, body, unroll):
    def step(j, carry):
        body(j)
        return carry

    lax.fori_loop(0, strips, step, 0, unroll=unroll)


def advance(first, count, classes, source, coefs, emit):
    shape = source.shape[2:]
    lanes = lax.broadcasted_iota(jnp.int32, shape, 1)
    center, above_c, below_c, side = coefs

    def body(k, carry):
        j = first + k
        cur, right_prev, left_cur = carry
        nxt = [source[j + 2, t] for t in range(classes)]
        left_next = [pltpu.roll(x, LANES - 1, 1) for x in nxt]
        right_cur = [pltpu.roll(x, 1, 1) for x in cur]
        above = cur[1:] + [roll_rows(cur[0], -1)]
        below = [roll_rows(cur[-1], 1)] + cur[:-1]
        new = []
        for t in range(classes):
            left = jnp.where(lanes == 0, right_prev[t], right_cur[t])
            right = jnp.where(lanes == LANES - 1, left_next[t], left_cur[t])
            new.append(
                center[j, t] * cur[t]
                + above_c[j, t] * above[t]
                + below_c[j, t] * below[t]
                + side[j, t] * (left + right)
            )
        emit(j, k, new)
        return nxt, right_cur, left_next

    prev, cur = ([source[first + at, t] for t in range(classes)] for at in range(2))
    ends = [pltpu.roll(x, 1, 1) for x in prev], [pltpu.roll(x, LANES - 1, 1) for x in cur]
    lax.fori_loop(0, count, body, (cur, *ends), unroll=min(count, UNROLL))


def run_steps(strips, per_chunk, classes, load, buffers, coefs, finish):
    center, above_c, below_c, side = coefs
    for buf in buffers:
        for edge in (0, strips + 1):
            buf[edge] = jnp.zeros(buf.shape[1:], jnp.float32)

    def begin(j):
        for t in range(classes):
            state, diffuse, drifts = load(j, t)
            half = 0.5 * drifts
            buffers[0][j + 1, t] = state
            center[j, t] = 1.0 - 4.0 * diffuse
            above_c[j, t] = diffuse - half
            below_c[j, t] = diffuse + half
            side[j, t] = diffuse

    per_strip(strips, begin, min(strips, UNROLL))
    for step in range(STEPS - 1):
        source, target = buffers[step % 2], buffers[1 - step % 2]

        def keep(j, _, new, target=target):
            for t in range(classes):
                target[j + 1, t] = new[t]

        advance(0, strips, classes, source, coefs, keep)
    source = buffers[(STEPS - 1) % 2]
    for chunk in range(SQUARE):
        emit = functools.partial(finish, chunk)
        advance(chunk * per_chunk, per_chunk, classes, source, coefs, emit)


def surpluses(s, prev, weight_ref):
    fine, mid, low, coef = (weight_ref[k] for k in range(4))
    return (
        fine * (s[0] - 0.5 * (prev + s[1])),
        mid * (s[1] - 0.5 * (prev + s[3])),
        fine * (s[2] - 0.5 * (s[1] + s[3])),
        low * (s[3] - 0.5 * (prev + s[7])),
        fine * (s[4] - 0.5 * (s[3] + s[5])),
        mid * (s[5] - 0.5 * (s[3] + s[7])),
        fine * (s[6] - 0.5 * (s[5] + s[7])),
        coef * s[7],
    )


def pack(odd, refs, far_ref, near_ref):
    many, strips = refs[0].shape[:2]
    upper = lax.broadcasted_iota(jnp.int32, (TILE, LANES), 0) < HALF

    def body(j):
        heads, tails = ([ref[at, j] for ref in refs] for at in (0, many - 1))
        mix_next = jnp.where(upper, pltpu.roll(tails[2], HALF, 0), tails[1])
        mix_prev = jnp.where(upper, heads[1], pltpu.roll(heads[2], HALF, 0))
        to_next, to_prev = (tails[0], mix_next), (heads[0], mix_prev)
        for k in range(2):
            at = pl.ds(k * TILE, TILE)
            far_ref[j, at] = jnp.where(odd, to_next[k], to_prev[k])
            near_ref[j, at] = jnp.where(odd, to_prev[k], to_next[k])

    per_strip(strips, body, 4)


def inner_kernel(
    per_chunk, depth, parity_ref, level_ref, coef_ref, dens_ref, diff_ref, drift_ref,
    far_ref, near_ref, state_ref, keep_ref, weight_ref, *refs
):
    many, strips = dens_ref.shape[:2]
    *outs, scratch, state_a, state_b = refs[:-4]
    fields = (dens_ref, diff_ref, drift_ref)
    pack(parity_ref[0] == 1, fields, far_ref, near_ref)
    coef = coef_ref[0].astype(jnp.float32)
    for down in range(3):
        keep = jnp.where(level_ref[0] >= depth - down, 1.0, 0.0)
        keep_ref[down] = jnp.full((many, LANES), keep)
        weight_ref[down] = jnp.full((many, LANES), keep * coef)
    weight_ref[3] = jnp.full((many, LANES), coef)
    rows = [flat(ref) for ref in fields]
    by_row = flat(scratch)
    inside = many - 2

    def load(j, t):
        at = spaced(j * TILE + t, many, strips * TILE)
        return [ref[at, :] for ref in rows]

    def finish(chunk, j, part, new):
        for t in range(TILE):
            state_ref[j, t] = new[t]
        if inside <= 0:
            return
        weighted = surpluses(new, roll_rows(new[7], 1), weight_ref)
        for t in range(TILE):
            by_row[spaced(j * many * TILE + t, many, TILE), :] = weighted[t]
        for m in range(inside):
            outs[0][chunk, part * inside + m] = scratch[j, 1 + m]

    run_steps(strips, per_chunk, TILE, load, (state_a, state_b), refs[-4:], finish)


def edge_kernel(
    per_chunk, parity_ref, dens_ref, diff_ref, drift_ref, state_ref, weight_ref, far_ref,
    near_ref, *refs
):
    many, strips = dens_ref.shape[:2]
    odd = parity_ref[0] == 1
    out_ref, scratch, slab, state_a, state_b = refs[:-4]

    def stage(j):
        far, near = far_ref[j], near_ref[j]
        up, dn = jnp.where(odd, near, far), jnp.where(odd, far, near)
        up_mix, dn_mix = up[TILE:], dn[TILE:]
        tiles = (
            (up[:TILE], dens_ref, dn[:TILE]),
            (up_mix, diff_ref, dn_mix),
            (pltpu.roll(up_mix, HALF, 0), drift_ref, pltpu.roll(dn_mix, HALF, 0)),
        )
        for k, (before, ref, after) in enumerate(tiles):
            for e, tile in enumerate((before, ref[0, j], ref[many - 1, j], after)):
                slab[k, j, e * TILE : (e + 1) * TILE] = tile

    per_strip(strips, stage, 4)
    slabs = flat(slab)

    def load(j, t):
        return [
            slabs[pl.ds((k * strips + j) * SLAB + t, TILE, stride=HALF), :] for k in range(3)
        ]

    place = lax.broadcasted_iota(jnp.int32, (many, LANES), 0)
    by_row = flat(scratch)
    edges = sorted({0, many - 1})

    def finish(chunk, j, part, new):
        s = [state_ref[j, t] for t in range(TILE)]
        for t in range(HALF):
            s[t] = jnp.where(place == 0, new[t][2:3], s[t])
            s[HALF + t] = jnp.where(place == many - 1, new[t][5:6], s[HALF + t])
        before = new[HALF - 1][1:2]
        weighted = surpluses(s, jnp.where(place == 0, before, roll_rows(s[7], 1)), weight_ref)
        for t in range(TILE):
            by_row[spaced(j * many * TILE + t, many, TILE), :] = weighted[t]
        for e, m in enumerate(edges):
            out_ref[chunk, part * len(edges) + e] = scratch[j, m]
        last = per_chunk * len(edges) + part // TILE
        out_ref[chunk, last, pl.ds(lax.rem(part, TILE), 1), :] = weight_ref[3][0:1] * before

    run_steps(strips, per_chunk, HALF, load, (state_a, state_b), refs[-4:], finish)


def sum_kernel(parts_ref, out_ref):
    total = parts_ref[0]
    for g in range(1, parts_ref.shape[0]):
        total = total + parts_ref[g]
    out_ref[...] = total


def spread_kernel(mine_ref, theirs_ref, out_ref):
    total = mine_ref[...] + theirs_ref[...]
    for g in range(out_ref.shape[0]):
        out_ref[g] = total


def nodal_kernel(per_chunk, keep_ref, *refs):
    *totals, out_ref, scratch = refs
    many, strips = out_ref.shape[:2]
    out, by_row = flat(out_ref), flat(scratch)
    fine, mid, low = (keep_ref[k] for k in range(3))
    place = lax.broadcasted_iota(jnp.int32, (many, LANES), 0)
    edges, inside = sorted({0, many - 1}), many - 2
    for chunk in range(SQUARE):

        def body(part, chunk=chunk):
            j = chunk * per_chunk + part
            for e, m in enumerate(edges):
                scratch[j, m] = totals[0][chunk, part * len(edges) + e]
            for m in range(inside):
                scratch[j, 1 + m] = totals[1][chunk, part * inside + m]
            w = [by_row[spaced(j * many * TILE + t, many, TILE), :] for t in range(TILE)]
            last = per_chunk * len(edges) + part // TILE
            before = totals[0][chunk, last, pl.ds(lax.rem(part, TILE), 1), :]
            prev = jnp.where(place == 0, before, roll_rows(w[7], 1))
            v3 = 0.5 * (prev + w[7]) + low * w[3]
            v1 = 0.5 * (prev + v3) + mid * w[1]
            v5 = 0.5 * (v3 + w[7]) + mid * w[5]
            values = (
                0.5 * (prev + v1) + fine * w[0],
                v1,
                0.5 * (v1 + v3) + fine * w[2],
                v3,
                0.5 * (v3 + v5) + fine * w[4],
                v5,
                0.5 * (v5 + w[7]) + fine * w[6],
                w[7],
            )
            for t in range(TILE):
                out[spaced(j * TILE + t, many, strips * TILE), :] = values[t]

        per_strip(per_chunk, body, min(per_chunk, 4))


def call(kernel, out_shapes, operands, in_smem=0, scratch=(), flops=0):
    spaces = [pltpu.SMEM] * in_smem + [pltpu.VMEM] * (len(operands) - in_smem)
    specs = [pl.BlockSpec(memory_space=space) for space in spaces]
    moved = 4 * sum(x.size for x in operands)
    return pl.pallas_call(
        kernel,
        out_shape=[jax.ShapeDtypeStruct(shape, jnp.float32) for shape in out_shapes],
        in_specs=specs,
        out_specs=[pl.BlockSpec(memory_space=pltpu.VMEM) for _ in out_shapes],
        scratch_shapes=list(scratch),
        compiler_params=pltpu.CompilerParams(vmem_limit_bytes=VMEM_LIMIT),
        cost_estimate=pl.CostEstimate(flops=flops, bytes_accessed=moved, transcendentals=0),
    )(*operands)


def on_device(density, diffusion, drift_speed, levels, coefficient):
    rows, cols = density.shape[1:]
    doms, grids = lax.axis_size("dom"), lax.axis_size("grp")
    many, strips = rows // TILE, cols // LANES
    per_chunk = strips // SQUARE
    depth = (rows * doms).bit_length() - 1
    tiles = [tiles_of(x[0]) for x in (density, diffusion, drift_speed)]
    squares = [list(range(g, g + SQUARE)) for g in range(0, grids, SQUARE)]
    parity = (lax.axis_index("dom") % 2).astype(jnp.int32)[None]

    def vmem(*shape):
        return pltpu.VMEM(shape, jnp.float32)

    place = (strips, TILE, many, LANES)
    pieces = (strips, many, TILE, LANES)
    far, near, state, keep, weight, *inside = call(
        functools.partial(inner_kernel, per_chunk, depth),
        [(strips, 2 * TILE, LANES)] * 2
        + [place, (3, many, LANES), (4, many, LANES)]
        + [(SQUARE, per_chunk * (many - 2), TILE, LANES)] * (many > 2),
        (parity, levels, coefficient, *tiles),
        3,
        [vmem(*pieces)] + [vmem(strips + 2, *place[1:])] * 2 + [vmem(*place)] * 4,
        flops=40 * rows * cols,
    )
    far_pairs = [(d, d + 1) for d in range(1, doms - 1, 2)]
    near_pairs = [(d, d + 1) for d in range(0, doms, 2)]
    far, near = (
        lax.ppermute(array, "dom", pairs + [(b, a) for a, b in pairs])
        for array, pairs in ((far, far_pairs), (near, near_pairs))
    )
    (outside,) = call(
        functools.partial(edge_kernel, per_chunk),
        [(SQUARE, per_chunk * min(many, 2) + -(-per_chunk // TILE), TILE, LANES)],
        (parity, *tiles, state, weight, far, near),
        1,
        [vmem(*pieces), vmem(3, strips, SLAB, LANES)]
        + [vmem(strips + 2, HALF, TILE, LANES)] * 2
        + [vmem(strips, HALF, TILE, LANES)] * 4,
        flops=40 * SLAB * cols,
    )

    def exchange(array):
        return lax.all_to_all(array, "grp", 0, 0, axis_index_groups=squares, tiled=True)

    def over_grids(weighted):
        (total,) = call(sum_kernel, [weighted.shape[1:]], (exchange(weighted),))
        apart = SQUARE
        while apart < grids:
            other = lax.ppermute(total, "grp", [(g, g ^ apart) for g in range(grids)])
            apart *= 2
            if apart < grids:
                total = total + other
        (spread,) = call(spread_kernel, [weighted.shape], (total, other))
        return exchange(spread)

    totals = [over_grids(weighted) for weighted in (outside, *inside)]
    (nodal,) = call(
        functools.partial(nodal_kernel, per_chunk),
        [(many, strips, TILE, LANES)],
        (keep, *totals),
        0,
        [vmem(*pieces)],
    )
    return block_of(nodal)[None]


def solution(mesh):
    return jax.shard_map(
        on_device,
        mesh=mesh,
        in_specs=(
            P("grp", "dom", None),
            P("grp", "dom", None),
            P("grp", "dom", None),
            P("grp"),
            P("grp"),
        ),
        out_specs=P("grp", "dom", None),
        check_vma=False,
    )
```

```python
import functools

import jax
import jax.numpy as jnp
from jax import lax
from jax.experimental import pallas as pl
from jax.experimental.pallas import tpu as pltpu
from jax.sharding import PartitionSpec as P

STEPS = 4
LANES = 128
TILE = 8
HALF = TILE // 2
SLAB = 4 * TILE
SQUARE = 4
UNROLL = 16
VMEM_LIMIT = 40 * 1024 * 1024


def tiles_of(block):
    rows, cols = block.shape
    return block.reshape(rows // TILE, TILE, cols // LANES, LANES).transpose(0, 2, 1, 3)


def block_of(tiles):
    many, strips = tiles.shape[:2]
    return tiles.transpose(0, 2, 1, 3).reshape(many * TILE, strips * LANES)


def flat(ref):
    return ref.reshape(ref.size // LANES, LANES)


def spaced(first, count, stride):
    return pl.ds(first, count, stride=stride) if count > 1 else pl.ds(first, 1)


def roll_rows(value, shift):
    count = value.shape[0]
    return pltpu.roll(value, shift % count, 0) if count > 1 else value


def per_strip(strips, body, unroll):
    def step(j, carry):
        body(j)
        return carry

    lax.fori_loop(0, strips, step, 0, unroll=unroll)


def advance(first, count, classes, source, coefs, emit):
    shape = source.shape[2:]
    lanes = lax.broadcasted_iota(jnp.int32, shape, 1)
    center, above_c, below_c, side = coefs

    def body(k, carry):
        j = first + k
        cur, right_prev, left_cur = carry
        nxt = [source[j + 2, t] for t in range(classes)]
        left_next = [pltpu.roll(x, LANES - 1, 1) for x in nxt]
        right_cur = [pltpu.roll(x, 1, 1) for x in cur]
        above = cur[1:] + [roll_rows(cur[0], -1)]
        below = [roll_rows(cur[-1], 1)] + cur[:-1]
        new = []
        for t in range(classes):
            left = jnp.where(lanes == 0, right_prev[t], right_cur[t])
            right = jnp.where(lanes == LANES - 1, left_next[t], left_cur[t])
            new.append(
                center[j, t] * cur[t]
                + above_c[j, t] * above[t]
                + below_c[j, t] * below[t]
                + side[j, t] * (left + right)
            )
        emit(j, k, new)
        return nxt, right_cur, left_next

    prev, cur = ([source[first + at, t] for t in range(classes)] for at in range(2))
    ends = [pltpu.roll(x, 1, 1) for x in prev], [pltpu.roll(x, LANES - 1, 1) for x in cur]
    lax.fori_loop(0, count, body, (cur, *ends), unroll=min(count, UNROLL))


def run_steps(strips, classes, load, buffers, coefs, last):
    center, above_c, below_c, side = coefs
    for buf in buffers:
        for edge in (0, strips + 1):
            buf[edge] = jnp.zeros(buf.shape[1:], jnp.float32)

    def begin(j):
        for t in range(classes):
            state, diffuse, drifts = load(j, t)
            half = 0.5 * drifts
            buffers[0][j + 1, t] = state
            center[j, t] = 1.0 - 4.0 * diffuse
            above_c[j, t] = diffuse - half
            below_c[j, t] = diffuse + half
            side[j, t] = diffuse

    per_strip(strips, begin, min(strips, UNROLL))
    for step in range(STEPS - 1):
        source, target = buffers[step % 2], buffers[1 - step % 2]

        def keep(j, _, new, target=target):
            for t in range(classes):
                target[j + 1, t] = new[t]

        advance(0, strips, classes, source, coefs, keep)
    last(buffers[(STEPS - 1) % 2])


def surpluses(s, prev, weight_ref):
    fine, mid, low, coef = (weight_ref[k] for k in range(4))
    return (
        fine * (s[0] - 0.5 * (prev + s[1])),
        mid * (s[1] - 0.5 * (prev + s[3])),
        fine * (s[2] - 0.5 * (s[1] + s[3])),
        low * (s[3] - 0.5 * (prev + s[7])),
        fine * (s[4] - 0.5 * (s[3] + s[5])),
        mid * (s[5] - 0.5 * (s[3] + s[7])),
        fine * (s[6] - 0.5 * (s[5] + s[7])),
        coef * s[7],
    )


def pack_kernel(parity_ref, dens_ref, *refs):
    *ends, far_ref, near_ref = refs
    many, strips = dens_ref.shape[:2]
    odd = parity_ref[0] == 1
    upper = lax.broadcasted_iota(jnp.int32, (TILE, LANES), 0) < HALF

    def body(j):
        heads, tails = ([ref[j] for ref in ends[e::2]] for e in range(2))
        mix_next = jnp.where(upper, pltpu.roll(tails[1], HALF, 0), tails[0])
        mix_prev = jnp.where(upper, heads[0], pltpu.roll(heads[1], HALF, 0))
        to_next, to_prev = (dens_ref[many - 1, j], mix_next), (dens_ref[0, j], mix_prev)
        for k in range(2):
            at = pl.ds(k * TILE, TILE)
            far_ref[j, at] = jnp.where(odd, to_next[k], to_prev[k])
            near_ref[j, at] = jnp.where(odd, to_prev[k], to_next[k])

    per_strip(strips, body, 4)


def inner_kernel(
    depth, level_ref, coef_ref, dens_ref, diff_ref, drift_ref, out_ref, keep_ref, weight_ref,
    state_a, state_b, *coefs
):
    many, strips = dens_ref.shape[:2]
    refs = [flat(ref) for ref in (dens_ref, diff_ref, drift_ref)]

    def load(j, t):
        at = spaced(j * TILE + t, many, strips * TILE)
        return [ref[at, :] for ref in refs]

    def emit(j, _, new):
        for t in range(TILE):
            out_ref[j, t] = new[t]

    def last(source):
        advance(0, strips, TILE, source, coefs, emit)

    run_steps(strips, TILE, load, (state_a, state_b), coefs, last)
    coef = coef_ref[0].astype(jnp.float32)
    for down in range(3):
        keep = jnp.where(level_ref[0] >= depth - down, 1.0, 0.0)
        keep_ref[down] = jnp.full((many, LANES), keep)
        weight_ref[down] = jnp.full((many, LANES), keep * coef)
    weight_ref[3] = jnp.full((many, LANES), coef)


def partners(parity):
    return 0, 1 + parity, 2 - parity, 3


def edge_kernel(per_chunk, parity_ref, me_ref, weight_ref, dens_ref, *refs):
    many, strips = dens_ref.shape[:2]
    odd = parity_ref[0] == 1
    ends, (state_ref, far_ref, near_ref), out_refs = refs[:4], refs[4:7], refs[7:11]
    slab, state_a, state_b, *coefs = refs[11:]

    def stage(j):
        far, near = far_ref[j], near_ref[j]
        up, dn = jnp.where(odd, near, far), jnp.where(odd, far, near)
        up_mix, dn_mix = up[TILE:], dn[TILE:]
        tiles = (
            (up[:TILE], dens_ref[0, j], dens_ref[many - 1, j], dn[:TILE]),
            (up_mix, ends[0][j], ends[1][j], dn_mix),
            (pltpu.roll(up_mix, HALF, 0), ends[2][j], ends[3][j], pltpu.roll(dn_mix, HALF, 0)),
        )
        for k, column in enumerate(tiles):
            for e, tile in enumerate(column):
                slab[k, j, e * TILE : (e + 1) * TILE] = tile

    per_strip(strips, stage, 4)
    slabs = flat(slab)

    def load(j, t):
        return [
            slabs[pl.ds((k * strips + j) * SLAB + t, TILE, stride=HALF), :] for k in range(3)
        ]

    place = lax.broadcasted_iota(jnp.int32, (many, LANES), 0)

    def finish(out_ref, j, part, new):
        s = [state_ref[j, t] for t in range(TILE)]
        for t in range(HALF):
            s[t] = jnp.where(place == 0, new[t][2:3], s[t])
            s[HALF + t] = jnp.where(place == many - 1, new[t][5:6], s[HALF + t])
        before = new[HALF - 1][1:2]
        weighted = surpluses(s, jnp.where(place == 0, before, roll_rows(s[7], 1)), weight_ref)
        for t in range(TILE):
            out_ref[part * TILE + t] = weighted[t]
        out_ref[per_chunk * TILE + part // many, pl.ds(lax.rem(part, many), 1), :] = (
            weight_ref[3][0:1] * before
        )

    def last(source):
        for out_ref, away in zip(out_refs, partners(parity_ref[0])):
            first = (me_ref[0] ^ away) * per_chunk
            emit = functools.partial(finish, out_ref)
            advance(first, per_chunk, HALF, source, coefs, emit)

    run_steps(strips, HALF, load, (state_a, state_b), coefs, last)


def sum_kernel(*refs):
    *parts, out_ref = refs
    total = parts[0][...]
    for part in parts[1:]:
        total = total + part[...]
    out_ref[...] = total


def nodal_kernel(per_chunk, parity_ref, me_ref, keep_ref, *refs):
    *totals, out_ref = refs
    many, strips = out_ref.shape[:2]
    out = flat(out_ref)
    fine, mid, low = (keep_ref[k] for k in range(3))
    place = lax.broadcasted_iota(jnp.int32, (many, LANES), 0)
    for ref, away in zip(totals, partners(parity_ref[0])):
        first = (me_ref[0] ^ away) * per_chunk

        def body(part, ref=ref, first=first):
            w = [ref[part * TILE + t] for t in range(TILE)]
            before = ref[per_chunk * TILE + part // many, pl.ds(lax.rem(part, many), 1), :]
            prev = jnp.where(place == 0, before, roll_rows(w[7], 1))
            v3 = 0.5 * (prev + w[7]) + low * w[3]
            v1 = 0.5 * (prev + v3) + mid * w[1]
            v5 = 0.5 * (v3 + w[7]) + mid * w[5]
            values = (
                0.5 * (prev + v1) + fine * w[0],
                v1,
                0.5 * (v1 + v3) + fine * w[2],
                v3,
                0.5 * (v3 + v5) + fine * w[4],
                v5,
                0.5 * (v5 + w[7]) + fine * w[6],
                w[7],
            )
            for t in range(TILE):
                out[spaced((first + part) * TILE + t, many, strips * TILE), :] = values[t]

        per_strip(per_chunk, body, min(per_chunk, 4))


def call(kernel, out_shapes, operands, in_smem=0, scratch=(), flops=0):
    spaces = [pltpu.SMEM] * in_smem + [pltpu.VMEM] * (len(operands) - in_smem)
    specs = [pl.BlockSpec(memory_space=space) for space in spaces]
    moved = 4 * sum(x.size for x in operands)
    return pl.pallas_call(
        kernel,
        out_shape=[jax.ShapeDtypeStruct(shape, jnp.float32) for shape in out_shapes],
        in_specs=specs,
        out_specs=[pl.BlockSpec(memory_space=pltpu.VMEM) for _ in out_shapes],
        scratch_shapes=list(scratch),
        compiler_params=pltpu.CompilerParams(vmem_limit_bytes=VMEM_LIMIT),
        cost_estimate=pl.CostEstimate(flops=flops, bytes_accessed=moved, transcendentals=0),
    )(*operands)


def on_device(density, diffusion, drift_speed, levels, coefficient):
    rows, cols = density.shape[1:]
    doms, grids = lax.axis_size("dom"), lax.axis_size("grp")
    many, strips = rows // TILE, cols // LANES
    per_chunk = strips // SQUARE
    depth = (rows * doms).bit_length() - 1
    tiles = [tiles_of(x[0]) for x in (density, diffusion, drift_speed)]
    me = (lax.axis_index("grp") % SQUARE).astype(jnp.int32)[None]
    parity = (lax.axis_index("dom") % 2).astype(jnp.int32)[None]

    def vmem(*shape):
        return pltpu.VMEM(shape, jnp.float32)

    ends = [x[at] for x in tiles[1:] for at in (0, many - 1)]
    far, near = call(
        pack_kernel,
        [(strips, 2 * TILE, LANES)] * 2,
        (parity, tiles[0], *ends),
        1,
    )
    far_pairs = [(d, d + 1) for d in range(1, doms - 1, 2)]
    near_pairs = [(d, d + 1) for d in range(0, doms, 2)]
    far, near = (
        lax.ppermute(array, "dom", pairs + [(b, a) for a, b in pairs])
        for array, pairs in ((far, far_pairs), (near, near_pairs))
    )
    place = (strips, TILE, many, LANES)
    state, keep, weight = call(
        functools.partial(inner_kernel, depth),
        [place, (3, many, LANES), (4, many, LANES)],
        (levels, coefficient, *tiles),
        2,
        [vmem(strips + 2, *place[1:])] * 2 + [vmem(*place)] * 4,
        flops=40 * rows * cols,
    )
    chunk = (per_chunk * TILE + -(-per_chunk // many), many, LANES)
    own, *others = call(
        functools.partial(edge_kernel, per_chunk),
        [chunk] * SQUARE,
        (parity, me, weight, tiles[0], *ends, state, far, near),
        2,
        [vmem(3, strips, SLAB, LANES)]
        + [vmem(strips + 2, HALF, TILE, LANES)] * 2
        + [vmem(strips, HALF, TILE, LANES)] * 4,
        flops=40 * SLAB * cols,
    )

    def swap(array, meet):
        devices = [(g, d) for g in range(grids) for d in range(doms)]
        pairs = [(g * doms + d, (g ^ partners(d % 2)[meet]) * doms + d) for g, d in devices]
        return lax.ppermute(array, ("grp", "dom"), pairs)

    theirs = [swap(array, meet) for meet, array in enumerate(others, 1)]
    (total,) = call(sum_kernel, [chunk], (own, *theirs))
    apart = SQUARE
    while apart < grids:
        other = lax.ppermute(total, "grp", [(g, g ^ apart) for g in range(grids)])
        (total,) = call(sum_kernel, [chunk], (total, other))
        apart *= 2
    totals = [total] + [swap(total, meet) for meet in range(1, SQUARE)]
    (nodal,) = call(
        functools.partial(nodal_kernel, per_chunk),
        [(many, strips, TILE, LANES)],
        (parity, me, keep, *totals),
        2,
    )
    return block_of(nodal)[None]


def solution(mesh):
    return jax.shard_map(
        on_device,
        mesh=mesh,
        in_specs=(
            P("grp", "dom", None),
            P("grp", "dom", None),
            P("grp", "dom", None),
            P("grp"),
            P("grp"),
        ),
        out_specs=P("grp", "dom", None),
        check_vma=False,
    )
```

```python
import functools

import jax
import jax.numpy as jnp
from jax import lax
from jax.experimental import pallas as pl
from jax.experimental.pallas import tpu as pltpu
from jax.sharding import PartitionSpec as P

STEPS = 4
LANES = 128
TILE = 8
HALF = TILE // 2
SLAB = 4 * TILE
SQUARE = 4
UNROLL = 16
VMEM_LIMIT = 40 * 1024 * 1024
HALO_FLOPS = 4000


def tiles_of(block):
    rows, cols = block.shape
    return block.reshape(rows // TILE, TILE, cols // LANES, LANES).transpose(0, 2, 1, 3)


def block_of(tiles):
    many, strips = tiles.shape[:2]
    return tiles.transpose(0, 2, 1, 3).reshape(many * TILE, strips * LANES)


def flat(ref):
    return ref.reshape(ref.size // LANES, LANES)


def spaced(first, count, stride):
    return pl.ds(first, count, stride=stride) if count > 1 else pl.ds(first, 1)


def roll_rows(value, shift):
    count = value.shape[0]
    return pltpu.roll(value, shift % count, 0) if count > 1 else value


def per_strip(strips, body, unroll):
    def step(j, carry):
        body(j)
        return carry

    lax.fori_loop(0, strips, step, 0, unroll=unroll)


def advance(first, count, classes, source, coefs, emit):
    shape = source.shape[2:]
    lanes = lax.broadcasted_iota(jnp.int32, shape, 1)
    center, above_c, below_c, side = coefs

    def body(k, carry):
        j = first + k
        cur, right_prev, left_cur = carry
        nxt = [source[j + 2, t] for t in range(classes)]
        left_next = [pltpu.roll(x, LANES - 1, 1) for x in nxt]
        right_cur = [pltpu.roll(x, 1, 1) for x in cur]
        above = cur[1:] + [roll_rows(cur[0], -1)]
        below = [roll_rows(cur[-1], 1)] + cur[:-1]
        new = []
        for t in range(classes):
            left = jnp.where(lanes == 0, right_prev[t], right_cur[t])
            right = jnp.where(lanes == LANES - 1, left_next[t], left_cur[t])
            new.append(
                center[j, t] * cur[t]
                + above_c[j, t] * above[t]
                + below_c[j, t] * below[t]
                + side[j, t] * (left + right)
            )
        emit(j, k, new)
        return nxt, right_cur, left_next

    prev, cur = ([source[first + at, t] for t in range(classes)] for at in range(2))
    ends = [pltpu.roll(x, 1, 1) for x in prev], [pltpu.roll(x, LANES - 1, 1) for x in cur]
    lax.fori_loop(0, count, body, (cur, *ends), unroll=min(count, UNROLL))


def run_steps(strips, classes, load, buffers, coefs, last):
    center, above_c, below_c, side = coefs
    for buf in buffers:
        for edge in (0, strips + 1):
            buf[edge] = jnp.zeros(buf.shape[1:], jnp.float32)

    def begin(j):
        for t in range(classes):
            state, diffuse, drifts = load(j, t)
            half = 0.5 * drifts
            buffers[0][j + 1, t] = state
            center[j, t] = 1.0 - 4.0 * diffuse
            above_c[j, t] = diffuse - half
            below_c[j, t] = diffuse + half
            side[j, t] = diffuse

    per_strip(strips, begin, min(strips, UNROLL))
    for step in range(STEPS - 1):
        source, target = buffers[step % 2], buffers[1 - step % 2]

        def keep(j, _, new, target=target):
            for t in range(classes):
                target[j + 1, t] = new[t]

        advance(0, strips, classes, source, coefs, keep)
    last(buffers[(STEPS - 1) % 2])


def surpluses(s, prev, weights):
    fine, mid, low, coef = weights
    return (
        fine * (s[0] - 0.5 * (prev + s[1])),
        mid * (s[1] - 0.5 * (prev + s[3])),
        fine * (s[2] - 0.5 * (s[1] + s[3])),
        low * (s[3] - 0.5 * (prev + s[7])),
        fine * (s[4] - 0.5 * (s[3] + s[5])),
        mid * (s[5] - 0.5 * (s[3] + s[7])),
        fine * (s[6] - 0.5 * (s[5] + s[7])),
        coef * s[7],
    )


def pack_kernel(parity_ref, dens_ref, *refs):
    *ends, far_ref, near_ref = refs
    many, strips = dens_ref.shape[:2]
    odd = parity_ref[0] == 1
    upper = lax.broadcasted_iota(jnp.int32, (TILE, LANES), 0) < HALF

    def body(j):
        heads, tails = ([ref[j] for ref in ends[e::2]] for e in range(2))
        mix_next = jnp.where(upper, pltpu.roll(tails[1], HALF, 0), tails[0])
        mix_prev = jnp.where(upper, heads[0], pltpu.roll(heads[1], HALF, 0))
        to_next, to_prev = (dens_ref[many - 1, j], mix_next), (dens_ref[0, j], mix_prev)
        for k in range(2):
            at = pl.ds(k * TILE, TILE)
            far_ref[j, at] = jnp.where(odd, to_next[k], to_prev[k])
            near_ref[j, at] = jnp.where(odd, to_prev[k], to_next[k])

    per_strip(strips, body, 4)


def inner_kernel(dens_ref, diff_ref, drift_ref, out_ref, state_a, state_b, *coefs):
    many, strips = dens_ref.shape[:2]
    refs = [flat(ref) for ref in (dens_ref, diff_ref, drift_ref)]

    def load(j, t):
        at = spaced(j * TILE + t, many, strips * TILE)
        return [ref[at, :] for ref in refs]

    def emit(j, _, new):
        for t in range(TILE):
            out_ref[j, t] = new[t]

    def last(source):
        advance(0, strips, TILE, source, coefs, emit)

    run_steps(strips, TILE, load, (state_a, state_b), coefs, last)


def partners(parity):
    return 0, 1 + parity, 2 - parity, 3


def edge_kernel(
    per_chunk, depth, parity_ref, me_ref, level_ref, coef_ref, dens_ref, *refs
):
    many, strips = dens_ref.shape[:2]
    odd = parity_ref[0] == 1
    ends, (state_ref, far_ref, near_ref), out_refs = refs[:4], refs[4:7], refs[7:11]
    slab, state_a, state_b, *coefs = refs[11:]

    def stage(j):
        far, near = far_ref[j], near_ref[j]
        up, dn = jnp.where(odd, near, far), jnp.where(odd, far, near)
        up_mix, dn_mix = up[TILE:], dn[TILE:]
        tiles = (
            (up[:TILE], dens_ref[0, j], dens_ref[many - 1, j], dn[:TILE]),
            (up_mix, ends[0][j], ends[1][j], dn_mix),
            (pltpu.roll(up_mix, HALF, 0), ends[2][j], ends[3][j], pltpu.roll(dn_mix, HALF, 0)),
        )
        for k, column in enumerate(tiles):
            for e, tile in enumerate(column):
                slab[k, j, e * TILE : (e + 1) * TILE] = tile

    per_strip(strips, stage, 4)
    slabs = flat(slab)

    def load(j, t):
        return [
            slabs[pl.ds((k * strips + j) * SLAB + t, TILE, stride=HALF), :] for k in range(3)
        ]

    place = lax.broadcasted_iota(jnp.int32, (many, LANES), 0)
    coef = coef_ref[0].astype(jnp.float32)
    weights = [jnp.where(level_ref[0] >= depth - down, coef, 0.0) for down in range(3)] + [coef]

    def finish(out_ref, j, part, new):
        s = [state_ref[j, t] for t in range(TILE)]
        for t in range(HALF):
            s[t] = jnp.where(place == 0, new[t][2:3], s[t])
            s[HALF + t] = jnp.where(place == many - 1, new[t][5:6], s[HALF + t])
        before = new[HALF - 1][1:2]
        weighted = surpluses(s, jnp.where(place == 0, before, roll_rows(s[7], 1)), weights)
        for t in range(TILE):
            out_ref[part * TILE + t] = weighted[t]
        out_ref[per_chunk * TILE + part // many, pl.ds(lax.rem(part, many), 1), :] = (
            coef * before
        )

    def last(source):
        for out_ref, away in zip(out_refs, partners(parity_ref[0])):
            first = (me_ref[0] ^ away) * per_chunk
            emit = functools.partial(finish, out_ref)
            advance(first, per_chunk, HALF, source, coefs, emit)

    run_steps(strips, HALF, load, (state_a, state_b), coefs, last)


def sum_kernel(*refs):
    *parts, out_ref = refs
    total = parts[0][...]
    for part in parts[1:]:
        total = total + part[...]
    out_ref[...] = total


def nodal_kernel(per_chunk, depth, meets, parity_ref, me_ref, level_ref, *refs):
    totals, (out_ref, values, sems) = refs[: len(meets)], refs[-3:]
    many = values.shape[1]
    level = level_ref[0]
    fine, mid, low = (jnp.where(level >= depth - down, 1.0, 0.0) for down in range(3))
    place = lax.broadcasted_iota(jnp.int32, (many, LANES), 0)
    copies = []
    for k, (ref, meet) in enumerate(zip(totals, meets)):
        first = (me_ref[0] ^ partners(parity_ref[0])[meet]) * per_chunk
        by_row = flat(values.at[k])

        def body(part, ref=ref, by_row=by_row):
            w = [ref[part * TILE + t] for t in range(TILE)]
            before = ref[per_chunk * TILE + part // many, pl.ds(lax.rem(part, many), 1), :]
            prev = jnp.where(place == 0, before, roll_rows(w[7], 1))
            v3 = 0.5 * (prev + w[7]) + low * w[3]
            v1 = 0.5 * (prev + v3) + mid * w[1]
            v5 = 0.5 * (v3 + w[7]) + mid * w[5]
            rows = (
                0.5 * (prev + v1) + fine * w[0],
                v1,
                0.5 * (v1 + v3) + fine * w[2],
                v3,
                0.5 * (v3 + v5) + fine * w[4],
                v5,
                0.5 * (v5 + w[7]) + fine * w[6],
                w[7],
            )
            for t in range(TILE):
                by_row[spaced(part * TILE + t, many, per_chunk * TILE), :] = rows[t]

        per_strip(per_chunk, body, min(per_chunk, 4))
        for m in range(many):
            copy = pltpu.make_async_copy(
                values.at[k, m], out_ref.at[m, pl.ds(first, per_chunk)], sems.at[k, m]
            )
            copy.start()
            copies.append(copy)
    for copy in copies:
        copy.wait()


def call(
    kernel, out_shapes, operands, in_smem=0, scratch=(), flops=0, out_space=pltpu.VMEM, onto=None
):
    spaces = [pltpu.SMEM] * in_smem + [pltpu.VMEM] * (len(operands) - in_smem)
    alias = {}
    if onto is not None:
        alias = {len(operands): 0}
        spaces, operands = spaces + [out_space], (*operands, onto)
    specs = [pl.BlockSpec(memory_space=space) for space in spaces]
    moved = 4 * sum(x.size for x in operands)
    return pl.pallas_call(
        kernel,
        out_shape=[jax.ShapeDtypeStruct(shape, jnp.float32) for shape in out_shapes],
        in_specs=specs,
        out_specs=[pl.BlockSpec(memory_space=out_space) for _ in out_shapes],
        input_output_aliases=alias,
        scratch_shapes=list(scratch),
        compiler_params=pltpu.CompilerParams(vmem_limit_bytes=VMEM_LIMIT),
        cost_estimate=pl.CostEstimate(flops=flops, bytes_accessed=moved, transcendentals=0),
    )(*operands)


def on_device(density, diffusion, drift_speed, levels, coefficient):
    rows, cols = density.shape[1:]
    doms, grids = lax.axis_size("dom"), lax.axis_size("grp")
    many, strips = rows // TILE, cols // LANES
    per_chunk = strips // SQUARE
    depth = (rows * doms).bit_length() - 1
    tiles = [tiles_of(x[0]) for x in (density, diffusion, drift_speed)]
    me = (lax.axis_index("grp") % SQUARE).astype(jnp.int32)[None]
    parity = (lax.axis_index("dom") % 2).astype(jnp.int32)[None]

    def vmem(*shape):
        return pltpu.VMEM(shape, jnp.float32)

    ends = [x[at] for x in tiles[1:] for at in (0, many - 1)]
    far, near = call(
        pack_kernel,
        [(strips, 2 * TILE, LANES)] * 2,
        (parity, tiles[0], *ends),
        1,
        flops=HALO_FLOPS * rows * cols,
    )
    far_pairs = [(d, d + 1) for d in range(1, doms - 1, 2)]
    near_pairs = [(d, d + 1) for d in range(0, doms, 2)]
    far, near = (
        lax.ppermute(array, "dom", pairs + [(b, a) for a, b in pairs])
        for array, pairs in ((far, far_pairs), (near, near_pairs))
    )
    place = (strips, TILE, many, LANES)
    (state,) = call(
        inner_kernel,
        [place],
        tiles,
        0,
        [vmem(strips + 2, *place[1:])] * 2 + [vmem(*place)] * 4,
        flops=40 * rows * cols,
    )
    chunk = (per_chunk * TILE + -(-per_chunk // many), many, LANES)
    own, *others = call(
        functools.partial(edge_kernel, per_chunk, depth),
        [chunk] * SQUARE,
        (parity, me, levels, coefficient, tiles[0], *ends, state, far, near),
        4,
        [vmem(3, strips, SLAB, LANES)]
        + [vmem(strips + 2, HALF, TILE, LANES)] * 2
        + [vmem(strips, HALF, TILE, LANES)] * 4,
        flops=40 * SLAB * cols,
    )

    def swap(array, meet):
        devices = [(g, d) for g in range(grids) for d in range(doms)]
        pairs = [(g * doms + d, (g ^ partners(d % 2)[meet]) * doms + d) for g, d in devices]
        return lax.ppermute(array, ("grp", "dom"), pairs)

    theirs = [swap(array, meet) for meet, array in enumerate(others, 1)]
    (total,) = call(sum_kernel, [chunk], (own, *theirs))
    apart = SQUARE
    while apart < grids:
        other = lax.ppermute(total, "grp", [(g, g ^ apart) for g in range(grids)])
        (total,) = call(sum_kernel, [chunk], (total, other))
        apart *= 2
    totals = [total] + [swap(total, meet) for meet in range(1, SQUARE)]
    nodal = None
    for meets in ((0, 1, 2), (3,)):
        (nodal,) = call(
            functools.partial(nodal_kernel, per_chunk, depth, meets),
            [(many, strips, TILE, LANES)],
            (parity, me, levels, *(totals[meet] for meet in meets)),
            3,
            [
                vmem(len(meets), many, per_chunk, TILE, LANES),
                pltpu.SemaphoreType.DMA((len(meets), many)),
            ],
            out_space=pl.ANY,
            onto=nodal,
        )
    return block_of(nodal)[None]


def solution(mesh):
    return jax.shard_map(
        on_device,
        mesh=mesh,
        in_specs=(
            P("grp", "dom", None),
            P("grp", "dom", None),
            P("grp", "dom", None),
            P("grp"),
            P("grp"),
        ),
        out_specs=P("grp", "dom", None),
        check_vma=False,
    )
```

```python
import functools

import jax
import jax.numpy as jnp
from jax import lax
from jax.experimental import pallas as pl
from jax.experimental.pallas import tpu as pltpu
from jax.sharding import PartitionSpec as P

STEPS = 4
LANES = 128
TILE = 8
HALF = TILE // 2
SLAB = 4 * TILE
SQUARE = 4
UNROLL = 16
VMEM_LIMIT = 40 * 1024 * 1024
HALO_FLOPS = 4000


def tiles_of(block):
    rows, cols = block.shape
    return block.reshape(rows // TILE, TILE, cols // LANES, LANES).transpose(0, 2, 1, 3)


def block_of(tiles):
    many, strips = tiles.shape[:2]
    return tiles.transpose(0, 2, 1, 3).reshape(many * TILE, strips * LANES)


def flat(ref):
    return ref.reshape(ref.size // LANES, LANES)


def spaced(first, count, stride):
    return pl.ds(first, count, stride=stride) if count > 1 else pl.ds(first, 1)


def roll_rows(value, shift):
    count = value.shape[0]
    return pltpu.roll(value, shift % count, 0) if count > 1 else value


def per_strip(strips, body, unroll):
    def step(j, carry):
        body(j)
        return carry

    lax.fori_loop(0, strips, step, 0, unroll=unroll)


def advance(first, count, classes, source, coefs, emit):
    shape = source.shape[2:]
    lanes = lax.broadcasted_iota(jnp.int32, shape, 1)
    center, above_c, below_c, side = coefs

    def body(k, carry):
        j = first + k
        cur, right_prev, left_cur = carry
        nxt = [source[j + 2, t] for t in range(classes)]
        left_next = [pltpu.roll(x, LANES - 1, 1) for x in nxt]
        right_cur = [pltpu.roll(x, 1, 1) for x in cur]
        above = cur[1:] + [roll_rows(cur[0], -1)]
        below = [roll_rows(cur[-1], 1)] + cur[:-1]
        new = []
        for t in range(classes):
            left = jnp.where(lanes == 0, right_prev[t], right_cur[t])
            right = jnp.where(lanes == LANES - 1, left_next[t], left_cur[t])
            new.append(
                center[j, t] * cur[t]
                + above_c[j, t] * above[t]
                + below_c[j, t] * below[t]
                + side[j, t] * (left + right)
            )
        emit(j, k, new)
        return nxt, right_cur, left_next

    prev, cur = ([source[first + at, t] for t in range(classes)] for at in range(2))
    ends = [pltpu.roll(x, 1, 1) for x in prev], [pltpu.roll(x, LANES - 1, 1) for x in cur]
    lax.fori_loop(0, count, body, (cur, *ends), unroll=min(count, UNROLL))


def run_steps(strips, classes, load, buffers, coefs, last):
    center, above_c, below_c, side = coefs
    for buf in buffers:
        for edge in (0, strips + 1):
            buf[edge] = jnp.zeros(buf.shape[1:], jnp.float32)

    def begin(j):
        for t in range(classes):
            state, diffuse, drifts = load(j, t)
            half = 0.5 * drifts
            buffers[0][j + 1, t] = state
            center[j, t] = 1.0 - 4.0 * diffuse
            above_c[j, t] = diffuse - half
            below_c[j, t] = diffuse + half
            side[j, t] = diffuse

    per_strip(strips, begin, min(strips, UNROLL))
    for step in range(STEPS - 1):
        source, target = buffers[step % 2], buffers[1 - step % 2]

        def keep(j, _, new, target=target):
            for t in range(classes):
                target[j + 1, t] = new[t]

        advance(0, strips, classes, source, coefs, keep)
    last(buffers[(STEPS - 1) % 2])


def surpluses(s, prev, weights):
    fine, mid, low, coef = weights
    return (
        fine * (s[0] - 0.5 * (prev + s[1])),
        mid * (s[1] - 0.5 * (prev + s[3])),
        fine * (s[2] - 0.5 * (s[1] + s[3])),
        low * (s[3] - 0.5 * (prev + s[7])),
        fine * (s[4] - 0.5 * (s[3] + s[5])),
        mid * (s[5] - 0.5 * (s[3] + s[7])),
        fine * (s[6] - 0.5 * (s[5] + s[7])),
        coef * s[7],
    )


def pack_kernel(dom_ref, dens_ref, *refs):
    *ends, far_ref, near_ref = refs
    many, strips = dens_ref.shape[:2]
    odd = dom_ref[0] % 2 == 1
    upper = lax.broadcasted_iota(jnp.int32, (TILE, LANES), 0) < HALF

    def body(j):
        heads, tails = ([ref[j] for ref in ends[e::2]] for e in range(2))
        mix_next = jnp.where(upper, pltpu.roll(tails[1], HALF, 0), tails[0])
        mix_prev = jnp.where(upper, heads[0], pltpu.roll(heads[1], HALF, 0))
        to_next, to_prev = (dens_ref[many - 1, j], mix_next), (dens_ref[0, j], mix_prev)
        for k in range(2):
            at = pl.ds(k * TILE, TILE)
            far_ref[j, at] = jnp.where(odd, to_next[k], to_prev[k])
            near_ref[j, at] = jnp.where(odd, to_prev[k], to_next[k])

    per_strip(strips, body, 4)


def inner_kernel(dens_ref, diff_ref, drift_ref, out_ref, state_a, state_b, *coefs):
    many, strips = dens_ref.shape[:2]
    refs = [flat(ref) for ref in (dens_ref, diff_ref, drift_ref)]

    def load(j, t):
        at = spaced(j * TILE + t, many, strips * TILE)
        return [ref[at, :] for ref in refs]

    def emit(j, _, new):
        for t in range(TILE):
            out_ref[j, t] = new[t]

    def last(source):
        advance(0, strips, TILE, source, coefs, emit)

    run_steps(strips, TILE, load, (state_a, state_b), coefs, last)


def partners(dom):
    return 0, 1 + dom % 2, 2 - dom % 2, 3


def edge_kernel(
    per_chunk, depth, doms, dom_ref, me_ref, level_ref, coef_ref, dens_ref, *refs
):
    many, strips = dens_ref.shape[:2]
    dom = dom_ref[0]
    odd = dom % 2 == 1
    ends, (state_ref, far_ref, near_ref), out_refs = refs[:4], refs[4:7], refs[7:11]
    slab, state_a, state_b, *coefs = refs[11:]

    def stage(j):
        far, near = far_ref[j], near_ref[j]
        up = jnp.where(dom == 0, 0.0, jnp.where(odd, near, far))
        dn = jnp.where(dom == doms - 1, 0.0, jnp.where(odd, far, near))
        up_mix, dn_mix = up[TILE:], dn[TILE:]
        tiles = (
            (up[:TILE], dens_ref[0, j], dens_ref[many - 1, j], dn[:TILE]),
            (up_mix, ends[0][j], ends[1][j], dn_mix),
            (pltpu.roll(up_mix, HALF, 0), ends[2][j], ends[3][j], pltpu.roll(dn_mix, HALF, 0)),
        )
        for k, column in enumerate(tiles):
            for e, tile in enumerate(column):
                slab[k, j, e * TILE : (e + 1) * TILE] = tile

    per_strip(strips, stage, 4)
    slabs = flat(slab)

    def load(j, t):
        return [
            slabs[pl.ds((k * strips + j) * SLAB + t, TILE, stride=HALF), :] for k in range(3)
        ]

    place = lax.broadcasted_iota(jnp.int32, (many, LANES), 0)
    coef = coef_ref[0].astype(jnp.float32)
    weights = [jnp.where(level_ref[0] >= depth - down, coef, 0.0) for down in range(3)] + [coef]

    def finish(out_ref, j, part, new):
        s = [state_ref[j, t] for t in range(TILE)]
        for t in range(HALF):
            s[t] = jnp.where(place == 0, new[t][2:3], s[t])
            s[HALF + t] = jnp.where(place == many - 1, new[t][5:6], s[HALF + t])
        before = new[HALF - 1][1:2]
        weighted = surpluses(s, jnp.where(place == 0, before, roll_rows(s[7], 1)), weights)
        for t in range(TILE):
            out_ref[part * TILE + t] = weighted[t]
        out_ref[per_chunk * TILE + part // many, pl.ds(lax.rem(part, many), 1), :] = (
            coef * before
        )

    def last(source):
        for out_ref, away in zip(out_refs, partners(dom_ref[0])):
            first = (me_ref[0] ^ away) * per_chunk
            emit = functools.partial(finish, out_ref)
            advance(first, per_chunk, HALF, source, coefs, emit)

    run_steps(strips, HALF, load, (state_a, state_b), coefs, last)


def sum_kernel(*refs):
    *parts, out_ref = refs
    total = parts[0][...]
    for part in parts[1:]:
        total = total + part[...]
    out_ref[...] = total


def nodal_kernel(per_chunk, depth, dom_ref, me_ref, level_ref, *refs):
    *totals, out_ref, values, sems = refs
    many = values.shape[1]
    level = level_ref[0]
    fine, mid, low = (jnp.where(level >= depth - down, 1.0, 0.0) for down in range(3))
    place = lax.broadcasted_iota(jnp.int32, (many, LANES), 0)
    copies = []
    for k, (ref, away) in enumerate(zip(totals, partners(dom_ref[0]))):
        first = (me_ref[0] ^ away) * per_chunk
        by_row = flat(values.at[k])

        def body(part, ref=ref, by_row=by_row):
            w = [ref[part * TILE + t] for t in range(TILE)]
            before = ref[per_chunk * TILE + part // many, pl.ds(lax.rem(part, many), 1), :]
            prev = jnp.where(place == 0, before, roll_rows(w[7], 1))
            v3 = 0.5 * (prev + w[7]) + low * w[3]
            v1 = 0.5 * (prev + v3) + mid * w[1]
            v5 = 0.5 * (v3 + w[7]) + mid * w[5]
            rows = (
                0.5 * (prev + v1) + fine * w[0],
                v1,
                0.5 * (v1 + v3) + fine * w[2],
                v3,
                0.5 * (v3 + v5) + fine * w[4],
                v5,
                0.5 * (v5 + w[7]) + fine * w[6],
                w[7],
            )
            for t in range(TILE):
                by_row[spaced(part * TILE + t, many, per_chunk * TILE), :] = rows[t]

        per_strip(per_chunk, body, min(per_chunk, 4))
        for m in range(many):
            copy = pltpu.make_async_copy(
                values.at[k, m], out_ref.at[m, pl.ds(first, per_chunk)], sems.at[k, m]
            )
            copy.start()
            copies.append(copy)
    for copy in copies:
        copy.wait()


def call(
    kernel, out_shapes, operands, in_smem=0, scratch=(), flops=0, out_space=pltpu.VMEM
):
    spaces = [pltpu.SMEM] * in_smem + [pltpu.VMEM] * (len(operands) - in_smem)
    specs = [pl.BlockSpec(memory_space=space) for space in spaces]
    moved = 4 * sum(x.size for x in operands)
    return pl.pallas_call(
        kernel,
        out_shape=[jax.ShapeDtypeStruct(shape, jnp.float32) for shape in out_shapes],
        in_specs=specs,
        out_specs=[pl.BlockSpec(memory_space=out_space) for _ in out_shapes],
        scratch_shapes=list(scratch),
        compiler_params=pltpu.CompilerParams(vmem_limit_bytes=VMEM_LIMIT),
        cost_estimate=pl.CostEstimate(flops=flops, bytes_accessed=moved, transcendentals=0),
    )(*operands)


def on_device(density, diffusion, drift_speed, levels, coefficient):
    rows, cols = density.shape[1:]
    doms, grids = lax.axis_size("dom"), lax.axis_size("grp")
    many, strips = rows // TILE, cols // LANES
    per_chunk = strips // SQUARE
    depth = (rows * doms).bit_length() - 1
    tiles = [tiles_of(x[0]) for x in (density, diffusion, drift_speed)]
    me = (lax.axis_index("grp") % SQUARE).astype(jnp.int32)[None]
    dom = lax.axis_index("dom").astype(jnp.int32)[None]

    def vmem(*shape):
        return pltpu.VMEM(shape, jnp.float32)

    ends = [x[at] for x in tiles[1:] for at in (0, many - 1)]
    far, near = call(
        pack_kernel,
        [(strips, 2 * TILE, LANES)] * 2,
        (dom, tiles[0], *ends),
        1,
        flops=HALO_FLOPS * rows * cols,
    )
    near_pairs = [(d, d ^ 1) for d in range(doms)]
    far_pairs = [(d, min(max((d - 1 ^ 1) + 1, 0), doms - 1)) for d in range(doms)]
    far, near = (
        lax.ppermute(array, "dom", pairs) for array, pairs in ((far, far_pairs), (near, near_pairs))
    )
    place = (strips, TILE, many, LANES)
    (state,) = call(
        inner_kernel,
        [place],
        tiles,
        0,
        [vmem(strips + 2, *place[1:])] * 2 + [vmem(*place)] * 4,
        flops=40 * rows * cols,
    )
    chunk = (per_chunk * TILE + -(-per_chunk // many), many, LANES)
    own, *others = call(
        functools.partial(edge_kernel, per_chunk, depth, doms),
        [chunk] * SQUARE,
        (dom, me, levels, coefficient, tiles[0], *ends, state, far, near),
        4,
        [vmem(3, strips, SLAB, LANES)]
        + [vmem(strips + 2, HALF, TILE, LANES)] * 2
        + [vmem(strips, HALF, TILE, LANES)] * 4,
        flops=40 * SLAB * cols,
    )

    def swap(array, meet):
        devices = [(g, d) for g in range(grids) for d in range(doms)]
        pairs = [(g * doms + d, (g ^ partners(d % 2)[meet]) * doms + d) for g, d in devices]
        return lax.ppermute(array, ("grp", "dom"), pairs)

    theirs = [swap(array, meet) for meet, array in enumerate(others, 1)]
    (total,) = call(sum_kernel, [chunk], (own, *theirs))
    apart = SQUARE
    while apart < grids:
        other = lax.ppermute(total, "grp", [(g, g ^ apart) for g in range(grids)])
        (total,) = call(sum_kernel, [chunk], (total, other))
        apart *= 2
    totals = [total] + [swap(total, meet) for meet in range(1, SQUARE)]
    (nodal,) = call(
        functools.partial(nodal_kernel, per_chunk, depth),
        [(many, strips, TILE, LANES)],
        (dom, me, levels, *totals),
        3,
        [vmem(SQUARE, many, per_chunk, TILE, LANES), pltpu.SemaphoreType.DMA((SQUARE, many))],
        out_space=pl.ANY,
    )
    return block_of(nodal)[None]


def solution(mesh):
    return jax.shard_map(
        on_device,
        mesh=mesh,
        in_specs=(
            P("grp", "dom", None),
            P("grp", "dom", None),
            P("grp", "dom", None),
            P("grp"),
            P("grp"),
        ),
        out_specs=P("grp", "dom", None),
        check_vma=False,
    )
```

```python
import functools

import jax
import jax.numpy as jnp
from jax import lax
from jax.experimental import pallas as pl
from jax.experimental.pallas import tpu as pltpu
from jax.sharding import PartitionSpec as P

STEPS = 4
LANES = 128
TILE = 8
HALF = TILE // 2
SLAB = 4 * TILE
SQUARE = 4
UNROLL = 16
VMEM_LIMIT = 40 * 1024 * 1024
HALO_FLOPS = 4000


def tiles_of(block):
    rows, cols = block.shape
    return block.reshape(rows // TILE, TILE, cols // LANES, LANES).transpose(0, 2, 1, 3)


def block_of(tiles):
    many, strips = tiles.shape[:2]
    return tiles.transpose(0, 2, 1, 3).reshape(many * TILE, strips * LANES)


def flat(ref):
    return ref.reshape(ref.size // LANES, LANES)


def spaced(first, count, stride):
    return pl.ds(first, count, stride=stride) if count > 1 else pl.ds(first, 1)


def roll_rows(value, shift):
    count = value.shape[0]
    return pltpu.roll(value, shift % count, 0) if count > 1 else value


def per_strip(strips, body, unroll):
    def step(j, carry):
        body(j)
        return carry

    lax.fori_loop(0, strips, step, 0, unroll=unroll)


def advance(first, count, classes, source, coefs, emit):
    shape = source.shape[2:]
    lanes = lax.broadcasted_iota(jnp.int32, shape, 1)
    center, above_c, below_c, side = coefs

    def body(k, carry):
        j = first + k
        cur, right_prev, left_cur = carry
        nxt = [source[j + 2, t] for t in range(classes)]
        left_next = [pltpu.roll(x, LANES - 1, 1) for x in nxt]
        right_cur = [pltpu.roll(x, 1, 1) for x in cur]
        above = cur[1:] + [roll_rows(cur[0], -1)]
        below = [roll_rows(cur[-1], 1)] + cur[:-1]
        new = []
        for t in range(classes):
            left = jnp.where(lanes == 0, right_prev[t], right_cur[t])
            right = jnp.where(lanes == LANES - 1, left_next[t], left_cur[t])
            new.append(
                center[j, t] * cur[t]
                + above_c[j, t] * above[t]
                + below_c[j, t] * below[t]
                + side[j, t] * (left + right)
            )
        emit(j, k, new)
        return nxt, right_cur, left_next

    prev, cur = ([source[first + at, t] for t in range(classes)] for at in range(2))
    ends = [pltpu.roll(x, 1, 1) for x in prev], [pltpu.roll(x, LANES - 1, 1) for x in cur]
    lax.fori_loop(0, count, body, (cur, *ends), unroll=min(count, UNROLL))


def run_steps(strips, classes, load, buffers, coefs, last):
    center, above_c, below_c, side = coefs
    for buf in buffers:
        for edge in (0, strips + 1):
            buf[edge] = jnp.zeros(buf.shape[1:], jnp.float32)

    def begin(j):
        for t in range(classes):
            state, diffuse, drifts = load(j, t)
            half = 0.5 * drifts
            buffers[0][j + 1, t] = state
            center[j, t] = 1.0 - 4.0 * diffuse
            above_c[j, t] = diffuse - half
            below_c[j, t] = diffuse + half
            side[j, t] = diffuse

    per_strip(strips, begin, min(strips, UNROLL))
    for step in range(STEPS - 1):
        source, target = buffers[step % 2], buffers[1 - step % 2]

        def keep(j, _, new, target=target):
            for t in range(classes):
                target[j + 1, t] = new[t]

        advance(0, strips, classes, source, coefs, keep)
    last(buffers[(STEPS - 1) % 2])


def surpluses(s, prev, weights):
    fine, mid, low, coef = weights
    return (
        fine * (s[0] - 0.5 * (prev + s[1])),
        mid * (s[1] - 0.5 * (prev + s[3])),
        fine * (s[2] - 0.5 * (s[1] + s[3])),
        low * (s[3] - 0.5 * (prev + s[7])),
        fine * (s[4] - 0.5 * (s[3] + s[5])),
        mid * (s[5] - 0.5 * (s[3] + s[7])),
        fine * (s[6] - 0.5 * (s[5] + s[7])),
        coef * s[7],
    )


def first_kernel(out_ref):
    out_ref[...] = jnp.zeros(out_ref.shape, jnp.float32)


def pack_kernel(dom_ref, ready_ref, dens_ref, *refs):
    del ready_ref
    diff_ref, drift_ref, far_ref, near_ref = refs
    many, strips = dens_ref.shape[:2]
    odd = dom_ref[0] % 2 == 1
    upper = lax.broadcasted_iota(jnp.int32, (TILE, LANES), 0) < HALF

    def body(j):
        mix_next = jnp.where(upper, pltpu.roll(drift_ref[many - 1, j], HALF, 0), diff_ref[many - 1, j])
        mix_prev = jnp.where(upper, diff_ref[0, j], pltpu.roll(drift_ref[0, j], HALF, 0))
        to_next, to_prev = (dens_ref[many - 1, j], mix_next), (dens_ref[0, j], mix_prev)
        for k in range(2):
            at = pl.ds(k * TILE, TILE)
            far_ref[j, at] = jnp.where(odd, to_next[k], to_prev[k])
            near_ref[j, at] = jnp.where(odd, to_prev[k], to_next[k])

    per_strip(strips, body, 4)


def inner_kernel(dens_ref, diff_ref, drift_ref, out_ref, state_a, state_b, *coefs):
    many, strips = dens_ref.shape[:2]
    refs = [flat(ref) for ref in (dens_ref, diff_ref, drift_ref)]

    def load(j, t):
        at = spaced(j * TILE + t, many, strips * TILE)
        return [ref[at, :] for ref in refs]

    def emit(j, _, new):
        for t in range(TILE):
            out_ref[j, t] = new[t]

    def last(source):
        advance(0, strips, TILE, source, coefs, emit)

    run_steps(strips, TILE, load, (state_a, state_b), coefs, last)


def partners(dom):
    return 0, 1 + dom % 2, 2 - dom % 2, 3


def edge_kernel(
    per_chunk, depth, doms, dom_ref, me_ref, level_ref, coef_ref, dens_ref, *refs
):
    many, strips = dens_ref.shape[:2]
    dom = dom_ref[0]
    odd = dom % 2 == 1
    diff_ref, drift_ref, state_ref, far_ref, near_ref, *rest = refs
    out_refs, (slab, state_a, state_b, *coefs) = rest[:SQUARE], rest[SQUARE:]

    def stage(j):
        far, near = far_ref[j], near_ref[j]
        up = jnp.where(dom == 0, 0.0, jnp.where(odd, near, far))
        dn = jnp.where(dom == doms - 1, 0.0, jnp.where(odd, far, near))
        up_mix, dn_mix = up[TILE:], dn[TILE:]
        tiles = (
            (up[:TILE], dens_ref[0, j], dens_ref[many - 1, j], dn[:TILE]),
            (up_mix, diff_ref[0, j], diff_ref[many - 1, j], dn_mix),
            (
                pltpu.roll(up_mix, HALF, 0),
                drift_ref[0, j],
                drift_ref[many - 1, j],
                pltpu.roll(dn_mix, HALF, 0),
            ),
        )
        for k, column in enumerate(tiles):
            for e, tile in enumerate(column):
                slab[k, j, e * TILE : (e + 1) * TILE] = tile

    per_strip(strips, stage, 4)
    slabs = flat(slab)

    def load(j, t):
        return [
            slabs[pl.ds((k * strips + j) * SLAB + t, TILE, stride=HALF), :] for k in range(3)
        ]

    place = lax.broadcasted_iota(jnp.int32, (many, LANES), 0)
    coef = coef_ref[0].astype(jnp.float32)
    weights = [jnp.where(level_ref[0] >= depth - down, coef, 0.0) for down in range(3)] + [coef]

    def finish(out_ref, j, part, new):
        s = [state_ref[j, t] for t in range(TILE)]
        for t in range(HALF):
            s[t] = jnp.where(place == 0, new[t][2:3], s[t])
            s[HALF + t] = jnp.where(place == many - 1, new[t][5:6], s[HALF + t])
        before = new[HALF - 1][1:2]
        weighted = surpluses(s, jnp.where(place == 0, before, roll_rows(s[7], 1)), weights)
        for t in range(TILE):
            out_ref[part * TILE + t] = weighted[t]
        out_ref[per_chunk * TILE + part // many, pl.ds(lax.rem(part, many), 1), :] = (
            coef * before
        )

    def last(source):
        for out_ref, away in zip(out_refs, partners(dom_ref[0])):
            first = (me_ref[0] ^ away) * per_chunk
            emit = functools.partial(finish, out_ref)
            advance(first, per_chunk, HALF, source, coefs, emit)

    run_steps(strips, HALF, load, (state_a, state_b), coefs, last)


def sum_kernel(*refs):
    *parts, out_ref = refs
    total = parts[0][...]
    for part in parts[1:]:
        total = total + part[...]
    out_ref[...] = total


def nodal_kernel(per_chunk, depth, dom_ref, me_ref, level_ref, *refs):
    *totals, out_ref, values, sems = refs
    many = values.shape[1]
    level = level_ref[0]
    fine, mid, low = (jnp.where(level >= depth - down, 1.0, 0.0) for down in range(3))
    place = lax.broadcasted_iota(jnp.int32, (many, LANES), 0)
    copies = []
    for k, (ref, away) in enumerate(zip(totals, partners(dom_ref[0]))):
        first = (me_ref[0] ^ away) * per_chunk
        by_row = flat(values.at[k])

        def body(part, ref=ref, by_row=by_row):
            w = [ref[part * TILE + t] for t in range(TILE)]
            before = ref[per_chunk * TILE + part // many, pl.ds(lax.rem(part, many), 1), :]
            prev = jnp.where(place == 0, before, roll_rows(w[7], 1))
            v3 = 0.5 * (prev + w[7]) + low * w[3]
            v1 = 0.5 * (prev + v3) + mid * w[1]
            v5 = 0.5 * (v3 + w[7]) + mid * w[5]
            rows = (
                0.5 * (prev + v1) + fine * w[0],
                v1,
                0.5 * (v1 + v3) + fine * w[2],
                v3,
                0.5 * (v3 + v5) + fine * w[4],
                v5,
                0.5 * (v5 + w[7]) + fine * w[6],
                w[7],
            )
            for t in range(TILE):
                by_row[spaced(part * TILE + t, many, per_chunk * TILE), :] = rows[t]

        per_strip(per_chunk, body, min(per_chunk, 4))
        for m in range(many):
            copy = pltpu.make_async_copy(
                values.at[k, m], out_ref.at[m, pl.ds(first, per_chunk)], sems.at[k, m]
            )
            copy.start()
            copies.append(copy)
    for copy in copies:
        copy.wait()


def call(
    kernel, out_shapes, operands, in_smem=0, scratch=(), flops=0, out_space=pltpu.VMEM
):
    spaces = [pltpu.SMEM] * in_smem + [pltpu.VMEM] * (len(operands) - in_smem)
    specs = [pl.BlockSpec(memory_space=space) for space in spaces]
    moved = 4 * sum(x.size for x in operands)
    return pl.pallas_call(
        kernel,
        out_shape=[jax.ShapeDtypeStruct(shape, jnp.float32) for shape in out_shapes],
        in_specs=specs,
        out_specs=[pl.BlockSpec(memory_space=out_space) for _ in out_shapes],
        scratch_shapes=list(scratch),
        compiler_params=pltpu.CompilerParams(vmem_limit_bytes=VMEM_LIMIT),
        cost_estimate=pl.CostEstimate(flops=flops, bytes_accessed=moved, transcendentals=0),
    )(*operands)


def on_device(density, diffusion, drift_speed, levels, coefficient):
    rows, cols = density.shape[1:]
    doms, grids = lax.axis_size("dom"), lax.axis_size("grp")
    many, strips = rows // TILE, cols // LANES
    per_chunk = strips // SQUARE
    depth = (rows * doms).bit_length() - 1
    tiles = [tiles_of(x[0]) for x in (density, diffusion, drift_speed)]
    me = (lax.axis_index("grp") % SQUARE).astype(jnp.int32)[None]
    dom = lax.axis_index("dom").astype(jnp.int32)[None]

    def vmem(*shape):
        return pltpu.VMEM(shape, jnp.float32)

    near_pairs = [(d, d ^ 1) for d in range(doms)]
    far_pairs = [(d, min(max((d - 1 ^ 1) + 1, 0), doms - 1)) for d in range(doms)]
    (first,) = call(first_kernel, [(TILE, LANES)], (), flops=HALO_FLOPS * rows * cols)
    ready = lax.ppermute(first, "dom", near_pairs)
    far, near = call(
        pack_kernel,
        [(strips, 2 * TILE, LANES)] * 2,
        (dom, ready, *tiles),
        1,
    )
    far, near = (
        lax.ppermute(array, "dom", pairs) for array, pairs in ((far, far_pairs), (near, near_pairs))
    )
    place = (strips, TILE, many, LANES)
    (state,) = call(
        inner_kernel,
        [place],
        tiles,
        0,
        [vmem(strips + 2, *place[1:])] * 2 + [vmem(*place)] * 4,
        flops=40 * rows * cols,
    )
    chunk = (per_chunk * TILE + -(-per_chunk // many), many, LANES)
    own, *others = call(
        functools.partial(edge_kernel, per_chunk, depth, doms),
        [chunk] * SQUARE,
        (dom, me, levels, coefficient, *tiles, state, far, near),
        4,
        [vmem(3, strips, SLAB, LANES)]
        + [vmem(strips + 2, HALF, TILE, LANES)] * 2
        + [vmem(strips, HALF, TILE, LANES)] * 4,
        flops=40 * SLAB * cols,
    )

    def swap(array, meet):
        devices = [(g, d) for g in range(grids) for d in range(doms)]
        pairs = [(g * doms + d, (g ^ partners(d % 2)[meet]) * doms + d) for g, d in devices]
        return lax.ppermute(array, ("grp", "dom"), pairs)

    theirs = [swap(array, meet) for meet, array in enumerate(others, 1)]
    (total,) = call(sum_kernel, [chunk], (own, *theirs))
    apart = SQUARE
    while apart < grids:
        other = lax.ppermute(total, "grp", [(g, g ^ apart) for g in range(grids)])
        (total,) = call(sum_kernel, [chunk], (total, other))
        apart *= 2
    totals = [total] + [swap(total, meet) for meet in range(1, SQUARE)]
    (nodal,) = call(
        functools.partial(nodal_kernel, per_chunk, depth),
        [(many, strips, TILE, LANES)],
        (dom, me, levels, *totals),
        3,
        [vmem(SQUARE, many, per_chunk, TILE, LANES), pltpu.SemaphoreType.DMA((SQUARE, many))],
        out_space=pl.ANY,
    )
    return block_of(nodal)[None]


def solution(mesh):
    return jax.shard_map(
        on_device,
        mesh=mesh,
        in_specs=(
            P("grp", "dom", None),
            P("grp", "dom", None),
            P("grp", "dom", None),
            P("grp"),
            P("grp"),
        ),
        out_specs=P("grp", "dom", None),
        check_vma=False,
    )
```

```python
import functools

import jax
import jax.numpy as jnp
from jax import lax
from jax.experimental import pallas as pl
from jax.experimental.pallas import tpu as pltpu
from jax.sharding import PartitionSpec as P

STEPS = 4
LANES = 128
TILE = 8
HALF = TILE // 2
SLAB = 4 * TILE
SQUARE = 4
UNROLL = 16
STREAMS = 2
VMEM_LIMIT = 40 * 1024 * 1024
HALO_FLOPS = 4000


def tiles_of(block):
    rows, cols = block.shape
    return block.reshape(rows // TILE, TILE, cols // LANES, LANES).transpose(0, 2, 1, 3)


def block_of(tiles):
    many, strips = tiles.shape[:2]
    return tiles.transpose(0, 2, 1, 3).reshape(many * TILE, strips * LANES)


def flat(ref):
    return ref.reshape(ref.size // LANES, LANES)


def spaced(first, count, stride):
    return pl.ds(first, count, stride=stride) if count > 1 else pl.ds(first, 1)


def roll_rows(value, shift):
    count = value.shape[0]
    return pltpu.roll(value, shift % count, 0) if count > 1 else value


def per_strip(strips, body, unroll):
    def step(j, carry):
        body(j)
        return carry

    lax.fori_loop(0, strips, step, 0, unroll=unroll)


def advance(first, count, classes, source, coefs, emit):
    shape = source.shape[2:]
    lanes = lax.broadcasted_iota(jnp.int32, shape, 1)
    center, above_c, below_c, side = coefs

    def body(k, carry):
        j = first + k
        cur, right_prev, left_cur = carry
        nxt = [source[j + 2, t] for t in range(classes)]
        left_next = [pltpu.roll(x, LANES - 1, 1) for x in nxt]
        right_cur = [pltpu.roll(x, 1, 1) for x in cur]
        above = cur[1:] + [roll_rows(cur[0], -1)]
        below = [roll_rows(cur[-1], 1)] + cur[:-1]
        new = []
        for t in range(classes):
            left = jnp.where(lanes == 0, right_prev[t], right_cur[t])
            right = jnp.where(lanes == LANES - 1, left_next[t], left_cur[t])
            new.append(
                center[j, t] * cur[t]
                + above_c[j, t] * above[t]
                + below_c[j, t] * below[t]
                + side[j, t] * (left + right)
            )
        emit(j, k, new)
        return nxt, right_cur, left_next

    prev, cur = ([source[first + at, t] for t in range(classes)] for at in range(2))
    ends = [pltpu.roll(x, 1, 1) for x in prev], [pltpu.roll(x, LANES - 1, 1) for x in cur]
    lax.fori_loop(0, count, body, (cur, *ends), unroll=min(count, UNROLL))


def run_steps(strips, classes, load, buffers, coefs, last):
    center, above_c, below_c, side = coefs
    for buf in buffers:
        for edge in (0, strips + 1):
            buf[edge] = jnp.zeros(buf.shape[1:], jnp.float32)

    def begin(j):
        for t in range(classes):
            state, diffuse, drifts = load(j, t)
            half = 0.5 * drifts
            buffers[0][j + 1, t] = state
            center[j, t] = 1.0 - 4.0 * diffuse
            above_c[j, t] = diffuse - half
            below_c[j, t] = diffuse + half
            side[j, t] = diffuse

    per_strip(strips, begin, min(strips, UNROLL))
    for step in range(STEPS - 1):
        source, target = buffers[step % 2], buffers[1 - step % 2]

        def keep(j, _, new, target=target):
            for t in range(classes):
                target[j + 1, t] = new[t]

        advance(0, strips, classes, source, coefs, keep)
    last(buffers[(STEPS - 1) % 2])


def surpluses(s, prev, weights):
    fine, mid, low, coef = weights
    return (
        fine * (s[0] - 0.5 * (prev + s[1])),
        mid * (s[1] - 0.5 * (prev + s[3])),
        fine * (s[2] - 0.5 * (s[1] + s[3])),
        low * (s[3] - 0.5 * (prev + s[7])),
        fine * (s[4] - 0.5 * (s[3] + s[5])),
        mid * (s[5] - 0.5 * (s[3] + s[7])),
        fine * (s[6] - 0.5 * (s[5] + s[7])),
        coef * s[7],
    )


def pack_kernel(dom_ref, dens_ref, *refs):
    *ends, far_ref, near_ref = refs
    many, strips = dens_ref.shape[:2]
    odd = dom_ref[0] % 2 == 1
    upper = lax.broadcasted_iota(jnp.int32, (TILE, LANES), 0) < HALF

    def body(j):
        heads, tails = ([ref[j] for ref in ends[e::2]] for e in range(2))
        mix_next = jnp.where(upper, pltpu.roll(tails[1], HALF, 0), tails[0])
        mix_prev = jnp.where(upper, heads[0], pltpu.roll(heads[1], HALF, 0))
        to_next, to_prev = (dens_ref[many - 1, j], mix_next), (dens_ref[0, j], mix_prev)
        for k in range(2):
            at = pl.ds(k * TILE, TILE)
            far_ref[j, at] = jnp.where(odd, to_next[k], to_prev[k])
            near_ref[j, at] = jnp.where(odd, to_prev[k], to_next[k])

    per_strip(strips, body, 4)


def inner_kernel(dens_ref, diff_ref, drift_ref, out_ref, state_a, state_b, *coefs):
    many, strips = dens_ref.shape[:2]
    refs = [flat(ref) for ref in (dens_ref, diff_ref, drift_ref)]

    def load(j, t):
        at = spaced(j * TILE + t, many, strips * TILE)
        return [ref[at, :] for ref in refs]

    def emit(j, _, new):
        for t in range(TILE):
            out_ref[j, t] = new[t]

    def last(source):
        advance(0, strips, TILE, source, coefs, emit)

    run_steps(strips, TILE, load, (state_a, state_b), coefs, last)


def partners(dom):
    return 0, 1 + dom % 2, 2 - dom % 2, 3


def edge_kernel(
    per_chunk, depth, doms, dom_ref, me_ref, level_ref, coef_ref, dens_ref, *refs
):
    many, strips = dens_ref.shape[:2]
    dom = dom_ref[0]
    odd = dom % 2 == 1
    ends, (state_ref, far_ref, near_ref), refs = refs[:4], refs[4:7], refs[7:]
    out_refs, (slab, state_a, state_b, *coefs) = refs[:-7], refs[-7:]

    def stage(j):
        far, near = far_ref[j], near_ref[j]
        up = jnp.where(dom == 0, 0.0, jnp.where(odd, near, far))
        dn = jnp.where(dom == doms - 1, 0.0, jnp.where(odd, far, near))
        up_mix, dn_mix = up[TILE:], dn[TILE:]
        tiles = (
            (up[:TILE], dens_ref[0, j], dens_ref[many - 1, j], dn[:TILE]),
            (up_mix, ends[0][j], ends[1][j], dn_mix),
            (pltpu.roll(up_mix, HALF, 0), ends[2][j], ends[3][j], pltpu.roll(dn_mix, HALF, 0)),
        )
        for k, column in enumerate(tiles):
            for e, tile in enumerate(column):
                slab[k, j, e * TILE : (e + 1) * TILE] = tile

    per_strip(strips, stage, 4)
    slabs = flat(slab)

    def load(j, t):
        return [
            slabs[pl.ds((k * strips + j) * SLAB + t, TILE, stride=HALF), :] for k in range(3)
        ]

    place = lax.broadcasted_iota(jnp.int32, (many, LANES), 0)
    coef = coef_ref[0].astype(jnp.float32)
    weights = [jnp.where(level_ref[0] >= depth - down, coef, 0.0) for down in range(3)] + [coef]

    def finish(out_ref, j, part, new):
        s = [state_ref[j, t] for t in range(TILE)]
        for t in range(HALF):
            s[t] = jnp.where(place == 0, new[t][2:3], s[t])
            s[HALF + t] = jnp.where(place == many - 1, new[t][5:6], s[HALF + t])
        before = new[HALF - 1][1:2]
        weighted = surpluses(s, jnp.where(place == 0, before, roll_rows(s[7], 1)), weights)
        for t in range(TILE):
            out_ref[part * TILE + t] = weighted[t]
        out_ref[per_chunk * TILE + part // many, pl.ds(lax.rem(part, many), 1), :] = (
            coef * before
        )

    def last(source):
        for k, out_ref in enumerate(out_refs):
            stream, meet = divmod(k, SQUARE)
            chunk = stream * SQUARE + (me_ref[0] ^ partners(dom_ref[0])[meet])
            emit = functools.partial(finish, out_ref)
            advance(chunk * per_chunk, per_chunk, HALF, source, coefs, emit)

    run_steps(strips, HALF, load, (state_a, state_b), coefs, last)


def sum_kernel(*refs):
    *parts, out_ref = refs
    total = parts[0][...]
    for part in parts[1:]:
        total = total + part[...]
    out_ref[...] = total


def nodal_kernel(per_chunk, depth, stream, dom_ref, me_ref, level_ref, *refs):
    totals, (out_ref, values, sems) = refs[:SQUARE], refs[-3:]
    many = values.shape[1]
    level = level_ref[0]
    fine, mid, low = (jnp.where(level >= depth - down, 1.0, 0.0) for down in range(3))
    place = lax.broadcasted_iota(jnp.int32, (many, LANES), 0)
    copies = []
    for k, (ref, away) in enumerate(zip(totals, partners(dom_ref[0]))):
        first = (stream * SQUARE + (me_ref[0] ^ away)) * per_chunk
        by_row = flat(values.at[k])

        def body(part, ref=ref, by_row=by_row):
            w = [ref[part * TILE + t] for t in range(TILE)]
            before = ref[per_chunk * TILE + part // many, pl.ds(lax.rem(part, many), 1), :]
            prev = jnp.where(place == 0, before, roll_rows(w[7], 1))
            v3 = 0.5 * (prev + w[7]) + low * w[3]
            v1 = 0.5 * (prev + v3) + mid * w[1]
            v5 = 0.5 * (v3 + w[7]) + mid * w[5]
            rows = (
                0.5 * (prev + v1) + fine * w[0],
                v1,
                0.5 * (v1 + v3) + fine * w[2],
                v3,
                0.5 * (v3 + v5) + fine * w[4],
                v5,
                0.5 * (v5 + w[7]) + fine * w[6],
                w[7],
            )
            for t in range(TILE):
                by_row[spaced(part * TILE + t, many, per_chunk * TILE), :] = rows[t]

        per_strip(per_chunk, body, min(per_chunk, 4))
        for m in range(many):
            copy = pltpu.make_async_copy(
                values.at[k, m], out_ref.at[m, pl.ds(first, per_chunk)], sems.at[k, m]
            )
            copy.start()
            copies.append(copy)
    for copy in copies:
        copy.wait()


def call(
    kernel, out_shapes, operands, in_smem=0, scratch=(), flops=0, out_space=pltpu.VMEM, onto=None
):
    spaces = [pltpu.SMEM] * in_smem + [pltpu.VMEM] * (len(operands) - in_smem)
    alias = {}
    if onto is not None:
        alias = {len(operands): 0}
        spaces, operands = spaces + [out_space], (*operands, onto)
    specs = [pl.BlockSpec(memory_space=space) for space in spaces]
    moved = 4 * sum(x.size for x in operands)
    return pl.pallas_call(
        kernel,
        out_shape=[jax.ShapeDtypeStruct(shape, jnp.float32) for shape in out_shapes],
        in_specs=specs,
        out_specs=[pl.BlockSpec(memory_space=out_space) for _ in out_shapes],
        input_output_aliases=alias,
        scratch_shapes=list(scratch),
        compiler_params=pltpu.CompilerParams(vmem_limit_bytes=VMEM_LIMIT),
        cost_estimate=pl.CostEstimate(flops=flops, bytes_accessed=moved, transcendentals=0),
    )(*operands)


def on_device(density, diffusion, drift_speed, levels, coefficient):
    rows, cols = density.shape[1:]
    doms, grids = lax.axis_size("dom"), lax.axis_size("grp")
    many, strips = rows // TILE, cols // LANES
    per_chunk = strips // (SQUARE * STREAMS)
    depth = (rows * doms).bit_length() - 1
    tiles = [tiles_of(x[0]) for x in (density, diffusion, drift_speed)]
    me = (lax.axis_index("grp") % SQUARE).astype(jnp.int32)[None]
    dom = lax.axis_index("dom").astype(jnp.int32)[None]

    def vmem(*shape):
        return pltpu.VMEM(shape, jnp.float32)

    ends = [x[at] for x in tiles[1:] for at in (0, many - 1)]
    far, near = call(
        pack_kernel,
        [(strips, 2 * TILE, LANES)] * 2,
        (dom, tiles[0], *ends),
        1,
        flops=HALO_FLOPS * rows * cols,
    )
    near_pairs = [(d, d ^ 1) for d in range(doms)]
    far_pairs = [(d, min(max((d - 1 ^ 1) + 1, 0), doms - 1)) for d in range(doms)]
    far, near = (
        lax.ppermute(array, "dom", pairs) for array, pairs in ((far, far_pairs), (near, near_pairs))
    )
    place = (strips, TILE, many, LANES)
    (state,) = call(
        inner_kernel,
        [place],
        tiles,
        0,
        [vmem(strips + 2, *place[1:])] * 2 + [vmem(*place)] * 4,
        flops=40 * rows * cols,
    )
    chunk = (per_chunk * TILE + -(-per_chunk // many), many, LANES)
    weighted = call(
        functools.partial(edge_kernel, per_chunk, depth, doms),
        [chunk] * (SQUARE * STREAMS),
        (dom, me, levels, coefficient, tiles[0], *ends, state, far, near),
        4,
        [vmem(3, strips, SLAB, LANES)]
        + [vmem(strips + 2, HALF, TILE, LANES)] * 2
        + [vmem(strips, HALF, TILE, LANES)] * 4,
        flops=40 * SLAB * cols,
    )

    def swap(array, meet):
        devices = [(g, d) for g in range(grids) for d in range(doms)]
        pairs = [(g * doms + d, (g ^ partners(d % 2)[meet]) * doms + d) for g, d in devices]
        return lax.ppermute(array, ("grp", "dom"), pairs)

    def over_grids(own, *others):
        theirs = [swap(array, meet) for meet, array in enumerate(others, 1)]
        (total,) = call(sum_kernel, [chunk], (own, *theirs))
        apart = SQUARE
        while apart < grids:
            other = lax.ppermute(total, "grp", [(g, g ^ apart) for g in range(grids)])
            (total,) = call(sum_kernel, [chunk], (total, other))
            apart *= 2
        return [total] + [swap(total, meet) for meet in range(1, SQUARE)]

    nodal = None
    for stream in range(STREAMS):
        totals = over_grids(*weighted[stream * SQUARE : (stream + 1) * SQUARE])
        (nodal,) = call(
            functools.partial(nodal_kernel, per_chunk, depth, stream),
            [(many, strips, TILE, LANES)],
            (dom, me, levels, *totals),
            3,
            [vmem(SQUARE, many, per_chunk, TILE, LANES), pltpu.SemaphoreType.DMA((SQUARE, many))],
            out_space=pl.ANY,
            onto=nodal,
        )
    return block_of(nodal)[None]


def solution(mesh):
    return jax.shard_map(
        on_device,
        mesh=mesh,
        in_specs=(
            P("grp", "dom", None),
            P("grp", "dom", None),
            P("grp", "dom", None),
            P("grp"),
            P("grp"),
        ),
        out_specs=P("grp", "dom", None),
        check_vma=False,
    )
```

```python
import functools

import jax
import jax.numpy as jnp
from jax import lax
from jax.experimental import pallas as pl
from jax.experimental.pallas import tpu as pltpu
from jax.sharding import PartitionSpec as P

STEPS = 4
LANES = 128
TILE = 8
HALF = TILE // 2
SLAB = 4 * TILE
SQUARE = 4
UNROLL = 16
STREAMS = 2
VMEM_LIMIT = 40 * 1024 * 1024
HALO_FLOPS = 4000


def tiles_of(block):
    rows, cols = block.shape
    return block.reshape(rows // TILE, TILE, cols // LANES, LANES).transpose(0, 2, 1, 3)


def block_of(tiles):
    many, strips = tiles.shape[:2]
    return tiles.transpose(0, 2, 1, 3).reshape(many * TILE, strips * LANES)


def flat(ref):
    return ref.reshape(ref.size // LANES, LANES)


def spaced(first, count, stride):
    return pl.ds(first, count, stride=stride) if count > 1 else pl.ds(first, 1)


def roll_rows(value, shift):
    count = value.shape[0]
    return pltpu.roll(value, shift % count, 0) if count > 1 else value


def per_strip(strips, body, unroll):
    def step(j, carry):
        body(j)
        return carry

    lax.fori_loop(0, strips, step, 0, unroll=unroll)


def advance(first, count, classes, source, coefs, emit):
    shape = source.shape[2:]
    lanes = lax.broadcasted_iota(jnp.int32, shape, 1)
    center, above_c, below_c, side = coefs

    def body(k, carry):
        j = first + k
        cur, right_prev, left_cur = carry
        nxt = [source[j + 2, t] for t in range(classes)]
        left_next = [pltpu.roll(x, LANES - 1, 1) for x in nxt]
        right_cur = [pltpu.roll(x, 1, 1) for x in cur]
        above = cur[1:] + [roll_rows(cur[0], -1)]
        below = [roll_rows(cur[-1], 1)] + cur[:-1]
        new = []
        for t in range(classes):
            left = jnp.where(lanes == 0, right_prev[t], right_cur[t])
            right = jnp.where(lanes == LANES - 1, left_next[t], left_cur[t])
            new.append(
                center[j, t] * cur[t]
                + above_c[j, t] * above[t]
                + below_c[j, t] * below[t]
                + side[j, t] * (left + right)
            )
        emit(j, k, new)
        return nxt, right_cur, left_next

    prev, cur = ([source[first + at, t] for t in range(classes)] for at in range(2))
    ends = [pltpu.roll(x, 1, 1) for x in prev], [pltpu.roll(x, LANES - 1, 1) for x in cur]
    lax.fori_loop(0, count, body, (cur, *ends), unroll=min(count, UNROLL))


def run_steps(strips, classes, load, buffers, coefs, last):
    center, above_c, below_c, side = coefs
    for buf in buffers:
        for edge in (0, strips + 1):
            buf[edge] = jnp.zeros(buf.shape[1:], jnp.float32)

    def begin(j):
        for t in range(classes):
            state, diffuse, drifts = load(j, t)
            half = 0.5 * drifts
            buffers[0][j + 1, t] = state
            center[j, t] = 1.0 - 4.0 * diffuse
            above_c[j, t] = diffuse - half
            below_c[j, t] = diffuse + half
            side[j, t] = diffuse

    per_strip(strips, begin, min(strips, UNROLL))
    for step in range(STEPS - 1):
        source, target = buffers[step % 2], buffers[1 - step % 2]

        def keep(j, _, new, target=target):
            for t in range(classes):
                target[j + 1, t] = new[t]

        advance(0, strips, classes, source, coefs, keep)
    last(buffers[(STEPS - 1) % 2])


def surpluses(s, prev, weights):
    fine, mid, low, coef = weights
    return (
        fine * (s[0] - 0.5 * (prev + s[1])),
        mid * (s[1] - 0.5 * (prev + s[3])),
        fine * (s[2] - 0.5 * (s[1] + s[3])),
        low * (s[3] - 0.5 * (prev + s[7])),
        fine * (s[4] - 0.5 * (s[3] + s[5])),
        mid * (s[5] - 0.5 * (s[3] + s[7])),
        fine * (s[6] - 0.5 * (s[5] + s[7])),
        coef * s[7],
    )


def pack_kernel(dom_ref, dens_ref, *refs):
    *ends, far_ref, near_ref = refs
    many, strips = dens_ref.shape[:2]
    odd = dom_ref[0] % 2 == 1
    upper = lax.broadcasted_iota(jnp.int32, (TILE, LANES), 0) < HALF

    def body(j):
        heads, tails = ([ref[j] for ref in ends[e::2]] for e in range(2))
        mix_next = jnp.where(upper, pltpu.roll(tails[1], HALF, 0), tails[0])
        mix_prev = jnp.where(upper, heads[0], pltpu.roll(heads[1], HALF, 0))
        to_next, to_prev = (dens_ref[many - 1, j], mix_next), (dens_ref[0, j], mix_prev)
        for k in range(2):
            at = pl.ds(k * TILE, TILE)
            far_ref[j, at] = jnp.where(odd, to_next[k], to_prev[k])
            near_ref[j, at] = jnp.where(odd, to_prev[k], to_next[k])

    per_strip(strips, body, 4)


def inner_kernel(dens_ref, diff_ref, drift_ref, out_ref, state_a, state_b, *coefs):
    many, strips = dens_ref.shape[:2]
    refs = [flat(ref) for ref in (dens_ref, diff_ref, drift_ref)]

    def load(j, t):
        at = spaced(j * TILE + t, many, strips * TILE)
        return [ref[at, :] for ref in refs]

    def emit(j, _, new):
        for t in range(TILE):
            out_ref[j, t] = new[t]

    def last(source):
        advance(0, strips, TILE, source, coefs, emit)

    run_steps(strips, TILE, load, (state_a, state_b), coefs, last)


def partners(dom):
    return 0, 1 + dom % 2, 2 - dom % 2, 3


def edge_kernel(
    per_chunk, depth, doms, dom_ref, me_ref, level_ref, coef_ref, dens_ref, *refs
):
    many, strips = dens_ref.shape[:2]
    dom = dom_ref[0]
    odd = dom % 2 == 1
    ends, (state_ref, far_ref, near_ref), refs = refs[:4], refs[4:7], refs[7:]
    out_refs, (slab, state_a, state_b, *coefs) = refs[:-7], refs[-7:]
    chunk_refs = []
    for own_ref, second_ref, sent_ref in zip(*(out_refs[k::3] for k in range(3))):
        chunk_refs += [own_ref, sent_ref.at[0], second_ref, sent_ref.at[1]]

    def stage(j):
        far, near = far_ref[j], near_ref[j]
        up = jnp.where(dom == 0, 0.0, jnp.where(odd, near, far))
        dn = jnp.where(dom == doms - 1, 0.0, jnp.where(odd, far, near))
        up_mix, dn_mix = up[TILE:], dn[TILE:]
        tiles = (
            (up[:TILE], dens_ref[0, j], dens_ref[many - 1, j], dn[:TILE]),
            (up_mix, ends[0][j], ends[1][j], dn_mix),
            (pltpu.roll(up_mix, HALF, 0), ends[2][j], ends[3][j], pltpu.roll(dn_mix, HALF, 0)),
        )
        for k, column in enumerate(tiles):
            for e, tile in enumerate(column):
                slab[k, j, e * TILE : (e + 1) * TILE] = tile

    per_strip(strips, stage, 4)
    slabs = flat(slab)

    def load(j, t):
        return [
            slabs[pl.ds((k * strips + j) * SLAB + t, TILE, stride=HALF), :] for k in range(3)
        ]

    place = lax.broadcasted_iota(jnp.int32, (many, LANES), 0)
    coef = coef_ref[0].astype(jnp.float32)
    weights = [jnp.where(level_ref[0] >= depth - down, coef, 0.0) for down in range(3)] + [coef]

    def finish(out_ref, j, part, new):
        s = [state_ref[j, t] for t in range(TILE)]
        for t in range(HALF):
            s[t] = jnp.where(place == 0, new[t][2:3], s[t])
            s[HALF + t] = jnp.where(place == many - 1, new[t][5:6], s[HALF + t])
        before = new[HALF - 1][1:2]
        weighted = surpluses(s, jnp.where(place == 0, before, roll_rows(s[7], 1)), weights)
        for t in range(TILE):
            out_ref[part * TILE + t] = weighted[t]
        out_ref[per_chunk * TILE + part // many, pl.ds(lax.rem(part, many), 1), :] = (
            coef * before
        )

    def last(source):
        for k, out_ref in enumerate(chunk_refs):
            stream, meet = divmod(k, SQUARE)
            chunk = stream * SQUARE + (me_ref[0] ^ partners(dom_ref[0])[meet])
            emit = functools.partial(finish, out_ref)
            advance(chunk * per_chunk, per_chunk, HALF, source, coefs, emit)

    run_steps(strips, HALF, load, (state_a, state_b), coefs, last)


def first_kernel(own_ref, second_ref, theirs_ref, own_out, second_out):
    own_out[...] = own_ref[...] + theirs_ref[0]
    second_out[...] = second_ref[...] + theirs_ref[1]


def sum_kernel(mine_ref, theirs_ref, out_ref):
    out_ref[...] = mine_ref[...] + theirs_ref[...]


def pair_kernel(own_ref, second_ref, out_ref):
    out_ref[0] = own_ref[...]
    out_ref[1] = second_ref[...]


def nodal_kernel(per_chunk, depth, stream, dom_ref, me_ref, level_ref, *refs):
    (own_ref, second_ref, theirs_ref), (out_ref, values, sems) = refs[:3], refs[-3:]
    totals = own_ref, theirs_ref.at[0], second_ref, theirs_ref.at[1]
    many = values.shape[1]
    level = level_ref[0]
    fine, mid, low = (jnp.where(level >= depth - down, 1.0, 0.0) for down in range(3))
    place = lax.broadcasted_iota(jnp.int32, (many, LANES), 0)
    copies = []
    for k, (ref, away) in enumerate(zip(totals, partners(dom_ref[0]))):
        first = (stream * SQUARE + (me_ref[0] ^ away)) * per_chunk
        by_row = flat(values.at[k])

        def body(part, ref=ref, by_row=by_row):
            w = [ref[part * TILE + t] for t in range(TILE)]
            before = ref[per_chunk * TILE + part // many, pl.ds(lax.rem(part, many), 1), :]
            prev = jnp.where(place == 0, before, roll_rows(w[7], 1))
            v3 = 0.5 * (prev + w[7]) + low * w[3]
            v1 = 0.5 * (prev + v3) + mid * w[1]
            v5 = 0.5 * (v3 + w[7]) + mid * w[5]
            rows = (
                0.5 * (prev + v1) + fine * w[0],
                v1,
                0.5 * (v1 + v3) + fine * w[2],
                v3,
                0.5 * (v3 + v5) + fine * w[4],
                v5,
                0.5 * (v5 + w[7]) + fine * w[6],
                w[7],
            )
            for t in range(TILE):
                by_row[spaced(part * TILE + t, many, per_chunk * TILE), :] = rows[t]

        per_strip(per_chunk, body, min(per_chunk, 4))
        for m in range(many):
            copy = pltpu.make_async_copy(
                values.at[k, m], out_ref.at[m, pl.ds(first, per_chunk)], sems.at[k, m]
            )
            copy.start()
            copies.append(copy)
    for copy in copies:
        copy.wait()


def call(
    kernel, out_shapes, operands, in_smem=0, scratch=(), flops=0, out_space=pltpu.VMEM, onto=None
):
    spaces = [pltpu.SMEM] * in_smem + [pltpu.VMEM] * (len(operands) - in_smem)
    alias = {}
    if onto is not None:
        alias = {len(operands): 0}
        spaces, operands = spaces + [out_space], (*operands, onto)
    specs = [pl.BlockSpec(memory_space=space) for space in spaces]
    moved = 4 * sum(x.size for x in operands)
    return pl.pallas_call(
        kernel,
        out_shape=[jax.ShapeDtypeStruct(shape, jnp.float32) for shape in out_shapes],
        in_specs=specs,
        out_specs=[pl.BlockSpec(memory_space=out_space) for _ in out_shapes],
        input_output_aliases=alias,
        scratch_shapes=list(scratch),
        compiler_params=pltpu.CompilerParams(vmem_limit_bytes=VMEM_LIMIT),
        cost_estimate=pl.CostEstimate(flops=flops, bytes_accessed=moved, transcendentals=0),
    )(*operands)


def on_device(density, diffusion, drift_speed, levels, coefficient):
    rows, cols = density.shape[1:]
    doms, grids = lax.axis_size("dom"), lax.axis_size("grp")
    many, strips = rows // TILE, cols // LANES
    per_chunk = strips // (SQUARE * STREAMS)
    depth = (rows * doms).bit_length() - 1
    tiles = [tiles_of(x[0]) for x in (density, diffusion, drift_speed)]
    me = (lax.axis_index("grp") % SQUARE).astype(jnp.int32)[None]
    dom = lax.axis_index("dom").astype(jnp.int32)[None]

    def vmem(*shape):
        return pltpu.VMEM(shape, jnp.float32)

    ends = [x[at] for x in tiles[1:] for at in (0, many - 1)]
    far, near = call(
        pack_kernel,
        [(strips, 2 * TILE, LANES)] * 2,
        (dom, tiles[0], *ends),
        1,
        flops=HALO_FLOPS * rows * cols,
    )
    near_pairs = [(d, d ^ 1) for d in range(doms)]
    far_pairs = [(d, min(max((d - 1 ^ 1) + 1, 0), doms - 1)) for d in range(doms)]
    far, near = (
        lax.ppermute(array, "dom", pairs) for array, pairs in ((far, far_pairs), (near, near_pairs))
    )
    place = (strips, TILE, many, LANES)
    (state,) = call(
        inner_kernel,
        [place],
        tiles,
        0,
        [vmem(strips + 2, *place[1:])] * 2 + [vmem(*place)] * 4,
        flops=40 * rows * cols,
    )
    chunk = (per_chunk * TILE + -(-per_chunk // many), many, LANES)
    weighted = call(
        functools.partial(edge_kernel, per_chunk, depth, doms),
        [chunk, chunk, (2, *chunk)] * STREAMS,
        (dom, me, levels, coefficient, tiles[0], *ends, state, far, near),
        4,
        [vmem(3, strips, SLAB, LANES)]
        + [vmem(strips + 2, HALF, TILE, LANES)] * 2
        + [vmem(strips, HALF, TILE, LANES)] * 4,
        flops=40 * SLAB * cols,
    )

    def swap(array, meet):
        devices = [(g, d) for g in range(grids) for d in range(doms)]
        pairs = [(g * doms + d, (g ^ partners(d % 2)[meet]) * doms + d) for g, d in devices]
        return lax.ppermute(array, ("grp", "dom"), pairs)

    def over_grids(own, second, sent):
        own, second = call(first_kernel, [chunk] * 2, (own, second, swap(sent, 1)))
        (total,) = call(sum_kernel, [chunk], (own, swap(second, 2)))
        apart = SQUARE
        while apart < grids:
            other = lax.ppermute(total, "grp", [(g, g ^ apart) for g in range(grids)])
            (total,) = call(sum_kernel, [chunk], (total, other))
            apart *= 2
        second = swap(total, 2)
        (pair,) = call(pair_kernel, [(2, *chunk)], (total, second))
        return total, second, swap(pair, 1)

    nodal = None
    for stream in range(STREAMS):
        totals = over_grids(*weighted[stream * 3 : (stream + 1) * 3])
        (nodal,) = call(
            functools.partial(nodal_kernel, per_chunk, depth, stream),
            [(many, strips, TILE, LANES)],
            (dom, me, levels, *totals),
            3,
            [vmem(SQUARE, many, per_chunk, TILE, LANES), pltpu.SemaphoreType.DMA((SQUARE, many))],
            out_space=pl.ANY,
            onto=nodal,
        )
    return block_of(nodal)[None]


def solution(mesh):
    return jax.shard_map(
        on_device,
        mesh=mesh,
        in_specs=(
            P("grp", "dom", None),
            P("grp", "dom", None),
            P("grp", "dom", None),
            P("grp"),
            P("grp"),
        ),
        out_specs=P("grp", "dom", None),
        check_vma=False,
    )
```

```python
import functools

import jax
import jax.numpy as jnp
from jax import lax
from jax.experimental import pallas as pl
from jax.experimental.pallas import tpu as pltpu
from jax.sharding import PartitionSpec as P

STEPS = 4
LANES = 128
TILE = 8
HALF = TILE // 2
SLAB = 4 * TILE
SQUARE = 4
UNROLL = 16
VMEM_LIMIT = 40 * 1024 * 1024
LOAD_FLOPS = 4000


def tiles_of(block):
    rows, cols = block.shape
    return block.reshape(rows // TILE, TILE, cols // LANES, LANES).transpose(0, 2, 1, 3)


def block_of(tiles):
    many, strips = tiles.shape[:2]
    return tiles.transpose(0, 2, 1, 3).reshape(many * TILE, strips * LANES)


def flat(ref):
    return ref.reshape(ref.size // LANES, LANES)


def spaced(first, count, stride):
    return pl.ds(first, count, stride=stride) if count > 1 else pl.ds(first, 1)


def roll_rows(value, shift):
    count = value.shape[0]
    return pltpu.roll(value, shift % count, 0) if count > 1 else value


def per_strip(strips, body, unroll):
    def step(j, carry):
        body(j)
        return carry

    lax.fori_loop(0, strips, step, 0, unroll=unroll)


def advance(first, count, classes, source, coefs, emit):
    shape = source.shape[2:]
    lanes = lax.broadcasted_iota(jnp.int32, shape, 1)
    center, above_c, below_c, side = coefs

    def body(k, carry):
        j = first + k
        cur, right_prev, left_cur = carry
        nxt = [source[j + 2, t] for t in range(classes)]
        left_next = [pltpu.roll(x, LANES - 1, 1) for x in nxt]
        right_cur = [pltpu.roll(x, 1, 1) for x in cur]
        above = cur[1:] + [roll_rows(cur[0], -1)]
        below = [roll_rows(cur[-1], 1)] + cur[:-1]
        new = []
        for t in range(classes):
            left = jnp.where(lanes == 0, right_prev[t], right_cur[t])
            right = jnp.where(lanes == LANES - 1, left_next[t], left_cur[t])
            new.append(
                center[j, t] * cur[t]
                + above_c[j, t] * above[t]
                + below_c[j, t] * below[t]
                + side[j, t] * (left + right)
            )
        emit(j, k, new)
        return nxt, right_cur, left_next

    prev, cur = ([source[first + at, t] for t in range(classes)] for at in range(2))
    ends = [pltpu.roll(x, 1, 1) for x in prev], [pltpu.roll(x, LANES - 1, 1) for x in cur]
    lax.fori_loop(0, count, body, (cur, *ends), unroll=min(count, UNROLL))


def run_steps(strips, classes, load, buffers, coefs, last):
    center, above_c, below_c, side = coefs
    for buf in buffers:
        for edge in (0, strips + 1):
            buf[edge] = jnp.zeros(buf.shape[1:], jnp.float32)

    def begin(j):
        for t in range(classes):
            state, diffuse, drifts = load(j, t)
            half = 0.5 * drifts
            buffers[0][j + 1, t] = state
            center[j, t] = 1.0 - 4.0 * diffuse
            above_c[j, t] = diffuse - half
            below_c[j, t] = diffuse + half
            side[j, t] = diffuse

    per_strip(strips, begin, min(strips, UNROLL))
    for step in range(STEPS - 1):
        source, target = buffers[step % 2], buffers[1 - step % 2]

        def keep(j, _, new, target=target):
            for t in range(classes):
                target[j + 1, t] = new[t]

        advance(0, strips, classes, source, coefs, keep)
    last(buffers[(STEPS - 1) % 2])


def surpluses(s, prev, weights):
    fine, mid, low, coef = weights
    return (
        fine * (s[0] - 0.5 * (prev + s[1])),
        mid * (s[1] - 0.5 * (prev + s[3])),
        fine * (s[2] - 0.5 * (s[1] + s[3])),
        low * (s[3] - 0.5 * (prev + s[7])),
        fine * (s[4] - 0.5 * (s[3] + s[5])),
        mid * (s[5] - 0.5 * (s[3] + s[7])),
        fine * (s[6] - 0.5 * (s[5] + s[7])),
        coef * s[7],
    )


def ones_kernel(out_ref):
    out_ref[...] = jnp.ones(out_ref.shape, jnp.float32)


def weights_kernel(depth, level_ref, coef_ref, ones_ref, keep_ref, weight_ref):
    coef = coef_ref[0].astype(jnp.float32)
    for down in range(3):
        keep_ref[down] = jnp.where(level_ref[0] >= depth - down, ones_ref[...], 0.0)
        weight_ref[down] = coef * keep_ref[down]
    weight_ref[3] = coef * ones_ref[...]


def pack_kernel(dom_ref, weight_ref, dens_ref, diff_ref, drift_ref, near_ref, far_ref):
    del weight_ref
    many, strips = dens_ref.shape[:2]
    odd = dom_ref[0] % 2 == 1
    upper = lax.broadcasted_iota(jnp.int32, (TILE, LANES), 0) < HALF

    def body(j):
        drift_last = pltpu.roll(drift_ref[many - 1, j], HALF, 0)
        mix_next = jnp.where(upper, drift_last, diff_ref[many - 1, j])
        mix_prev = jnp.where(upper, diff_ref[0, j], pltpu.roll(drift_ref[0, j], HALF, 0))
        to_next, to_prev = (dens_ref[many - 1, j], mix_next), (dens_ref[0, j], mix_prev)
        for k in range(2):
            at = pl.ds(k * TILE, TILE)
            far_ref[j, at] = jnp.where(odd, to_next[k], to_prev[k])
            near_ref[j, at] = jnp.where(odd, to_prev[k], to_next[k])

    per_strip(strips, body, 4)


def inner_kernel(dens_ref, diff_ref, drift_ref, out_ref, state_a, state_b, *coefs):
    many, strips = dens_ref.shape[:2]
    refs = [flat(ref) for ref in (dens_ref, diff_ref, drift_ref)]

    def load(j, t):
        at = spaced(j * TILE + t, many, strips * TILE)
        return [ref[at, :] for ref in refs]

    def emit(j, _, new):
        for t in range(TILE):
            out_ref[j, t] = new[t]

    def last(source):
        advance(0, strips, TILE, source, coefs, emit)

    run_steps(strips, TILE, load, (state_a, state_b), coefs, last)


def partners(dom):
    return 0, 1 + dom % 2, 2 - dom % 2, 3


def edge_kernel(
    per_chunk, doms, dom_ref, me_ref, weight_ref, dens_ref, *refs
):
    many, strips = dens_ref.shape[:2]
    dom = dom_ref[0]
    odd = dom % 2 == 1
    diff_ref, drift_ref, state_ref, near_ref, far_ref, *rest = refs
    out_refs, (slab, state_a, state_b, *coefs) = rest[:SQUARE], rest[SQUARE:]

    def stage(j):
        far, near = far_ref[j], near_ref[j]
        up = jnp.where(dom == 0, 0.0, jnp.where(odd, near, far))
        dn = jnp.where(dom == doms - 1, 0.0, jnp.where(odd, far, near))
        up_mix, dn_mix = up[TILE:], dn[TILE:]
        tiles = (
            (up[:TILE], dens_ref[0, j], dens_ref[many - 1, j], dn[:TILE]),
            (up_mix, diff_ref[0, j], diff_ref[many - 1, j], dn_mix),
            (
                pltpu.roll(up_mix, HALF, 0),
                drift_ref[0, j],
                drift_ref[many - 1, j],
                pltpu.roll(dn_mix, HALF, 0),
            ),
        )
        for k, column in enumerate(tiles):
            for e, tile in enumerate(column):
                slab[k, j, e * TILE : (e + 1) * TILE] = tile

    per_strip(strips, stage, 4)
    slabs = flat(slab)

    def load(j, t):
        return [
            slabs[pl.ds((k * strips + j) * SLAB + t, TILE, stride=HALF), :] for k in range(3)
        ]

    place = lax.broadcasted_iota(jnp.int32, (many, LANES), 0)
    weights = [weight_ref[k] for k in range(4)]

    def finish(out_ref, j, part, new):
        s = [state_ref[j, t] for t in range(TILE)]
        for t in range(HALF):
            s[t] = jnp.where(place == 0, new[t][2:3], s[t])
            s[HALF + t] = jnp.where(place == many - 1, new[t][5:6], s[HALF + t])
        before = new[HALF - 1][1:2]
        weighted = surpluses(s, jnp.where(place == 0, before, roll_rows(s[7], 1)), weights)
        for t in range(TILE):
            out_ref[part * TILE + t] = weighted[t]
        out_ref[per_chunk * TILE + part // many, pl.ds(lax.rem(part, many), 1), :] = (
            weights[3][0:1] * before
        )

    def last(source):
        for out_ref, away in zip(out_refs, partners(dom_ref[0])):
            first = (me_ref[0] ^ away) * per_chunk
            emit = functools.partial(finish, out_ref)
            advance(first, per_chunk, HALF, source, coefs, emit)

    run_steps(strips, HALF, load, (state_a, state_b), coefs, last)


def sum_kernel(*refs):
    *parts, out_ref = refs
    total = parts[0][...]
    for part in parts[1:]:
        total = total + part[...]
    out_ref[...] = total


def nodal_kernel(per_chunk, dom_ref, me_ref, keep_ref, *refs):
    *totals, out_ref, values, sems = refs
    many = values.shape[1]
    fine, mid, low = (keep_ref[k] for k in range(3))
    place = lax.broadcasted_iota(jnp.int32, (many, LANES), 0)
    copies = []
    for k, (ref, away) in enumerate(zip(totals, partners(dom_ref[0]))):
        first = (me_ref[0] ^ away) * per_chunk
        by_row = flat(values.at[k])

        def body(part, ref=ref, by_row=by_row):
            w = [ref[part * TILE + t] for t in range(TILE)]
            before = ref[per_chunk * TILE + part // many, pl.ds(lax.rem(part, many), 1), :]
            prev = jnp.where(place == 0, before, roll_rows(w[7], 1))
            v3 = 0.5 * (prev + w[7]) + low * w[3]
            v1 = 0.5 * (prev + v3) + mid * w[1]
            v5 = 0.5 * (v3 + w[7]) + mid * w[5]
            rows = (
                0.5 * (prev + v1) + fine * w[0],
                v1,
                0.5 * (v1 + v3) + fine * w[2],
                v3,
                0.5 * (v3 + v5) + fine * w[4],
                v5,
                0.5 * (v5 + w[7]) + fine * w[6],
                w[7],
            )
            for t in range(TILE):
                by_row[spaced(part * TILE + t, many, per_chunk * TILE), :] = rows[t]

        per_strip(per_chunk, body, min(per_chunk, 4))
        for m in range(many):
            copy = pltpu.make_async_copy(
                values.at[k, m], out_ref.at[m, pl.ds(first, per_chunk)], sems.at[k, m]
            )
            copy.start()
            copies.append(copy)
    for copy in copies:
        copy.wait()


def call(
    kernel, out_shapes, operands, in_smem=0, scratch=(), flops=0, out_space=pltpu.VMEM
):
    spaces = [pltpu.SMEM] * in_smem + [pltpu.VMEM] * (len(operands) - in_smem)
    specs = [pl.BlockSpec(memory_space=space) for space in spaces]
    moved = 4 * sum(x.size for x in operands)
    return pl.pallas_call(
        kernel,
        out_shape=[jax.ShapeDtypeStruct(shape, jnp.float32) for shape in out_shapes],
        in_specs=specs,
        out_specs=[pl.BlockSpec(memory_space=out_space) for _ in out_shapes],
        scratch_shapes=list(scratch),
        compiler_params=pltpu.CompilerParams(vmem_limit_bytes=VMEM_LIMIT),
        cost_estimate=pl.CostEstimate(flops=flops, bytes_accessed=moved, transcendentals=0),
    )(*operands)


def on_device(density, diffusion, drift_speed, levels, coefficient):
    rows, cols = density.shape[1:]
    doms, grids = lax.axis_size("dom"), lax.axis_size("grp")
    many, strips = rows // TILE, cols // LANES
    per_chunk = strips // SQUARE
    depth = (rows * doms).bit_length() - 1
    tiles = [tiles_of(x[0]) for x in (density, diffusion, drift_speed)]
    me = (lax.axis_index("grp") % SQUARE).astype(jnp.int32)[None]
    dom = lax.axis_index("dom").astype(jnp.int32)[None]

    def vmem(*shape):
        return pltpu.VMEM(shape, jnp.float32)

    near_pairs = [(d, d ^ 1) for d in range(doms)]
    far_pairs = [(d, min(max((d - 1 ^ 1) + 1, 0), doms - 1)) for d in range(doms)]
    (ones,) = call(ones_kernel, [(many, LANES)], (), flops=LOAD_FLOPS * rows * cols)
    keep, weight = call(
        functools.partial(weights_kernel, depth),
        [(3, many, LANES), (4, many, LANES)],
        (levels, coefficient, ones),
        2,
    )
    near, far = call(
        pack_kernel,
        [(strips, 2 * TILE, LANES)] * 2,
        (dom, weight, *tiles),
        1,
    )
    near = lax.ppermute(near, "dom", near_pairs)
    far = lax.ppermute(far, "dom", far_pairs)
    place = (strips, TILE, many, LANES)
    (state,) = call(
        inner_kernel,
        [place],
        tiles,
        0,
        [vmem(strips + 2, *place[1:])] * 2 + [vmem(*place)] * 4,
        flops=40 * rows * cols,
    )
    chunk = (per_chunk * TILE + -(-per_chunk // many), many, LANES)
    own, *others = call(
        functools.partial(edge_kernel, per_chunk, doms),
        [chunk] * SQUARE,
        (dom, me, weight, *tiles, state, near, far),
        2,
        [vmem(3, strips, SLAB, LANES)]
        + [vmem(strips + 2, HALF, TILE, LANES)] * 2
        + [vmem(strips, HALF, TILE, LANES)] * 4,
        flops=40 * SLAB * cols,
    )

    def swap(array, meet):
        devices = [(g, d) for g in range(grids) for d in range(doms)]
        pairs = [(g * doms + d, (g ^ partners(d % 2)[meet]) * doms + d) for g, d in devices]
        return lax.ppermute(array, ("grp", "dom"), pairs)

    theirs = [swap(array, meet) for meet, array in enumerate(others, 1)]
    (total,) = call(sum_kernel, [chunk], (own, *theirs))
    apart = SQUARE
    while apart < grids:
        other = lax.ppermute(total, "grp", [(g, g ^ apart) for g in range(grids)])
        (total,) = call(sum_kernel, [chunk], (total, other))
        apart *= 2
    totals = [total] + [swap(total, meet) for meet in range(1, SQUARE)]
    (nodal,) = call(
        functools.partial(nodal_kernel, per_chunk),
        [(many, strips, TILE, LANES)],
        (dom, me, keep, *totals),
        2,
        [vmem(SQUARE, many, per_chunk, TILE, LANES), pltpu.SemaphoreType.DMA((SQUARE, many))],
        out_space=pl.ANY,
    )
    return block_of(nodal)[None]


def solution(mesh):
    return jax.shard_map(
        on_device,
        mesh=mesh,
        in_specs=(
            P("grp", "dom", None),
            P("grp", "dom", None),
            P("grp", "dom", None),
            P("grp"),
            P("grp"),
        ),
        out_specs=P("grp", "dom", None),
        check_vma=False,
    )
```

```python
import functools

import jax
import jax.numpy as jnp
from jax import lax
from jax.experimental import pallas as pl
from jax.experimental.pallas import tpu as pltpu
from jax.sharding import PartitionSpec as P

STEPS = 4
LANES = 128
TILE = 8
HALF = TILE // 2
SLAB = 4 * TILE
SQUARE = 4
UNROLL = 16
STREAMS = 2
VMEM_LIMIT = 40 * 1024 * 1024
LOAD_FLOPS = 4000


def tiles_of(block):
    rows, cols = block.shape
    return block.reshape(rows // TILE, TILE, cols // LANES, LANES).transpose(0, 2, 1, 3)


def block_of(tiles):
    many, strips = tiles.shape[:2]
    return tiles.transpose(0, 2, 1, 3).reshape(many * TILE, strips * LANES)


def flat(ref):
    return ref.reshape(ref.size // LANES, LANES)


def spaced(first, count, stride):
    return pl.ds(first, count, stride=stride) if count > 1 else pl.ds(first, 1)


def roll_rows(value, shift):
    count = value.shape[0]
    return pltpu.roll(value, shift % count, 0) if count > 1 else value


def per_strip(strips, body, unroll):
    def step(j, carry):
        body(j)
        return carry

    lax.fori_loop(0, strips, step, 0, unroll=unroll)


def advance(first, count, classes, source, coefs, emit):
    shape = source.shape[2:]
    lanes = lax.broadcasted_iota(jnp.int32, shape, 1)
    center, above_c, below_c, side = coefs

    def body(k, carry):
        j = first + k
        cur, right_prev, left_cur = carry
        nxt = [source[j + 2, t] for t in range(classes)]
        left_next = [pltpu.roll(x, LANES - 1, 1) for x in nxt]
        right_cur = [pltpu.roll(x, 1, 1) for x in cur]
        above = cur[1:] + [roll_rows(cur[0], -1)]
        below = [roll_rows(cur[-1], 1)] + cur[:-1]
        new = []
        for t in range(classes):
            left = jnp.where(lanes == 0, right_prev[t], right_cur[t])
            right = jnp.where(lanes == LANES - 1, left_next[t], left_cur[t])
            new.append(
                center[j, t] * cur[t]
                + above_c[j, t] * above[t]
                + below_c[j, t] * below[t]
                + side[j, t] * (left + right)
            )
        emit(j, k, new)
        return nxt, right_cur, left_next

    prev, cur = ([source[first + at, t] for t in range(classes)] for at in range(2))
    ends = [pltpu.roll(x, 1, 1) for x in prev], [pltpu.roll(x, LANES - 1, 1) for x in cur]
    lax.fori_loop(0, count, body, (cur, *ends), unroll=min(count, UNROLL))


def run_steps(strips, classes, load, buffers, coefs, last):
    center, above_c, below_c, side = coefs
    for buf in buffers:
        for edge in (0, strips + 1):
            buf[edge] = jnp.zeros(buf.shape[1:], jnp.float32)

    def begin(j):
        for t in range(classes):
            state, diffuse, drifts = load(j, t)
            half = 0.5 * drifts
            buffers[0][j + 1, t] = state
            center[j, t] = 1.0 - 4.0 * diffuse
            above_c[j, t] = diffuse - half
            below_c[j, t] = diffuse + half
            side[j, t] = diffuse

    per_strip(strips, begin, min(strips, UNROLL))
    for step in range(STEPS - 1):
        source, target = buffers[step % 2], buffers[1 - step % 2]

        def keep(j, _, new, target=target):
            for t in range(classes):
                target[j + 1, t] = new[t]

        advance(0, strips, classes, source, coefs, keep)
    last(buffers[(STEPS - 1) % 2])


def surpluses(s, prev, weights):
    fine, mid, low, coef = weights
    return (
        fine * (s[0] - 0.5 * (prev + s[1])),
        mid * (s[1] - 0.5 * (prev + s[3])),
        fine * (s[2] - 0.5 * (s[1] + s[3])),
        low * (s[3] - 0.5 * (prev + s[7])),
        fine * (s[4] - 0.5 * (s[3] + s[5])),
        mid * (s[5] - 0.5 * (s[3] + s[7])),
        fine * (s[6] - 0.5 * (s[5] + s[7])),
        coef * s[7],
    )


def ones_kernel(out_ref):
    out_ref[...] = jnp.ones(out_ref.shape, jnp.float32)


def weights_kernel(depth, level_ref, coef_ref, ones_ref, keep_ref, weight_ref):
    coef = coef_ref[0].astype(jnp.float32)
    for down in range(3):
        keep_ref[down] = jnp.where(level_ref[0] >= depth - down, ones_ref[...], 0.0)
        weight_ref[down] = coef * keep_ref[down]
    weight_ref[3] = coef * ones_ref[...]


def pack_kernel(dom_ref, weight_ref, dens_ref, diff_ref, drift_ref, near_ref, far_ref):
    del weight_ref
    many, strips = dens_ref.shape[:2]
    odd = dom_ref[0] % 2 == 1
    upper = lax.broadcasted_iota(jnp.int32, (TILE, LANES), 0) < HALF

    def body(j):
        drift_last = pltpu.roll(drift_ref[many - 1, j], HALF, 0)
        mix_next = jnp.where(upper, drift_last, diff_ref[many - 1, j])
        mix_prev = jnp.where(upper, diff_ref[0, j], pltpu.roll(drift_ref[0, j], HALF, 0))
        to_next, to_prev = (dens_ref[many - 1, j], mix_next), (dens_ref[0, j], mix_prev)
        for k in range(2):
            at = pl.ds(k * TILE, TILE)
            far_ref[j, at] = jnp.where(odd, to_next[k], to_prev[k])
            near_ref[j, at] = jnp.where(odd, to_prev[k], to_next[k])

    per_strip(strips, body, 4)


def inner_kernel(dens_ref, diff_ref, drift_ref, out_ref, state_a, state_b, *coefs):
    many, strips = dens_ref.shape[:2]
    refs = [flat(ref) for ref in (dens_ref, diff_ref, drift_ref)]

    def load(j, t):
        at = spaced(j * TILE + t, many, strips * TILE)
        return [ref[at, :] for ref in refs]

    def emit(j, _, new):
        for t in range(TILE):
            out_ref[j, t] = new[t]

    def last(source):
        advance(0, strips, TILE, source, coefs, emit)

    run_steps(strips, TILE, load, (state_a, state_b), coefs, last)


def partners(dom):
    return 0, 1 + dom % 2, 2 - dom % 2, 3


def edge_kernel(
    per_chunk, doms, dom_ref, me_ref, weight_ref, dens_ref, *refs
):
    many, strips = dens_ref.shape[:2]
    dom = dom_ref[0]
    odd = dom % 2 == 1
    diff_ref, drift_ref, state_ref, near_ref, far_ref, *rest = refs
    out_refs, (slab, state_a, state_b, *coefs) = rest[:-7], rest[-7:]

    def stage(j):
        far, near = far_ref[j], near_ref[j]
        up = jnp.where(dom == 0, 0.0, jnp.where(odd, near, far))
        dn = jnp.where(dom == doms - 1, 0.0, jnp.where(odd, far, near))
        up_mix, dn_mix = up[TILE:], dn[TILE:]
        tiles = (
            (up[:TILE], dens_ref[0, j], dens_ref[many - 1, j], dn[:TILE]),
            (up_mix, diff_ref[0, j], diff_ref[many - 1, j], dn_mix),
            (
                pltpu.roll(up_mix, HALF, 0),
                drift_ref[0, j],
                drift_ref[many - 1, j],
                pltpu.roll(dn_mix, HALF, 0),
            ),
        )
        for k, column in enumerate(tiles):
            for e, tile in enumerate(column):
                slab[k, j, e * TILE : (e + 1) * TILE] = tile

    per_strip(strips, stage, 4)
    slabs = flat(slab)

    def load(j, t):
        return [
            slabs[pl.ds((k * strips + j) * SLAB + t, TILE, stride=HALF), :] for k in range(3)
        ]

    place = lax.broadcasted_iota(jnp.int32, (many, LANES), 0)
    weights = [weight_ref[k] for k in range(4)]

    def finish(out_ref, j, part, new):
        s = [state_ref[j, t] for t in range(TILE)]
        for t in range(HALF):
            s[t] = jnp.where(place == 0, new[t][2:3], s[t])
            s[HALF + t] = jnp.where(place == many - 1, new[t][5:6], s[HALF + t])
        before = new[HALF - 1][1:2]
        weighted = surpluses(s, jnp.where(place == 0, before, roll_rows(s[7], 1)), weights)
        for t in range(TILE):
            out_ref[part * TILE + t] = weighted[t]
        out_ref[per_chunk * TILE + part // many, pl.ds(lax.rem(part, many), 1), :] = (
            weights[3][0:1] * before
        )

    def last(source):
        for k, out_ref in enumerate(out_refs):
            stream, meet = divmod(k, SQUARE)
            chunk = stream * SQUARE + (me_ref[0] ^ partners(dom_ref[0])[meet])
            emit = functools.partial(finish, out_ref)
            advance(chunk * per_chunk, per_chunk, HALF, source, coefs, emit)

    run_steps(strips, HALF, load, (state_a, state_b), coefs, last)


def sum_kernel(*refs):
    *parts, out_ref = refs
    total = parts[0][...]
    for part in parts[1:]:
        total = total + part[...]
    out_ref[...] = total


def nodal_kernel(per_chunk, stream, dom_ref, me_ref, keep_ref, *refs):
    totals, (out_ref, values, sems) = refs[:SQUARE], refs[-3:]
    many = values.shape[1]
    fine, mid, low = (keep_ref[k] for k in range(3))
    place = lax.broadcasted_iota(jnp.int32, (many, LANES), 0)
    copies = []
    for k, (ref, away) in enumerate(zip(totals, partners(dom_ref[0]))):
        first = (stream * SQUARE + (me_ref[0] ^ away)) * per_chunk
        by_row = flat(values.at[k])

        def body(part, ref=ref, by_row=by_row):
            w = [ref[part * TILE + t] for t in range(TILE)]
            before = ref[per_chunk * TILE + part // many, pl.ds(lax.rem(part, many), 1), :]
            prev = jnp.where(place == 0, before, roll_rows(w[7], 1))
            v3 = 0.5 * (prev + w[7]) + low * w[3]
            v1 = 0.5 * (prev + v3) + mid * w[1]
            v5 = 0.5 * (v3 + w[7]) + mid * w[5]
            rows = (
                0.5 * (prev + v1) + fine * w[0],
                v1,
                0.5 * (v1 + v3) + fine * w[2],
                v3,
                0.5 * (v3 + v5) + fine * w[4],
                v5,
                0.5 * (v5 + w[7]) + fine * w[6],
                w[7],
            )
            for t in range(TILE):
                by_row[spaced(part * TILE + t, many, per_chunk * TILE), :] = rows[t]

        per_strip(per_chunk, body, min(per_chunk, 4))
        for m in range(many):
            copy = pltpu.make_async_copy(
                values.at[k, m], out_ref.at[m, pl.ds(first, per_chunk)], sems.at[k, m]
            )
            copy.start()
            copies.append(copy)
    for copy in copies:
        copy.wait()


def call(
    kernel, out_shapes, operands, in_smem=0, scratch=(), flops=0, out_space=pltpu.VMEM, onto=None
):
    spaces = [pltpu.SMEM] * in_smem + [pltpu.VMEM] * (len(operands) - in_smem)
    alias = {}
    if onto is not None:
        alias = {len(operands): 0}
        spaces, operands = spaces + [out_space], (*operands, onto)
    specs = [pl.BlockSpec(memory_space=space) for space in spaces]
    moved = 4 * sum(x.size for x in operands)
    return pl.pallas_call(
        kernel,
        out_shape=[jax.ShapeDtypeStruct(shape, jnp.float32) for shape in out_shapes],
        in_specs=specs,
        out_specs=[pl.BlockSpec(memory_space=out_space) for _ in out_shapes],
        input_output_aliases=alias,
        scratch_shapes=list(scratch),
        compiler_params=pltpu.CompilerParams(vmem_limit_bytes=VMEM_LIMIT),
        cost_estimate=pl.CostEstimate(flops=flops, bytes_accessed=moved, transcendentals=0),
    )(*operands)


def on_device(density, diffusion, drift_speed, levels, coefficient):
    rows, cols = density.shape[1:]
    doms, grids = lax.axis_size("dom"), lax.axis_size("grp")
    many, strips = rows // TILE, cols // LANES
    per_chunk = strips // (SQUARE * STREAMS)
    depth = (rows * doms).bit_length() - 1
    tiles = [tiles_of(x[0]) for x in (density, diffusion, drift_speed)]
    me = (lax.axis_index("grp") % SQUARE).astype(jnp.int32)[None]
    dom = lax.axis_index("dom").astype(jnp.int32)[None]

    def vmem(*shape):
        return pltpu.VMEM(shape, jnp.float32)

    near_pairs = [(d, d ^ 1) for d in range(doms)]
    far_pairs = [(d, min(max((d - 1 ^ 1) + 1, 0), doms - 1)) for d in range(doms)]
    (ones,) = call(ones_kernel, [(many, LANES)], (), flops=LOAD_FLOPS * rows * cols)
    keep, weight = call(
        functools.partial(weights_kernel, depth),
        [(3, many, LANES), (4, many, LANES)],
        (levels, coefficient, ones),
        2,
    )
    near, far = call(
        pack_kernel,
        [(strips, 2 * TILE, LANES)] * 2,
        (dom, weight, *tiles),
        1,
    )
    near = lax.ppermute(near, "dom", near_pairs)
    far = lax.ppermute(far, "dom", far_pairs)
    place = (strips, TILE, many, LANES)
    (state,) = call(
        inner_kernel,
        [place],
        tiles,
        0,
        [vmem(strips + 2, *place[1:])] * 2 + [vmem(*place)] * 4,
        flops=40 * rows * cols,
    )
    chunk = (per_chunk * TILE + -(-per_chunk // many), many, LANES)
    weighted = call(
        functools.partial(edge_kernel, per_chunk, doms),
        [chunk] * (SQUARE * STREAMS),
        (dom, me, weight, *tiles, state, near, far),
        2,
        [vmem(3, strips, SLAB, LANES)]
        + [vmem(strips + 2, HALF, TILE, LANES)] * 2
        + [vmem(strips, HALF, TILE, LANES)] * 4,
        flops=40 * SLAB * cols,
    )

    def swap(array, meet):
        devices = [(g, d) for g in range(grids) for d in range(doms)]
        pairs = [(g * doms + d, (g ^ partners(d % 2)[meet]) * doms + d) for g, d in devices]
        return lax.ppermute(array, ("grp", "dom"), pairs)

    def over_grids(own, *others):
        theirs = [swap(array, meet) for meet, array in enumerate(others, 1)]
        (total,) = call(sum_kernel, [chunk], (own, *theirs))
        apart = SQUARE
        while apart < grids:
            other = lax.ppermute(total, "grp", [(g, g ^ apart) for g in range(grids)])
            (total,) = call(sum_kernel, [chunk], (total, other))
            apart *= 2
        return [total] + [swap(total, meet) for meet in range(1, SQUARE)]

    nodal = None
    for stream in range(STREAMS):
        totals = over_grids(*weighted[stream * SQUARE : (stream + 1) * SQUARE])
        (nodal,) = call(
            functools.partial(nodal_kernel, per_chunk, stream),
            [(many, strips, TILE, LANES)],
            (dom, me, keep, *totals),
            2,
            [vmem(SQUARE, many, per_chunk, TILE, LANES), pltpu.SemaphoreType.DMA((SQUARE, many))],
            out_space=pl.ANY,
            onto=nodal,
        )
    return block_of(nodal)[None]


def solution(mesh):
    return jax.shard_map(
        on_device,
        mesh=mesh,
        in_specs=(
            P("grp", "dom", None),
            P("grp", "dom", None),
            P("grp", "dom", None),
            P("grp"),
            P("grp"),
        ),
        out_specs=P("grp", "dom", None),
        check_vma=False,
    )
```

```python
import functools

import jax
import jax.numpy as jnp
from jax import lax
from jax.experimental import pallas as pl
from jax.experimental.pallas import tpu as pltpu
from jax.sharding import PartitionSpec as P

STEPS = 4
LANES = 128
TILE = 8
HALF = TILE // 2
SLAB = 4 * TILE
SQUARE = 4
UNROLL = 16
STREAMS = 2
VMEM_LIMIT = 40 * 1024 * 1024
LOAD_FLOPS = 4000


def tiles_of(block):
    rows, cols = block.shape
    return block.reshape(rows // TILE, TILE, cols // LANES, LANES).transpose(0, 2, 1, 3)


def block_of(tiles):
    many, strips = tiles.shape[:2]
    return tiles.transpose(0, 2, 1, 3).reshape(many * TILE, strips * LANES)


def flat(ref):
    return ref.reshape(ref.size // LANES, LANES)


def spaced(first, count, stride):
    return pl.ds(first, count, stride=stride) if count > 1 else pl.ds(first, 1)


def roll_rows(value, shift):
    count = value.shape[0]
    return pltpu.roll(value, shift % count, 0) if count > 1 else value


def per_strip(strips, body, unroll):
    def step(j, carry):
        body(j)
        return carry

    lax.fori_loop(0, strips, step, 0, unroll=unroll)


def advance(first, count, classes, source, coefs, emit):
    shape = source.shape[2:]
    lanes = lax.broadcasted_iota(jnp.int32, shape, 1)
    center, above_c, below_c, side = coefs

    def body(k, carry):
        j = first + k
        cur, right_prev, left_cur = carry
        nxt = [source[j + 2, t] for t in range(classes)]
        left_next = [pltpu.roll(x, LANES - 1, 1) for x in nxt]
        right_cur = [pltpu.roll(x, 1, 1) for x in cur]
        above = cur[1:] + [roll_rows(cur[0], -1)]
        below = [roll_rows(cur[-1], 1)] + cur[:-1]
        new = []
        for t in range(classes):
            left = jnp.where(lanes == 0, right_prev[t], right_cur[t])
            right = jnp.where(lanes == LANES - 1, left_next[t], left_cur[t])
            new.append(
                center[j, t] * cur[t]
                + above_c[j, t] * above[t]
                + below_c[j, t] * below[t]
                + side[j, t] * (left + right)
            )
        emit(j, k, new)
        return nxt, right_cur, left_next

    prev, cur = ([source[first + at, t] for t in range(classes)] for at in range(2))
    ends = [pltpu.roll(x, 1, 1) for x in prev], [pltpu.roll(x, LANES - 1, 1) for x in cur]
    lax.fori_loop(0, count, body, (cur, *ends), unroll=min(count, UNROLL))


def run_steps(strips, classes, load, buffers, coefs, last):
    center, above_c, below_c, side = coefs
    for buf in buffers:
        for edge in (0, strips + 1):
            buf[edge] = jnp.zeros(buf.shape[1:], jnp.float32)

    def begin(j):
        for t in range(classes):
            state, diffuse, drifts = load(j, t)
            half = 0.5 * drifts
            buffers[0][j + 1, t] = state
            center[j, t] = 1.0 - 4.0 * diffuse
            above_c[j, t] = diffuse - half
            below_c[j, t] = diffuse + half
            side[j, t] = diffuse

    per_strip(strips, begin, min(strips, UNROLL))
    for step in range(STEPS - 1):
        source, target = buffers[step % 2], buffers[1 - step % 2]

        def keep(j, _, new, target=target):
            for t in range(classes):
                target[j + 1, t] = new[t]

        advance(0, strips, classes, source, coefs, keep)
    last(buffers[(STEPS - 1) % 2])


def surpluses(s, prev, weights):
    fine, mid, low, coef = weights
    return (
        fine * (s[0] - 0.5 * (prev + s[1])),
        mid * (s[1] - 0.5 * (prev + s[3])),
        fine * (s[2] - 0.5 * (s[1] + s[3])),
        low * (s[3] - 0.5 * (prev + s[7])),
        fine * (s[4] - 0.5 * (s[3] + s[5])),
        mid * (s[5] - 0.5 * (s[3] + s[7])),
        fine * (s[6] - 0.5 * (s[5] + s[7])),
        coef * s[7],
    )


def ones_kernel(out_ref):
    out_ref[...] = jnp.ones(out_ref.shape, jnp.float32)


def weights_kernel(depth, level_ref, coef_ref, ones_ref, keep_ref, weight_ref):
    coef = coef_ref[0].astype(jnp.float32)
    for down in range(3):
        keep_ref[down] = jnp.where(level_ref[0] >= depth - down, ones_ref[...], 0.0)
        weight_ref[down] = coef * keep_ref[down]
    weight_ref[3] = coef * ones_ref[...]


def pack_kernel(dom_ref, weight_ref, dens_ref, diff_ref, drift_ref, near_ref, far_ref):
    del weight_ref
    many, strips = dens_ref.shape[:2]
    odd = dom_ref[0] % 2 == 1
    upper = lax.broadcasted_iota(jnp.int32, (TILE, LANES), 0) < HALF

    def body(j):
        drift_last = pltpu.roll(drift_ref[many - 1, j], HALF, 0)
        mix_next = jnp.where(upper, drift_last, diff_ref[many - 1, j])
        mix_prev = jnp.where(upper, diff_ref[0, j], pltpu.roll(drift_ref[0, j], HALF, 0))
        to_next, to_prev = (dens_ref[many - 1, j], mix_next), (dens_ref[0, j], mix_prev)
        for k in range(2):
            at = pl.ds(k * TILE, TILE)
            far_ref[j, at] = jnp.where(odd, to_next[k], to_prev[k])
            near_ref[j, at] = jnp.where(odd, to_prev[k], to_next[k])

    per_strip(strips, body, 4)


def inner_kernel(dens_ref, diff_ref, drift_ref, out_ref, state_a, state_b, *coefs):
    many, strips = dens_ref.shape[:2]
    refs = [flat(ref) for ref in (dens_ref, diff_ref, drift_ref)]

    def load(j, t):
        at = spaced(j * TILE + t, many, strips * TILE)
        return [ref[at, :] for ref in refs]

    def emit(j, _, new):
        for t in range(TILE):
            out_ref[j, t] = new[t]

    def last(source):
        advance(0, strips, TILE, source, coefs, emit)

    run_steps(strips, TILE, load, (state_a, state_b), coefs, last)


def partners(dom):
    return 0, 1 + dom % 2, 2 - dom % 2, 3


def edge_kernel(
    per_chunk, doms, dom_ref, me_ref, weight_ref, dens_ref, *refs
):
    many, strips = dens_ref.shape[:2]
    dom = dom_ref[0]
    odd = dom % 2 == 1
    diff_ref, drift_ref, state_ref, near_ref, far_ref, *rest = refs
    out_refs, (slab, state_a, state_b, *coefs) = rest[:-7], rest[-7:]

    def stage(j):
        far, near = far_ref[j], near_ref[j]
        up = jnp.where(dom == 0, 0.0, jnp.where(odd, near, far))
        dn = jnp.where(dom == doms - 1, 0.0, jnp.where(odd, far, near))
        up_mix, dn_mix = up[TILE:], dn[TILE:]
        tiles = (
            (up[:TILE], dens_ref[0, j], dens_ref[many - 1, j], dn[:TILE]),
            (up_mix, diff_ref[0, j], diff_ref[many - 1, j], dn_mix),
            (
                pltpu.roll(up_mix, HALF, 0),
                drift_ref[0, j],
                drift_ref[many - 1, j],
                pltpu.roll(dn_mix, HALF, 0),
            ),
        )
        for k, column in enumerate(tiles):
            for e, tile in enumerate(column):
                slab[k, j, e * TILE : (e + 1) * TILE] = tile

    per_strip(strips, stage, 4)
    slabs = flat(slab)

    def load(j, t):
        return [
            slabs[pl.ds((k * strips + j) * SLAB + t, TILE, stride=HALF), :] for k in range(3)
        ]

    place = lax.broadcasted_iota(jnp.int32, (many, LANES), 0)
    weights = [weight_ref[k] for k in range(4)]

    def finish(out_ref, j, part, new):
        s = [state_ref[j, t] for t in range(TILE)]
        for t in range(HALF):
            s[t] = jnp.where(place == 0, new[t][2:3], s[t])
            s[HALF + t] = jnp.where(place == many - 1, new[t][5:6], s[HALF + t])
        before = new[HALF - 1][1:2]
        weighted = surpluses(s, jnp.where(place == 0, before, roll_rows(s[7], 1)), weights)
        for t in range(TILE):
            out_ref[part * TILE + t] = weighted[t]
        out_ref[per_chunk * TILE + part // many, pl.ds(lax.rem(part, many), 1), :] = (
            weights[3][0:1] * before
        )

    def last(source):
        for out_ref, away in zip(out_refs, partners(dom_ref[0])):
            first = (me_ref[0] ^ away) * per_chunk
            emit = functools.partial(finish, out_ref)
            advance(first, per_chunk, HALF, source, coefs, emit)

    run_steps(strips, HALF, load, (state_a, state_b), coefs, last)


def split_kernel(per_chunk, *refs):
    parts, out_refs = refs[:SQUARE], refs[SQUARE:]
    size = per_chunk * TILE // STREAMS
    for stream, out_ref in enumerate(out_refs):
        for at, to in (
            (pl.ds(stream * size, size), pl.ds(0, size)),
            (pl.ds(per_chunk * TILE, out_ref.shape[0] - size), pl.ds(size, out_ref.shape[0] - size)),
        ):
            total = parts[0][at]
            for part in parts[1:]:
                total = total + part[at]
            out_ref[to] = total


def sum_kernel(*refs):
    *parts, out_ref = refs
    total = parts[0][...]
    for part in parts[1:]:
        total = total + part[...]
    out_ref[...] = total


def nodal_kernel(per_chunk, stream, dom_ref, me_ref, keep_ref, *refs):
    totals, (out_ref, values, sems) = refs[:SQUARE], refs[-3:]
    many, half = values.shape[1:3]
    fine, mid, low = (keep_ref[k] for k in range(3))
    place = lax.broadcasted_iota(jnp.int32, (many, LANES), 0)
    copies = []
    for k, (ref, away) in enumerate(zip(totals, partners(dom_ref[0]))):
        first = (me_ref[0] ^ away) * per_chunk + stream * half
        by_row = flat(values.at[k])

        def body(part, ref=ref, by_row=by_row):
            w = [ref[part * TILE + t] for t in range(TILE)]
            spot = stream * half + part
            before = ref[half * TILE + spot // many, pl.ds(lax.rem(spot, many), 1), :]
            prev = jnp.where(place == 0, before, roll_rows(w[7], 1))
            v3 = 0.5 * (prev + w[7]) + low * w[3]
            v1 = 0.5 * (prev + v3) + mid * w[1]
            v5 = 0.5 * (v3 + w[7]) + mid * w[5]
            rows = (
                0.5 * (prev + v1) + fine * w[0],
                v1,
                0.5 * (v1 + v3) + fine * w[2],
                v3,
                0.5 * (v3 + v5) + fine * w[4],
                v5,
                0.5 * (v5 + w[7]) + fine * w[6],
                w[7],
            )
            for t in range(TILE):
                by_row[spaced(part * TILE + t, many, half * TILE), :] = rows[t]

        per_strip(half, body, min(half, 4))
        for m in range(many):
            copy = pltpu.make_async_copy(
                values.at[k, m], out_ref.at[m, pl.ds(first, half)], sems.at[k, m]
            )
            copy.start()
            copies.append(copy)
    for copy in copies:
        copy.wait()


def call(
    kernel, out_shapes, operands, in_smem=0, scratch=(), flops=0, out_space=pltpu.VMEM, onto=None
):
    spaces = [pltpu.SMEM] * in_smem + [pltpu.VMEM] * (len(operands) - in_smem)
    alias = {}
    if onto is not None:
        alias = {len(operands): 0}
        spaces, operands = spaces + [out_space], (*operands, onto)
    specs = [pl.BlockSpec(memory_space=space) for space in spaces]
    moved = 4 * sum(x.size for x in operands)
    return pl.pallas_call(
        kernel,
        out_shape=[jax.ShapeDtypeStruct(shape, jnp.float32) for shape in out_shapes],
        in_specs=specs,
        out_specs=[pl.BlockSpec(memory_space=out_space) for _ in out_shapes],
        input_output_aliases=alias,
        scratch_shapes=list(scratch),
        compiler_params=pltpu.CompilerParams(vmem_limit_bytes=VMEM_LIMIT),
        cost_estimate=pl.CostEstimate(flops=flops, bytes_accessed=moved, transcendentals=0),
    )(*operands)


def on_device(density, diffusion, drift_speed, levels, coefficient):
    rows, cols = density.shape[1:]
    doms, grids = lax.axis_size("dom"), lax.axis_size("grp")
    many, strips = rows // TILE, cols // LANES
    per_chunk = strips // SQUARE
    depth = (rows * doms).bit_length() - 1
    tiles = [tiles_of(x[0]) for x in (density, diffusion, drift_speed)]
    me = (lax.axis_index("grp") % SQUARE).astype(jnp.int32)[None]
    dom = lax.axis_index("dom").astype(jnp.int32)[None]

    def vmem(*shape):
        return pltpu.VMEM(shape, jnp.float32)

    near_pairs = [(d, d ^ 1) for d in range(doms)]
    far_pairs = [(d, min(max((d - 1 ^ 1) + 1, 0), doms - 1)) for d in range(doms)]
    (ones,) = call(ones_kernel, [(many, LANES)], (), flops=LOAD_FLOPS * rows * cols)
    keep, weight = call(
        functools.partial(weights_kernel, depth),
        [(3, many, LANES), (4, many, LANES)],
        (levels, coefficient, ones),
        2,
    )
    near, far = call(
        pack_kernel,
        [(strips, 2 * TILE, LANES)] * 2,
        (dom, weight, *tiles),
        1,
    )
    near = lax.ppermute(near, "dom", near_pairs)
    far = lax.ppermute(far, "dom", far_pairs)
    place = (strips, TILE, many, LANES)
    (state,) = call(
        inner_kernel,
        [place],
        tiles,
        0,
        [vmem(strips + 2, *place[1:])] * 2 + [vmem(*place)] * 4,
        flops=40 * rows * cols,
    )
    chunk = (per_chunk * TILE + -(-per_chunk // many), many, LANES)
    own, *others = call(
        functools.partial(edge_kernel, per_chunk, doms),
        [chunk] * SQUARE,
        (dom, me, weight, *tiles, state, near, far),
        2,
        [vmem(3, strips, SLAB, LANES)]
        + [vmem(strips + 2, HALF, TILE, LANES)] * 2
        + [vmem(strips, HALF, TILE, LANES)] * 4,
        flops=40 * SLAB * cols,
    )

    def swap(array, meet):
        devices = [(g, d) for g in range(grids) for d in range(doms)]
        pairs = [(g * doms + d, (g ^ partners(d % 2)[meet]) * doms + d) for g, d in devices]
        return lax.ppermute(array, ("grp", "dom"), pairs)

    half = (chunk[0] - per_chunk * TILE + per_chunk * TILE // STREAMS, many, LANES)
    theirs = [swap(array, meet) for meet, array in enumerate(others, 1)]
    streams = call(
        functools.partial(split_kernel, per_chunk), [half] * STREAMS, (own, *theirs)
    )
    nodal = None
    for stream, total in enumerate(streams):
        apart = SQUARE
        while apart < grids:
            other = lax.ppermute(total, "grp", [(g, g ^ apart) for g in range(grids)])
            (total,) = call(sum_kernel, [half], (total, other))
            apart *= 2
        totals = [total] + [swap(total, meet) for meet in range(1, SQUARE)]
        (nodal,) = call(
            functools.partial(nodal_kernel, per_chunk, stream),
            [(many, strips, TILE, LANES)],
            (dom, me, keep, *totals),
            2,
            [
                vmem(SQUARE, many, per_chunk // STREAMS, TILE, LANES),
                pltpu.SemaphoreType.DMA((SQUARE, many)),
            ],
            out_space=pl.ANY,
            onto=nodal,
        )
    return block_of(nodal)[None]


def solution(mesh):
    return jax.shard_map(
        on_device,
        mesh=mesh,
        in_specs=(
            P("grp", "dom", None),
            P("grp", "dom", None),
            P("grp", "dom", None),
            P("grp"),
            P("grp"),
        ),
        out_specs=P("grp", "dom", None),
        check_vma=False,
    )
```

```python
import functools

import jax
import jax.numpy as jnp
from jax import lax
from jax.experimental import pallas as pl
from jax.experimental.pallas import tpu as pltpu
from jax.sharding import PartitionSpec as P

STEPS = 4
LANES = 128
TILE = 8
HALF = TILE // 2
SLAB = 4 * TILE
SQUARE = 4
UNROLL = 16
VMEM_LIMIT = 40 * 1024 * 1024
LOAD_FLOPS = 4000


def tiles_of(block):
    rows, cols = block.shape
    return block.reshape(rows // TILE, TILE, cols // LANES, LANES).transpose(0, 2, 1, 3)


def block_of(tiles):
    many, strips = tiles.shape[:2]
    return tiles.transpose(0, 2, 1, 3).reshape(many * TILE, strips * LANES)


def flat(ref):
    return ref.reshape(ref.size // LANES, LANES)


def spaced(first, count, stride):
    return pl.ds(first, count, stride=stride) if count > 1 else pl.ds(first, 1)


def roll_rows(value, shift):
    count = value.shape[0]
    return pltpu.roll(value, shift % count, 0) if count > 1 else value


def per_strip(strips, body, unroll):
    def step(j, carry):
        body(j)
        return carry

    lax.fori_loop(0, strips, step, 0, unroll=unroll)


def advance(first, count, classes, source, coefs, emit):
    shape = source.shape[2:]
    lanes = lax.broadcasted_iota(jnp.int32, shape, 1)
    center, above_c, below_c, side = coefs

    def body(k, carry):
        j = first + k
        cur, right_prev, left_cur = carry
        nxt = [source[j + 2, t] for t in range(classes)]
        left_next = [pltpu.roll(x, LANES - 1, 1) for x in nxt]
        right_cur = [pltpu.roll(x, 1, 1) for x in cur]
        above = cur[1:] + [roll_rows(cur[0], -1)]
        below = [roll_rows(cur[-1], 1)] + cur[:-1]
        new = []
        for t in range(classes):
            left = jnp.where(lanes == 0, right_prev[t], right_cur[t])
            right = jnp.where(lanes == LANES - 1, left_next[t], left_cur[t])
            new.append(
                center[j, t] * cur[t]
                + above_c[j, t] * above[t]
                + below_c[j, t] * below[t]
                + side[j, t] * (left + right)
            )
        emit(j, k, new)
        return nxt, right_cur, left_next

    prev, cur = ([source[first + at, t] for t in range(classes)] for at in range(2))
    ends = [pltpu.roll(x, 1, 1) for x in prev], [pltpu.roll(x, LANES - 1, 1) for x in cur]
    lax.fori_loop(0, count, body, (cur, *ends), unroll=min(count, UNROLL))


def run_steps(strips, classes, load, buffers, coefs, last):
    center, above_c, below_c, side = coefs
    for buf in buffers:
        for edge in (0, strips + 1):
            buf[edge] = jnp.zeros(buf.shape[1:], jnp.float32)

    def begin(j):
        for t in range(classes):
            state, diffuse, drifts = load(j, t)
            half = 0.5 * drifts
            buffers[0][j + 1, t] = state
            center[j, t] = 1.0 - 4.0 * diffuse
            above_c[j, t] = diffuse - half
            below_c[j, t] = diffuse + half
            side[j, t] = diffuse

    per_strip(strips, begin, min(strips, UNROLL))
    for step in range(STEPS - 1):
        source, target = buffers[step % 2], buffers[1 - step % 2]

        def keep(j, _, new, target=target):
            for t in range(classes):
                target[j + 1, t] = new[t]

        advance(0, strips, classes, source, coefs, keep)
    last(buffers[(STEPS - 1) % 2])


def surpluses(s, prev, weights):
    fine, mid, low, coef = weights
    return (
        fine * (s[0] - 0.5 * (prev + s[1])),
        mid * (s[1] - 0.5 * (prev + s[3])),
        fine * (s[2] - 0.5 * (s[1] + s[3])),
        low * (s[3] - 0.5 * (prev + s[7])),
        fine * (s[4] - 0.5 * (s[3] + s[5])),
        mid * (s[5] - 0.5 * (s[3] + s[7])),
        fine * (s[6] - 0.5 * (s[5] + s[7])),
        coef * s[7],
    )


def ones_kernel(out_ref):
    out_ref[...] = jnp.ones(out_ref.shape, jnp.float32)


def weights_kernel(depth, level_ref, coef_ref, ones_ref, keep_ref, weight_ref):
    coef = coef_ref[0].astype(jnp.float32)
    for down in range(3):
        keep_ref[down] = jnp.where(level_ref[0] >= depth - down, ones_ref[...], 0.0)
        weight_ref[down] = coef * keep_ref[down]
    weight_ref[3] = coef * ones_ref[...]


def pack_kernel(dom_ref, weight_ref, dens_ref, diff_ref, drift_ref, near_ref, far_ref):
    del weight_ref
    many, strips = dens_ref.shape[:2]
    odd = dom_ref[0] % 2 == 1
    upper = lax.broadcasted_iota(jnp.int32, (TILE, LANES), 0) < HALF

    def body(j):
        drift_last = pltpu.roll(drift_ref[many - 1, j], HALF, 0)
        mix_next = jnp.where(upper, drift_last, diff_ref[many - 1, j])
        mix_prev = jnp.where(upper, diff_ref[0, j], pltpu.roll(drift_ref[0, j], HALF, 0))
        to_next, to_prev = (dens_ref[many - 1, j], mix_next), (dens_ref[0, j], mix_prev)
        for k in range(2):
            at = pl.ds(k * TILE, TILE)
            far_ref[j, at] = jnp.where(odd, to_next[k], to_prev[k])
            near_ref[j, at] = jnp.where(odd, to_prev[k], to_next[k])

    per_strip(strips, body, 4)


def middle_tiles(many):
    return list(range(many // 4, many - many // 4)) if many >= 4 else []


def outer_tiles(many):
    return [m for m in range(many) if m not in middle_tiles(many)]


def emit_tiles(tiles, per_chunk, scratch, out_ref, j, part, weighted, before):
    many = scratch.shape[1]
    by_row = flat(scratch)
    for t in range(TILE):
        by_row[spaced(j * many * TILE + t, many, TILE), :] = weighted[t]
    for k, m in enumerate(tiles):
        out_ref[part * len(tiles) + k] = scratch[j, m]
    last = per_chunk * len(tiles) + part // TILE
    out_ref[last, pl.ds(lax.rem(part, TILE), 1), :] = before


def inner_kernel(
    per_chunk, dom_ref, me_ref, weight_ref, dens_ref, diff_ref, drift_ref, state_ref, *refs
):
    many, strips = dens_ref.shape[:2]
    *out_refs, scratch, state_a, state_b = refs[:-4]
    coefs = refs[-4:]
    rows = [flat(ref) for ref in (dens_ref, diff_ref, drift_ref)]
    weights = [weight_ref[k] for k in range(4)]
    tiles = middle_tiles(many)

    def load(j, t):
        at = spaced(j * TILE + t, many, strips * TILE)
        return [ref[at, :] for ref in rows]

    def finish(out_ref, j, part, new):
        for t in range(TILE):
            state_ref[j, t] = new[t]
        if out_ref is not None:
            weighted = surpluses(new, roll_rows(new[7], 1), weights)
            before = weighted[7][tiles[0] - 1 : tiles[0]]
            emit_tiles(tiles, per_chunk, scratch, out_ref, j, part, weighted, before)

    def last(source):
        for out_ref, away in zip(out_refs or [None] * SQUARE, partners(dom_ref[0])):
            first = (me_ref[0] ^ away) * per_chunk
            emit = functools.partial(finish, out_ref)
            advance(first, per_chunk, TILE, source, coefs, emit)

    run_steps(strips, TILE, load, (state_a, state_b), coefs, last)


def partners(dom):
    return 0, 1 + dom % 2, 2 - dom % 2, 3


def edge_kernel(
    per_chunk, doms, dom_ref, me_ref, weight_ref, dens_ref, *refs
):
    many, strips = dens_ref.shape[:2]
    dom = dom_ref[0]
    odd = dom % 2 == 1
    diff_ref, drift_ref, state_ref, near_ref, far_ref, *rest = refs
    out_refs, (scratch, slab, state_a, state_b, *coefs) = rest[:-8], rest[-8:]

    def stage(j):
        far, near = far_ref[j], near_ref[j]
        up = jnp.where(dom == 0, 0.0, jnp.where(odd, near, far))
        dn = jnp.where(dom == doms - 1, 0.0, jnp.where(odd, far, near))
        up_mix, dn_mix = up[TILE:], dn[TILE:]
        tiles = (
            (up[:TILE], dens_ref[0, j], dens_ref[many - 1, j], dn[:TILE]),
            (up_mix, diff_ref[0, j], diff_ref[many - 1, j], dn_mix),
            (
                pltpu.roll(up_mix, HALF, 0),
                drift_ref[0, j],
                drift_ref[many - 1, j],
                pltpu.roll(dn_mix, HALF, 0),
            ),
        )
        for k, column in enumerate(tiles):
            for e, tile in enumerate(column):
                slab[k, j, e * TILE : (e + 1) * TILE] = tile

    per_strip(strips, stage, 4)
    slabs = flat(slab)

    def load(j, t):
        return [
            slabs[pl.ds((k * strips + j) * SLAB + t, TILE, stride=HALF), :] for k in range(3)
        ]

    place = lax.broadcasted_iota(jnp.int32, (many, LANES), 0)
    weights = [weight_ref[k] for k in range(4)]

    def finish(out_ref, j, part, new):
        s = [state_ref[j, t] for t in range(TILE)]
        for t in range(HALF):
            s[t] = jnp.where(place == 0, new[t][2:3], s[t])
            s[HALF + t] = jnp.where(place == many - 1, new[t][5:6], s[HALF + t])
        before = new[HALF - 1][1:2]
        weighted = surpluses(s, jnp.where(place == 0, before, roll_rows(s[7], 1)), weights)
        before = weights[3][0:1] * before
        tiles = outer_tiles(many)
        emit_tiles(tiles, per_chunk, scratch, out_ref, j, part, weighted, before)

    def last(source):
        for out_ref, away in zip(out_refs, partners(dom_ref[0])):
            first = (me_ref[0] ^ away) * per_chunk
            emit = functools.partial(finish, out_ref)
            advance(first, per_chunk, HALF, source, coefs, emit)

    run_steps(strips, HALF, load, (state_a, state_b), coefs, last)


def sum_kernel(*refs):
    *parts, out_ref = refs
    total = parts[0][...]
    for part in parts[1:]:
        total = total + part[...]
    out_ref[...] = total


def nodal_kernel(per_chunk, tiles, dom_ref, me_ref, keep_ref, *refs):
    totals, middles, (out_ref, values, sems) = refs[:SQUARE], refs[SQUARE:-3], refs[-3:]
    count = len(tiles)
    fine, mid, low = (keep_ref[k, 0:count] for k in range(3))
    place = lax.broadcasted_iota(jnp.int32, (count, LANES), 0)
    gaps = [k for k in range(1, count) if tiles[k] != tiles[k - 1] + 1]
    copies = []
    for k, (ref, away) in enumerate(zip(totals, partners(dom_ref[0]))):
        first = (me_ref[0] ^ away) * per_chunk
        by_row = flat(values.at[k])

        def body(part, k=k, ref=ref, by_row=by_row):
            w = [
                flat(ref)[spaced(part * count * TILE + t, count, TILE), :] for t in range(TILE)
            ]
            before = ref[per_chunk * count + part // TILE, pl.ds(lax.rem(part, TILE), 1), :]
            prev = jnp.where(place == 0, before, roll_rows(w[7], 1))
            for gap in gaps:
                across = tiles[gap] - tiles[gap - 1] - 1
                before = middles[k][part * across + across - 1, TILE - 1 : TILE, :]
                prev = jnp.where(place == gap, before, prev)
            v3 = 0.5 * (prev + w[7]) + low * w[3]
            v1 = 0.5 * (prev + v3) + mid * w[1]
            v5 = 0.5 * (v3 + w[7]) + mid * w[5]
            rows = (
                0.5 * (prev + v1) + fine * w[0],
                v1,
                0.5 * (v1 + v3) + fine * w[2],
                v3,
                0.5 * (v3 + v5) + fine * w[4],
                v5,
                0.5 * (v5 + w[7]) + fine * w[6],
                w[7],
            )
            for t in range(TILE):
                by_row[spaced(part * TILE + t, count, per_chunk * TILE), :] = rows[t]

        per_strip(per_chunk, body, min(per_chunk, 4))
        for e, m in enumerate(tiles):
            copy = pltpu.make_async_copy(
                values.at[k, e], out_ref.at[m, pl.ds(first, per_chunk)], sems.at[k, e]
            )
            copy.start()
            copies.append(copy)
    for copy in copies:
        copy.wait()


def call(
    kernel, out_shapes, operands, in_smem=0, scratch=(), flops=0, out_space=pltpu.VMEM, onto=None
):
    spaces = [pltpu.SMEM] * in_smem + [pltpu.VMEM] * (len(operands) - in_smem)
    alias = {}
    if onto is not None:
        alias = {len(operands): 0}
        spaces, operands = spaces + [out_space], (*operands, onto)
    specs = [pl.BlockSpec(memory_space=space) for space in spaces]
    moved = 4 * sum(x.size for x in operands)
    return pl.pallas_call(
        kernel,
        out_shape=[jax.ShapeDtypeStruct(shape, jnp.float32) for shape in out_shapes],
        in_specs=specs,
        out_specs=[pl.BlockSpec(memory_space=out_space) for _ in out_shapes],
        input_output_aliases=alias,
        scratch_shapes=list(scratch),
        compiler_params=pltpu.CompilerParams(vmem_limit_bytes=VMEM_LIMIT),
        cost_estimate=pl.CostEstimate(flops=flops, bytes_accessed=moved, transcendentals=0),
    )(*operands)


def on_device(density, diffusion, drift_speed, levels, coefficient):
    rows, cols = density.shape[1:]
    doms, grids = lax.axis_size("dom"), lax.axis_size("grp")
    many, strips = rows // TILE, cols // LANES
    per_chunk = strips // SQUARE
    depth = (rows * doms).bit_length() - 1
    tiles = [tiles_of(x[0]) for x in (density, diffusion, drift_speed)]
    me = (lax.axis_index("grp") % SQUARE).astype(jnp.int32)[None]
    dom = lax.axis_index("dom").astype(jnp.int32)[None]

    def vmem(*shape):
        return pltpu.VMEM(shape, jnp.float32)

    near_pairs = [(d, d ^ 1) for d in range(doms)]
    far_pairs = [(d, min(max((d - 1 ^ 1) + 1, 0), doms - 1)) for d in range(doms)]
    (ones,) = call(ones_kernel, [(many, LANES)], (), flops=LOAD_FLOPS * rows * cols)
    keep, weight = call(
        functools.partial(weights_kernel, depth),
        [(3, many, LANES), (4, many, LANES)],
        (levels, coefficient, ones),
        2,
    )
    near, far = call(
        pack_kernel,
        [(strips, 2 * TILE, LANES)] * 2,
        (dom, weight, *tiles),
        1,
    )
    near = lax.ppermute(near, "dom", near_pairs)
    far = lax.ppermute(far, "dom", far_pairs)
    place = (strips, TILE, many, LANES)
    pieces = (strips, many, TILE, LANES)

    def chunk(tiles):
        return per_chunk * len(tiles) + -(-per_chunk // TILE), TILE, LANES

    middle, outer = middle_tiles(many), outer_tiles(many)
    state, *inside = call(
        functools.partial(inner_kernel, per_chunk),
        [place] + [chunk(middle)] * (SQUARE if middle else 0),
        (dom, me, weight, *tiles),
        2,
        [vmem(*pieces)] + [vmem(strips + 2, *place[1:])] * 2 + [vmem(*place)] * 4,
        flops=40 * rows * cols,
    )
    outside = call(
        functools.partial(edge_kernel, per_chunk, doms),
        [chunk(outer)] * SQUARE,
        (dom, me, weight, *tiles, state, near, far),
        2,
        [vmem(*pieces), vmem(3, strips, SLAB, LANES)]
        + [vmem(strips + 2, HALF, TILE, LANES)] * 2
        + [vmem(strips, HALF, TILE, LANES)] * 4,
        flops=40 * SLAB * cols,
    )

    def swap(array, meet):
        devices = [(g, d) for g in range(grids) for d in range(doms)]
        pairs = [(g * doms + d, (g ^ partners(d % 2)[meet]) * doms + d) for g, d in devices]
        return lax.ppermute(array, ("grp", "dom"), pairs)

    def over_grids(own, *others):
        theirs = [swap(array, meet) for meet, array in enumerate(others, 1)]
        (total,) = call(sum_kernel, [own.shape], (own, *theirs))
        apart = SQUARE
        while apart < grids:
            other = lax.ppermute(total, "grp", [(g, g ^ apart) for g in range(grids)])
            (total,) = call(sum_kernel, [own.shape], (total, other))
            apart *= 2
        return [total] + [swap(total, meet) for meet in range(1, SQUARE)]

    nodal, totals = None, []
    for some, weighted in ((middle, inside), (outer, outside)):
        if not some:
            continue
        totals = over_grids(*weighted) + totals
        (nodal,) = call(
            functools.partial(nodal_kernel, per_chunk, some),
            [(many, strips, TILE, LANES)],
            (dom, me, keep, *totals),
            2,
            [
                vmem(SQUARE, len(some), per_chunk, TILE, LANES),
                pltpu.SemaphoreType.DMA((SQUARE, len(some))),
            ],
            out_space=pl.ANY,
            onto=nodal,
        )
    return block_of(nodal)[None]


def solution(mesh):
    return jax.shard_map(
        on_device,
        mesh=mesh,
        in_specs=(
            P("grp", "dom", None),
            P("grp", "dom", None),
            P("grp", "dom", None),
            P("grp"),
            P("grp"),
        ),
        out_specs=P("grp", "dom", None),
        check_vma=False,
    )
```

```python
import functools

import jax
import jax.numpy as jnp
from jax import lax
from jax.experimental import pallas as pl
from jax.experimental.pallas import tpu as pltpu
from jax.sharding import PartitionSpec as P

STEPS = 4
LANES = 128
TILE = 8
HALF = TILE // 2
SLAB = 4 * TILE
SQUARE = 4
UNROLL = 16
VMEM_LIMIT = 40 * 1024 * 1024
LOAD_FLOPS = 4000
MIDDLE_FLOPS = 2000


def tiles_of(block):
    rows, cols = block.shape
    return block.reshape(rows // TILE, TILE, cols // LANES, LANES).transpose(0, 2, 1, 3)


def block_of(tiles):
    many, strips = tiles.shape[:2]
    return tiles.transpose(0, 2, 1, 3).reshape(many * TILE, strips * LANES)


def flat(ref):
    return ref.reshape(ref.size // LANES, LANES)


def spaced(first, count, stride):
    return pl.ds(first, count, stride=stride) if count > 1 else pl.ds(first, 1)


def roll_rows(value, shift):
    count = value.shape[0]
    return pltpu.roll(value, shift % count, 0) if count > 1 else value


def per_strip(strips, body, unroll):
    def step(j, carry):
        body(j)
        return carry

    lax.fori_loop(0, strips, step, 0, unroll=unroll)


def advance(first, count, classes, source, coefs, emit):
    shape = source.shape[2:]
    lanes = lax.broadcasted_iota(jnp.int32, shape, 1)
    center, above_c, below_c, side = coefs

    def body(k, carry):
        j = first + k
        cur, right_prev, left_cur = carry
        nxt = [source[j + 2, t] for t in range(classes)]
        left_next = [pltpu.roll(x, LANES - 1, 1) for x in nxt]
        right_cur = [pltpu.roll(x, 1, 1) for x in cur]
        above = cur[1:] + [roll_rows(cur[0], -1)]
        below = [roll_rows(cur[-1], 1)] + cur[:-1]
        new = []
        for t in range(classes):
            left = jnp.where(lanes == 0, right_prev[t], right_cur[t])
            right = jnp.where(lanes == LANES - 1, left_next[t], left_cur[t])
            new.append(
                center[j, t] * cur[t]
                + above_c[j, t] * above[t]
                + below_c[j, t] * below[t]
                + side[j, t] * (left + right)
            )
        emit(j, k, new)
        return nxt, right_cur, left_next

    prev, cur = ([source[first + at, t] for t in range(classes)] for at in range(2))
    ends = [pltpu.roll(x, 1, 1) for x in prev], [pltpu.roll(x, LANES - 1, 1) for x in cur]
    lax.fori_loop(0, count, body, (cur, *ends), unroll=min(count, UNROLL))


def run_steps(strips, classes, load, buffers, coefs, last):
    center, above_c, below_c, side = coefs
    for buf in buffers:
        for edge in (0, strips + 1):
            buf[edge] = jnp.zeros(buf.shape[1:], jnp.float32)

    def begin(j):
        for t in range(classes):
            state, diffuse, drifts = load(j, t)
            half = 0.5 * drifts
            buffers[0][j + 1, t] = state
            center[j, t] = 1.0 - 4.0 * diffuse
            above_c[j, t] = diffuse - half
            below_c[j, t] = diffuse + half
            side[j, t] = diffuse

    per_strip(strips, begin, min(strips, UNROLL))
    for step in range(STEPS - 1):
        source, target = buffers[step % 2], buffers[1 - step % 2]

        def keep(j, _, new, target=target):
            for t in range(classes):
                target[j + 1, t] = new[t]

        advance(0, strips, classes, source, coefs, keep)
    last(buffers[(STEPS - 1) % 2])


def surpluses(s, prev, weights):
    fine, mid, low, coef = weights
    return (
        fine * (s[0] - 0.5 * (prev + s[1])),
        mid * (s[1] - 0.5 * (prev + s[3])),
        fine * (s[2] - 0.5 * (s[1] + s[3])),
        low * (s[3] - 0.5 * (prev + s[7])),
        fine * (s[4] - 0.5 * (s[3] + s[5])),
        mid * (s[5] - 0.5 * (s[3] + s[7])),
        fine * (s[6] - 0.5 * (s[5] + s[7])),
        coef * s[7],
    )


def ones_kernel(out_ref):
    out_ref[...] = jnp.ones(out_ref.shape, jnp.float32)


def weights_kernel(depth, level_ref, coef_ref, ones_ref, keep_ref, weight_ref):
    coef = coef_ref[0].astype(jnp.float32)
    for down in range(3):
        keep_ref[down] = jnp.where(level_ref[0] >= depth - down, ones_ref[...], 0.0)
        weight_ref[down] = coef * keep_ref[down]
    weight_ref[3] = coef * ones_ref[...]


def pack_kernel(dom_ref, weight_ref, dens_ref, diff_ref, drift_ref, near_ref, far_ref):
    del weight_ref
    many, strips = dens_ref.shape[:2]
    odd = dom_ref[0] % 2 == 1
    upper = lax.broadcasted_iota(jnp.int32, (TILE, LANES), 0) < HALF

    def body(j):
        drift_last = pltpu.roll(drift_ref[many - 1, j], HALF, 0)
        mix_next = jnp.where(upper, drift_last, diff_ref[many - 1, j])
        mix_prev = jnp.where(upper, diff_ref[0, j], pltpu.roll(drift_ref[0, j], HALF, 0))
        to_next, to_prev = (dens_ref[many - 1, j], mix_next), (dens_ref[0, j], mix_prev)
        for k in range(2):
            at = pl.ds(k * TILE, TILE)
            far_ref[j, at] = jnp.where(odd, to_next[k], to_prev[k])
            near_ref[j, at] = jnp.where(odd, to_prev[k], to_next[k])

    per_strip(strips, body, 4)


def middle_tiles(many):
    return list(range(1, many - 1)) if many >= 4 else []


def outer_tiles(many):
    return [m for m in range(many) if m not in middle_tiles(many)]


def emit_tiles(tiles, per_chunk, scratch, out_ref, j, part, weighted, before):
    many = scratch.shape[1]
    by_row = flat(scratch)
    for t in range(TILE):
        by_row[spaced(j * many * TILE + t, many, TILE), :] = weighted[t]
    for k, m in enumerate(tiles):
        out_ref[part * len(tiles) + k] = scratch[j, m]
    last = per_chunk * len(tiles) + part // TILE
    out_ref[last, pl.ds(lax.rem(part, TILE), 1), :] = before


def inner_kernel(
    per_chunk, dom_ref, me_ref, weight_ref, dens_ref, diff_ref, drift_ref, state_ref, *refs
):
    many, strips = dens_ref.shape[:2]
    *out_refs, scratch, state_a, state_b = refs[:-4]
    coefs = refs[-4:]
    rows = [flat(ref) for ref in (dens_ref, diff_ref, drift_ref)]
    weights = [weight_ref[k] for k in range(4)]
    tiles = middle_tiles(many)

    def load(j, t):
        at = spaced(j * TILE + t, many, strips * TILE)
        return [ref[at, :] for ref in rows]

    def finish(out_ref, j, part, new):
        for t in range(TILE):
            state_ref[j, t] = new[t]
        if out_ref is not None:
            weighted = surpluses(new, roll_rows(new[7], 1), weights)
            before = weighted[7][tiles[0] - 1 : tiles[0]]
            emit_tiles(tiles, per_chunk, scratch, out_ref, j, part, weighted, before)

    def last(source):
        for out_ref, away in zip(out_refs or [None] * SQUARE, partners(dom_ref[0])):
            first = (me_ref[0] ^ away) * per_chunk
            emit = functools.partial(finish, out_ref)
            advance(first, per_chunk, TILE, source, coefs, emit)

    run_steps(strips, TILE, load, (state_a, state_b), coefs, last)


def partners(dom):
    return 0, 1 + dom % 2, 2 - dom % 2, 3


def edge_kernel(
    per_chunk, doms, dom_ref, me_ref, weight_ref, dens_ref, *refs
):
    many, strips = dens_ref.shape[:2]
    dom = dom_ref[0]
    odd = dom % 2 == 1
    diff_ref, drift_ref, state_ref, near_ref, far_ref, *rest = refs
    kept_ref, sent_ref, scratch, slab, state_a, state_b, *coefs = rest
    out_refs = kept_ref.at[0], sent_ref.at[0], kept_ref.at[1], sent_ref.at[1]

    def stage(j):
        far, near = far_ref[j], near_ref[j]
        up = jnp.where(dom == 0, 0.0, jnp.where(odd, near, far))
        dn = jnp.where(dom == doms - 1, 0.0, jnp.where(odd, far, near))
        up_mix, dn_mix = up[TILE:], dn[TILE:]
        tiles = (
            (up[:TILE], dens_ref[0, j], dens_ref[many - 1, j], dn[:TILE]),
            (up_mix, diff_ref[0, j], diff_ref[many - 1, j], dn_mix),
            (
                pltpu.roll(up_mix, HALF, 0),
                drift_ref[0, j],
                drift_ref[many - 1, j],
                pltpu.roll(dn_mix, HALF, 0),
            ),
        )
        for k, column in enumerate(tiles):
            for e, tile in enumerate(column):
                slab[k, j, e * TILE : (e + 1) * TILE] = tile

    per_strip(strips, stage, 4)
    slabs = flat(slab)

    def load(j, t):
        return [
            slabs[pl.ds((k * strips + j) * SLAB + t, TILE, stride=HALF), :] for k in range(3)
        ]

    place = lax.broadcasted_iota(jnp.int32, (many, LANES), 0)
    weights = [weight_ref[k] for k in range(4)]

    def finish(out_ref, j, part, new):
        s = [state_ref[j, t] for t in range(TILE)]
        for t in range(HALF):
            s[t] = jnp.where(place == 0, new[t][2:3], s[t])
            s[HALF + t] = jnp.where(place == many - 1, new[t][5:6], s[HALF + t])
        before = new[HALF - 1][1:2]
        weighted = surpluses(s, jnp.where(place == 0, before, roll_rows(s[7], 1)), weights)
        before = weights[3][0:1] * before
        tiles = outer_tiles(many)
        emit_tiles(tiles, per_chunk, scratch, out_ref, j, part, weighted, before)

    def last(source):
        for out_ref, away in zip(out_refs, partners(dom_ref[0])):
            first = (me_ref[0] ^ away) * per_chunk
            emit = functools.partial(finish, out_ref)
            advance(first, per_chunk, HALF, source, coefs, emit)

    run_steps(strips, HALF, load, (state_a, state_b), coefs, last)


def sum_kernel(*refs):
    *parts, out_ref = refs
    total = parts[0][...]
    for part in parts[1:]:
        total = total + part[...]
    out_ref[...] = total


def swapped_kernel(mine_ref, theirs_ref, out_ref):
    for k in range(2):
        out_ref[k] = mine_ref[k] + theirs_ref[1 - k]


def nodal_kernel(per_chunk, tiles, dom_ref, me_ref, keep_ref, *refs):
    out_ref, values, sems = refs[-3:]
    if refs[0].ndim == 4:
        totals, middles = [refs[k % 2].at[k // 2] for k in range(SQUARE)], refs[2:]
    else:
        totals, middles = refs[:SQUARE], ()
    count = len(tiles)
    fine, mid, low = (keep_ref[k, 0:count] for k in range(3))
    place = lax.broadcasted_iota(jnp.int32, (count, LANES), 0)
    gaps = [k for k in range(1, count) if tiles[k] != tiles[k - 1] + 1]
    copies = []
    for k, (ref, away) in enumerate(zip(totals, partners(dom_ref[0]))):
        first = (me_ref[0] ^ away) * per_chunk
        by_row = flat(values.at[k])

        def body(part, k=k, ref=ref, by_row=by_row):
            w = [
                flat(ref)[spaced(part * count * TILE + t, count, TILE), :] for t in range(TILE)
            ]
            before = ref[per_chunk * count + part // TILE, pl.ds(lax.rem(part, TILE), 1), :]
            prev = jnp.where(place == 0, before, roll_rows(w[7], 1))
            for gap in gaps:
                across = tiles[gap] - tiles[gap - 1] - 1
                before = middles[k][part * across + across - 1, TILE - 1 : TILE, :]
                prev = jnp.where(place == gap, before, prev)
            v3 = 0.5 * (prev + w[7]) + low * w[3]
            v1 = 0.5 * (prev + v3) + mid * w[1]
            v5 = 0.5 * (v3 + w[7]) + mid * w[5]
            rows = (
                0.5 * (prev + v1) + fine * w[0],
                v1,
                0.5 * (v1 + v3) + fine * w[2],
                v3,
                0.5 * (v3 + v5) + fine * w[4],
                v5,
                0.5 * (v5 + w[7]) + fine * w[6],
                w[7],
            )
            for t in range(TILE):
                by_row[spaced(part * TILE + t, count, per_chunk * TILE), :] = rows[t]

        per_strip(per_chunk, body, min(per_chunk, 4))
        for e, m in enumerate(tiles):
            copy = pltpu.make_async_copy(
                values.at[k, e], out_ref.at[m, pl.ds(first, per_chunk)], sems.at[k, e]
            )
            copy.start()
            copies.append(copy)
    for copy in copies:
        copy.wait()


def call(
    kernel, out_shapes, operands, in_smem=0, scratch=(), flops=0, out_space=pltpu.VMEM, onto=None
):
    spaces = [pltpu.SMEM] * in_smem + [pltpu.VMEM] * (len(operands) - in_smem)
    alias = {}
    if onto is not None:
        alias = {len(operands): 0}
        spaces, operands = spaces + [out_space], (*operands, onto)
    specs = [pl.BlockSpec(memory_space=space) for space in spaces]
    moved = 4 * sum(x.size for x in operands)
    return pl.pallas_call(
        kernel,
        out_shape=[jax.ShapeDtypeStruct(shape, jnp.float32) for shape in out_shapes],
        in_specs=specs,
        out_specs=[pl.BlockSpec(memory_space=out_space) for _ in out_shapes],
        input_output_aliases=alias,
        scratch_shapes=list(scratch),
        compiler_params=pltpu.CompilerParams(vmem_limit_bytes=VMEM_LIMIT),
        cost_estimate=pl.CostEstimate(flops=flops, bytes_accessed=moved, transcendentals=0),
    )(*operands)


def on_device(density, diffusion, drift_speed, levels, coefficient):
    rows, cols = density.shape[1:]
    doms, grids = lax.axis_size("dom"), lax.axis_size("grp")
    many, strips = rows // TILE, cols // LANES
    per_chunk = strips // SQUARE
    depth = (rows * doms).bit_length() - 1
    tiles = [tiles_of(x[0]) for x in (density, diffusion, drift_speed)]
    me = (lax.axis_index("grp") % SQUARE).astype(jnp.int32)[None]
    dom = lax.axis_index("dom").astype(jnp.int32)[None]

    def vmem(*shape):
        return pltpu.VMEM(shape, jnp.float32)

    near_pairs = [(d, d ^ 1) for d in range(doms)]
    far_pairs = [(d, min(max((d - 1 ^ 1) + 1, 0), doms - 1)) for d in range(doms)]
    (ones,) = call(ones_kernel, [(many, LANES)], (), flops=LOAD_FLOPS * rows * cols)
    keep, weight = call(
        functools.partial(weights_kernel, depth),
        [(3, many, LANES), (4, many, LANES)],
        (levels, coefficient, ones),
        2,
    )
    near, far = call(
        pack_kernel,
        [(strips, 2 * TILE, LANES)] * 2,
        (dom, weight, *tiles),
        1,
    )
    near = lax.ppermute(near, "dom", near_pairs)
    far = lax.ppermute(far, "dom", far_pairs)
    place = (strips, TILE, many, LANES)
    pieces = (strips, many, TILE, LANES)

    def chunk(tiles):
        return per_chunk * len(tiles) + -(-per_chunk // TILE), TILE, LANES

    middle, outer = middle_tiles(many), outer_tiles(many)
    state, *inside = call(
        functools.partial(inner_kernel, per_chunk),
        [place] + [chunk(middle)] * (SQUARE if middle else 0),
        (dom, me, weight, *tiles),
        2,
        [vmem(*pieces)] + [vmem(strips + 2, *place[1:])] * 2 + [vmem(*place)] * 4,
        flops=40 * rows * cols,
    )
    kept, sent = call(
        functools.partial(edge_kernel, per_chunk, doms),
        [(2, *chunk(outer))] * 2,
        (dom, me, weight, *tiles, state, near, far),
        2,
        [vmem(*pieces), vmem(3, strips, SLAB, LANES)]
        + [vmem(strips + 2, HALF, TILE, LANES)] * 2
        + [vmem(strips, HALF, TILE, LANES)] * 4,
        flops=40 * SLAB * cols,
    )

    def swap(array, meet):
        devices = [(g, d) for g in range(grids) for d in range(doms)]
        pairs = [(g * doms + d, (g ^ partners(d % 2)[meet]) * doms + d) for g, d in devices]
        return lax.ppermute(array, ("grp", "dom"), pairs)

    def add(kernel, *parts):
        return call(kernel, [parts[0].shape], parts)[0]

    def over_squares(total):
        apart = SQUARE
        while apart < grids:
            other = lax.ppermute(total, "grp", [(g, g ^ apart) for g in range(grids)])
            total = add(sum_kernel, total, other)
            apart *= 2
        return total

    def nodal_values(some, totals, onto, flops=0):
        return call(
            functools.partial(nodal_kernel, per_chunk, some),
            [(many, strips, TILE, LANES)],
            (dom, me, keep, *totals),
            2,
            [
                vmem(SQUARE, len(some), per_chunk, TILE, LANES),
                pltpu.SemaphoreType.DMA((SQUARE, len(some))),
            ],
            flops=flops,
            out_space=pl.ANY,
            onto=onto,
        )[0]

    nodal, inner_totals = None, []
    if middle:
        own, *others = inside
        theirs = [swap(array, meet) for meet, array in enumerate(others, 1)]
        total = over_squares(add(sum_kernel, own, *theirs))
        inner_totals = [total] + [swap(total, meet) for meet in range(1, SQUARE)]
        nodal = nodal_values(middle, inner_totals, None, MIDDLE_FLOPS * rows * cols)
    kept = add(sum_kernel, kept, swap(sent, 1))
    kept = over_squares(add(swapped_kernel, kept, swap(kept, 2)))
    nodal = nodal_values(outer, [kept, swap(kept, 1), *inner_totals], nodal)
    return block_of(nodal)[None]


def solution(mesh):
    return jax.shard_map(
        on_device,
        mesh=mesh,
        in_specs=(
            P("grp", "dom", None),
            P("grp", "dom", None),
            P("grp", "dom", None),
            P("grp"),
            P("grp"),
        ),
        out_specs=P("grp", "dom", None),
        check_vma=False,
    )
```

```python
import functools

import jax
import jax.numpy as jnp
from jax import lax
from jax.experimental import pallas as pl
from jax.experimental.pallas import tpu as pltpu
from jax.sharding import PartitionSpec as P

STEPS = 4
LANES = 128
TILE = 8
HALF = TILE // 2
SLAB = 4 * TILE
SQUARE = 4
UNROLL = 16
VMEM_LIMIT = 40 * 1024 * 1024
LOAD_FLOPS = 4000


def tiles_of(block):
    rows, cols = block.shape
    return block.reshape(rows // TILE, TILE, cols // LANES, LANES).transpose(0, 2, 1, 3)


def block_of(tiles):
    many, strips = tiles.shape[:2]
    return tiles.transpose(0, 2, 1, 3).reshape(many * TILE, strips * LANES)


def flat(ref):
    return ref.reshape(ref.size // LANES, LANES)


def spaced(first, count, stride):
    return pl.ds(first, count, stride=stride) if count > 1 else pl.ds(first, 1)


def roll_rows(value, shift):
    count = value.shape[0]
    return pltpu.roll(value, shift % count, 0) if count > 1 else value


def per_strip(strips, body, unroll):
    def step(j, carry):
        body(j)
        return carry

    lax.fori_loop(0, strips, step, 0, unroll=unroll)


def advance(first, count, classes, source, coefs, emit):
    shape = source.shape[2:]
    lanes = lax.broadcasted_iota(jnp.int32, shape, 1)
    center, above_c, below_c, side = coefs

    def body(k, carry):
        j = first + k
        cur, right_prev, left_cur = carry
        nxt = [source[j + 2, t] for t in range(classes)]
        left_next = [pltpu.roll(x, LANES - 1, 1) for x in nxt]
        right_cur = [pltpu.roll(x, 1, 1) for x in cur]
        above = cur[1:] + [roll_rows(cur[0], -1)]
        below = [roll_rows(cur[-1], 1)] + cur[:-1]
        new = []
        for t in range(classes):
            left = jnp.where(lanes == 0, right_prev[t], right_cur[t])
            right = jnp.where(lanes == LANES - 1, left_next[t], left_cur[t])
            new.append(
                center[j, t] * cur[t]
                + above_c[j, t] * above[t]
                + below_c[j, t] * below[t]
                + side[j, t] * (left + right)
            )
        emit(j, k, new)
        return nxt, right_cur, left_next

    prev, cur = ([source[first + at, t] for t in range(classes)] for at in range(2))
    ends = [pltpu.roll(x, 1, 1) for x in prev], [pltpu.roll(x, LANES - 1, 1) for x in cur]
    lax.fori_loop(0, count, body, (cur, *ends), unroll=min(count, UNROLL))


def run_steps(strips, classes, load, buffers, coefs, last):
    center, above_c, below_c, side = coefs
    for buf in buffers:
        for edge in (0, strips + 1):
            buf[edge] = jnp.zeros(buf.shape[1:], jnp.float32)

    def begin(j):
        for t in range(classes):
            state, diffuse, drifts = load(j, t)
            half = 0.5 * drifts
            buffers[0][j + 1, t] = state
            center[j, t] = 1.0 - 4.0 * diffuse
            above_c[j, t] = diffuse - half
            below_c[j, t] = diffuse + half
            side[j, t] = diffuse

    per_strip(strips, begin, min(strips, UNROLL))
    for step in range(STEPS - 1):
        source, target = buffers[step % 2], buffers[1 - step % 2]

        def keep(j, _, new, target=target):
            for t in range(classes):
                target[j + 1, t] = new[t]

        advance(0, strips, classes, source, coefs, keep)
    last(buffers[(STEPS - 1) % 2])


def surpluses(s, prev, weights):
    fine, mid, low, coef = weights
    return (
        fine * (s[0] - 0.5 * (prev + s[1])),
        mid * (s[1] - 0.5 * (prev + s[3])),
        fine * (s[2] - 0.5 * (s[1] + s[3])),
        low * (s[3] - 0.5 * (prev + s[7])),
        fine * (s[4] - 0.5 * (s[3] + s[5])),
        mid * (s[5] - 0.5 * (s[3] + s[7])),
        fine * (s[6] - 0.5 * (s[5] + s[7])),
        coef * s[7],
    )


def ones_kernel(out_ref):
    out_ref[...] = jnp.ones(out_ref.shape, jnp.float32)


def weights_kernel(depth, level_ref, coef_ref, ones_ref, keep_ref, weight_ref):
    coef = coef_ref[0].astype(jnp.float32)
    for down in range(3):
        keep_ref[down] = jnp.where(level_ref[0] >= depth - down, ones_ref[...], 0.0)
        weight_ref[down] = coef * keep_ref[down]
    weight_ref[3] = coef * ones_ref[...]


def pack_kernel(dom_ref, weight_ref, dens_ref, diff_ref, drift_ref, near_ref, far_ref):
    del weight_ref
    many, strips = dens_ref.shape[:2]
    odd = dom_ref[0] % 2 == 1
    upper = lax.broadcasted_iota(jnp.int32, (TILE, LANES), 0) < HALF

    def body(j):
        drift_last = pltpu.roll(drift_ref[many - 1, j], HALF, 0)
        mix_next = jnp.where(upper, drift_last, diff_ref[many - 1, j])
        mix_prev = jnp.where(upper, diff_ref[0, j], pltpu.roll(drift_ref[0, j], HALF, 0))
        to_next, to_prev = (dens_ref[many - 1, j], mix_next), (dens_ref[0, j], mix_prev)
        for k in range(2):
            at = pl.ds(k * TILE, TILE)
            far_ref[j, at] = jnp.where(odd, to_next[k], to_prev[k])
            near_ref[j, at] = jnp.where(odd, to_prev[k], to_next[k])

    per_strip(strips, body, 4)


def middle_tiles(many):
    return list(range(many // 4, many - many // 4)) if many >= 4 else []


def outer_tiles(many):
    return [m for m in range(many) if m not in middle_tiles(many)]


def emit_tiles(tiles, per_chunk, scratch, out_ref, j, part, weighted, before):
    many = scratch.shape[1]
    by_row = flat(scratch)
    for t in range(TILE):
        by_row[spaced(j * many * TILE + t, many, TILE), :] = weighted[t]
    for k, m in enumerate(tiles):
        out_ref[part * len(tiles) + k] = scratch[j, m]
    last = per_chunk * len(tiles) + part // TILE
    out_ref[last, pl.ds(lax.rem(part, TILE), 1), :] = before


def inner_kernel(
    per_chunk, dom_ref, me_ref, weight_ref, dens_ref, diff_ref, drift_ref, state_ref, *refs
):
    many, strips = dens_ref.shape[:2]
    *out_refs, scratch, state_a, state_b = refs[:-4]
    coefs = refs[-4:]
    rows = [flat(ref) for ref in (dens_ref, diff_ref, drift_ref)]
    weights = [weight_ref[k] for k in range(4)]
    tiles = middle_tiles(many)

    def load(j, t):
        at = spaced(j * TILE + t, many, strips * TILE)
        return [ref[at, :] for ref in rows]

    def finish(out_ref, j, part, new):
        for t in range(TILE):
            state_ref[j, t] = new[t]
        if out_ref is not None:
            weighted = surpluses(new, roll_rows(new[7], 1), weights)
            before = weighted[7][tiles[0] - 1 : tiles[0]]
            emit_tiles(tiles, per_chunk, scratch, out_ref, j, part, weighted, before)

    def last(source):
        for out_ref, away in zip(out_refs or [None] * SQUARE, partners(dom_ref[0])):
            first = (me_ref[0] ^ away) * per_chunk
            emit = functools.partial(finish, out_ref)
            advance(first, per_chunk, TILE, source, coefs, emit)

    run_steps(strips, TILE, load, (state_a, state_b), coefs, last)


def partners(dom):
    return 0, 1 + dom % 2, 2 - dom % 2, 3


def edge_kernel(
    per_chunk, doms, dom_ref, me_ref, weight_ref, dens_ref, *refs
):
    many, strips = dens_ref.shape[:2]
    dom = dom_ref[0]
    odd = dom % 2 == 1
    diff_ref, drift_ref, state_ref, near_ref, far_ref, *rest = refs
    out_refs, (scratch, slab, state_a, state_b, *coefs) = rest[:-8], rest[-8:]

    def stage(j):
        far, near = far_ref[j], near_ref[j]
        up = jnp.where(dom == 0, 0.0, jnp.where(odd, near, far))
        dn = jnp.where(dom == doms - 1, 0.0, jnp.where(odd, far, near))
        up_mix, dn_mix = up[TILE:], dn[TILE:]
        tiles = (
            (up[:TILE], dens_ref[0, j], dens_ref[many - 1, j], dn[:TILE]),
            (up_mix, diff_ref[0, j], diff_ref[many - 1, j], dn_mix),
            (
                pltpu.roll(up_mix, HALF, 0),
                drift_ref[0, j],
                drift_ref[many - 1, j],
                pltpu.roll(dn_mix, HALF, 0),
            ),
        )
        for k, column in enumerate(tiles):
            for e, tile in enumerate(column):
                slab[k, j, e * TILE : (e + 1) * TILE] = tile

    per_strip(strips, stage, 4)
    slabs = flat(slab)

    def load(j, t):
        return [
            slabs[pl.ds((k * strips + j) * SLAB + t, TILE, stride=HALF), :] for k in range(3)
        ]

    place = lax.broadcasted_iota(jnp.int32, (many, LANES), 0)
    weights = [weight_ref[k] for k in range(4)]

    def finish(out_ref, j, part, new):
        s = [state_ref[j, t] for t in range(TILE)]
        for t in range(HALF):
            s[t] = jnp.where(place == 0, new[t][2:3], s[t])
            s[HALF + t] = jnp.where(place == many - 1, new[t][5:6], s[HALF + t])
        before = new[HALF - 1][1:2]
        weighted = surpluses(s, jnp.where(place == 0, before, roll_rows(s[7], 1)), weights)
        before = weights[3][0:1] * before
        tiles = outer_tiles(many)
        emit_tiles(tiles, per_chunk, scratch, out_ref, j, part, weighted, before)

    def last(source):
        for out_ref, away in zip(out_refs, partners(dom_ref[0])):
            first = (me_ref[0] ^ away) * per_chunk
            emit = functools.partial(finish, out_ref)
            advance(first, per_chunk, HALF, source, coefs, emit)

    run_steps(strips, HALF, load, (state_a, state_b), coefs, last)


def sum_kernel(*refs):
    *parts, out_ref = refs
    total = parts[0][...]
    for part in parts[1:]:
        total = total + part[...]
    out_ref[...] = total


def nodal_kernel(per_chunk, tiles, dom_ref, me_ref, keep_ref, *refs):
    totals, middles, (out_ref, values, sems) = refs[:SQUARE], refs[SQUARE:-3], refs[-3:]
    count = len(tiles)
    fine, mid, low = (keep_ref[k, 0:count] for k in range(3))
    place = lax.broadcasted_iota(jnp.int32, (count, LANES), 0)
    gaps = [k for k in range(1, count) if tiles[k] != tiles[k - 1] + 1]
    copies = []
    for k, (ref, away) in enumerate(zip(totals, partners(dom_ref[0]))):
        first = (me_ref[0] ^ away) * per_chunk
        by_row = flat(values.at[k])

        def body(part, k=k, ref=ref, by_row=by_row):
            w = [
                flat(ref)[spaced(part * count * TILE + t, count, TILE), :] for t in range(TILE)
            ]
            before = ref[per_chunk * count + part // TILE, pl.ds(lax.rem(part, TILE), 1), :]
            prev = jnp.where(place == 0, before, roll_rows(w[7], 1))
            for gap in gaps:
                across = tiles[gap] - tiles[gap - 1] - 1
                before = middles[k][part * across + across - 1, TILE - 1 : TILE, :]
                prev = jnp.where(place == gap, before, prev)
            v3 = 0.5 * (prev + w[7]) + low * w[3]
            v1 = 0.5 * (prev + v3) + mid * w[1]
            v5 = 0.5 * (v3 + w[7]) + mid * w[5]
            rows = (
                0.5 * (prev + v1) + fine * w[0],
                v1,
                0.5 * (v1 + v3) + fine * w[2],
                v3,
                0.5 * (v3 + v5) + fine * w[4],
                v5,
                0.5 * (v5 + w[7]) + fine * w[6],
                w[7],
            )
            for t in range(TILE):
                by_row[spaced(part * TILE + t, count, per_chunk * TILE), :] = rows[t]

        per_strip(per_chunk, body, min(per_chunk, 4))
        for e, m in enumerate(tiles):
            copy = pltpu.make_async_copy(
                values.at[k, e], out_ref.at[m, pl.ds(first, per_chunk)], sems.at[k, e]
            )
            copy.start()
            copies.append(copy)
    for copy in copies:
        copy.wait()


def call(
    kernel, out_shapes, operands, in_smem=0, scratch=(), flops=0, out_space=pltpu.VMEM, onto=None
):
    spaces = [pltpu.SMEM] * in_smem + [pltpu.VMEM] * (len(operands) - in_smem)
    alias = {}
    if onto is not None:
        alias = {len(operands): 0}
        spaces, operands = spaces + [out_space], (*operands, onto)
    specs = [pl.BlockSpec(memory_space=space) for space in spaces]
    moved = 4 * sum(x.size for x in operands)
    return pl.pallas_call(
        kernel,
        out_shape=[jax.ShapeDtypeStruct(shape, jnp.float32) for shape in out_shapes],
        in_specs=specs,
        out_specs=[pl.BlockSpec(memory_space=out_space) for _ in out_shapes],
        input_output_aliases=alias,
        scratch_shapes=list(scratch),
        compiler_params=pltpu.CompilerParams(vmem_limit_bytes=VMEM_LIMIT),
        cost_estimate=pl.CostEstimate(flops=flops, bytes_accessed=moved, transcendentals=0),
    )(*operands)


def on_device(density, diffusion, drift_speed, levels, coefficient):
    rows, cols = density.shape[1:]
    doms, grids = lax.axis_size("dom"), lax.axis_size("grp")
    many, strips = rows // TILE, cols // LANES
    per_chunk = strips // SQUARE
    depth = (rows * doms).bit_length() - 1
    tiles = [tiles_of(x[0]) for x in (density, diffusion, drift_speed)]
    me = (lax.axis_index("grp") % SQUARE).astype(jnp.int32)[None]
    dom = lax.axis_index("dom").astype(jnp.int32)[None]

    def vmem(*shape):
        return pltpu.VMEM(shape, jnp.float32)

    near_pairs = [(d, d ^ 1) for d in range(doms)]
    far_pairs = [(d, min(max((d - 1 ^ 1) + 1, 0), doms - 1)) for d in range(doms)]
    (ones,) = call(ones_kernel, [(many, LANES)], (), flops=LOAD_FLOPS * rows * cols)
    keep, weight = call(
        functools.partial(weights_kernel, depth),
        [(3, many, LANES), (4, many, LANES)],
        (levels, coefficient, ones),
        2,
    )
    near, far = call(
        pack_kernel,
        [(strips, 2 * TILE, LANES)] * 2,
        (dom, weight, *tiles),
        1,
    )
    near = lax.ppermute(near, "dom", near_pairs)
    far = lax.ppermute(far, "dom", far_pairs)
    place = (strips, TILE, many, LANES)
    pieces = (strips, many, TILE, LANES)

    def chunk(tiles):
        return per_chunk * len(tiles) + -(-per_chunk // TILE), TILE, LANES

    middle, outer = middle_tiles(many), outer_tiles(many)
    state, *inside = call(
        functools.partial(inner_kernel, per_chunk),
        [place] + [chunk(middle)] * (SQUARE if middle else 0),
        (dom, me, weight, *tiles),
        2,
        [vmem(*pieces)] + [vmem(strips + 2, *place[1:])] * 2 + [vmem(*place)] * 4,
        flops=40 * rows * cols,
    )
    outside = call(
        functools.partial(edge_kernel, per_chunk, doms),
        [chunk(outer)] * SQUARE,
        (dom, me, weight, *tiles, state, near, far),
        2,
        [vmem(*pieces), vmem(3, strips, SLAB, LANES)]
        + [vmem(strips + 2, HALF, TILE, LANES)] * 2
        + [vmem(strips, HALF, TILE, LANES)] * 4,
        flops=40 * SLAB * cols,
    )

    def swap(array, meet):
        devices = [(g, d) for g in range(grids) for d in range(doms)]
        pairs = [(g * doms + d, (g ^ partners(d % 2)[meet]) * doms + d) for g, d in devices]
        return lax.ppermute(array, ("grp", "dom"), pairs)

    def over_grids(own, *others):
        theirs = [swap(others[meet - 1], meet) for meet in (3, 1, 2)]
        (total,) = call(sum_kernel, [own.shape], (own, *theirs))
        apart = SQUARE
        while apart < grids:
            other = lax.ppermute(total, "grp", [(g, g ^ apart) for g in range(grids)])
            (total,) = call(sum_kernel, [own.shape], (total, other))
            apart *= 2
        return [total] + [swap(total, meet) for meet in range(1, SQUARE)]

    nodal, totals = None, []
    for some, weighted in ((middle, inside), (outer, outside)):
        if not some:
            continue
        totals = over_grids(*weighted) + totals
        (nodal,) = call(
            functools.partial(nodal_kernel, per_chunk, some),
            [(many, strips, TILE, LANES)],
            (dom, me, keep, *totals),
            2,
            [
                vmem(SQUARE, len(some), per_chunk, TILE, LANES),
                pltpu.SemaphoreType.DMA((SQUARE, len(some))),
            ],
            out_space=pl.ANY,
            onto=nodal,
        )
    return block_of(nodal)[None]


def solution(mesh):
    return jax.shard_map(
        on_device,
        mesh=mesh,
        in_specs=(
            P("grp", "dom", None),
            P("grp", "dom", None),
            P("grp", "dom", None),
            P("grp"),
            P("grp"),
        ),
        out_specs=P("grp", "dom", None),
        check_vma=False,
    )
```

```python
import functools

import jax
import jax.numpy as jnp
from jax import lax
from jax.experimental import pallas as pl
from jax.experimental.pallas import tpu as pltpu
from jax.sharding import PartitionSpec as P

STEPS = 4
LANES = 128
TILE = 8
HALF = TILE // 2
SLAB = 4 * TILE
SQUARE = 4
UNROLL = 16
VMEM_LIMIT = 40 * 1024 * 1024
LOAD_FLOPS = 4000


def tiles_of(block):
    rows, cols = block.shape
    return block.reshape(rows // TILE, TILE, cols // LANES, LANES).transpose(0, 2, 1, 3)


def block_of(tiles):
    many, strips = tiles.shape[:2]
    return tiles.transpose(0, 2, 1, 3).reshape(many * TILE, strips * LANES)


def flat(ref):
    return ref.reshape(ref.size // LANES, LANES)


def spaced(first, count, stride):
    return pl.ds(first, count, stride=stride) if count > 1 else pl.ds(first, 1)


def roll_rows(value, shift):
    count = value.shape[0]
    return pltpu.roll(value, shift % count, 0) if count > 1 else value


def per_strip(strips, body, unroll):
    def step(j, carry):
        body(j)
        return carry

    lax.fori_loop(0, strips, step, 0, unroll=unroll)


def advance(first, count, classes, source, coefs, emit):
    shape = source.shape[2:]
    lanes = lax.broadcasted_iota(jnp.int32, shape, 1)
    center, above_c, below_c, side = coefs

    def body(k, carry):
        j = first + k
        cur, right_prev, left_cur = carry
        nxt = [source[j + 2, t] for t in range(classes)]
        left_next = [pltpu.roll(x, LANES - 1, 1) for x in nxt]
        right_cur = [pltpu.roll(x, 1, 1) for x in cur]
        above = cur[1:] + [roll_rows(cur[0], -1)]
        below = [roll_rows(cur[-1], 1)] + cur[:-1]
        new = []
        for t in range(classes):
            left = jnp.where(lanes == 0, right_prev[t], right_cur[t])
            right = jnp.where(lanes == LANES - 1, left_next[t], left_cur[t])
            new.append(
                center[j, t] * cur[t]
                + above_c[j, t] * above[t]
                + below_c[j, t] * below[t]
                + side[j, t] * (left + right)
            )
        emit(j, k, new)
        return nxt, right_cur, left_next

    prev, cur = ([source[first + at, t] for t in range(classes)] for at in range(2))
    ends = [pltpu.roll(x, 1, 1) for x in prev], [pltpu.roll(x, LANES - 1, 1) for x in cur]
    lax.fori_loop(0, count, body, (cur, *ends), unroll=min(count, UNROLL))


def run_steps(strips, classes, load, buffers, coefs, last):
    center, above_c, below_c, side = coefs
    for buf in buffers:
        for edge in (0, strips + 1):
            buf[edge] = jnp.zeros(buf.shape[1:], jnp.float32)

    def begin(j):
        for t in range(classes):
            state, diffuse, drifts = load(j, t)
            half = 0.5 * drifts
            buffers[0][j + 1, t] = state
            center[j, t] = 1.0 - 4.0 * diffuse
            above_c[j, t] = diffuse - half
            below_c[j, t] = diffuse + half
            side[j, t] = diffuse

    per_strip(strips, begin, min(strips, UNROLL))
    for step in range(STEPS - 1):
        source, target = buffers[step % 2], buffers[1 - step % 2]

        def keep(j, _, new, target=target):
            for t in range(classes):
                target[j + 1, t] = new[t]

        advance(0, strips, classes, source, coefs, keep)
    last(buffers[(STEPS - 1) % 2])


def surpluses(s, prev, weights):
    fine, mid, low, coef = weights
    return (
        fine * (s[0] - 0.5 * (prev + s[1])),
        mid * (s[1] - 0.5 * (prev + s[3])),
        fine * (s[2] - 0.5 * (s[1] + s[3])),
        low * (s[3] - 0.5 * (prev + s[7])),
        fine * (s[4] - 0.5 * (s[3] + s[5])),
        mid * (s[5] - 0.5 * (s[3] + s[7])),
        fine * (s[6] - 0.5 * (s[5] + s[7])),
        coef * s[7],
    )


def ones_kernel(out_ref):
    out_ref[...] = jnp.ones(out_ref.shape, jnp.float32)


def weights_kernel(depth, level_ref, coef_ref, ones_ref, keep_ref, weight_ref):
    coef = coef_ref[0].astype(jnp.float32)
    for down in range(3):
        keep_ref[down] = jnp.where(level_ref[0] >= depth - down, ones_ref[...], 0.0)
        weight_ref[down] = coef * keep_ref[down]
    weight_ref[3] = coef * ones_ref[...]


def pack_kernel(dom_ref, weight_ref, dens_ref, diff_ref, drift_ref, near_ref, far_ref):
    del weight_ref
    many, strips = dens_ref.shape[:2]
    odd = dom_ref[0] % 2 == 1
    upper = lax.broadcasted_iota(jnp.int32, (TILE, LANES), 0) < HALF

    def body(j):
        drift_last = pltpu.roll(drift_ref[many - 1, j], HALF, 0)
        mix_next = jnp.where(upper, drift_last, diff_ref[many - 1, j])
        mix_prev = jnp.where(upper, diff_ref[0, j], pltpu.roll(drift_ref[0, j], HALF, 0))
        to_next, to_prev = (dens_ref[many - 1, j], mix_next), (dens_ref[0, j], mix_prev)
        for k in range(2):
            at = pl.ds(k * TILE, TILE)
            far_ref[j, at] = jnp.where(odd, to_next[k], to_prev[k])
            near_ref[j, at] = jnp.where(odd, to_prev[k], to_next[k])

    per_strip(strips, body, 4)


def middle_tiles(many):
    return list(range(many // 4, many - 1)) if many >= 4 else []


def outer_tiles(many):
    return [m for m in range(many) if m not in middle_tiles(many)]


def emit_tiles(tiles, per_chunk, scratch, out_ref, j, part, weighted, before):
    many = scratch.shape[1]
    by_row = flat(scratch)
    for t in range(TILE):
        by_row[spaced(j * many * TILE + t, many, TILE), :] = weighted[t]
    for k, m in enumerate(tiles):
        out_ref[part * len(tiles) + k] = scratch[j, m]
    last = per_chunk * len(tiles) + part // TILE
    out_ref[last, pl.ds(lax.rem(part, TILE), 1), :] = before


def inner_kernel(
    per_chunk, dom_ref, me_ref, weight_ref, dens_ref, diff_ref, drift_ref, state_ref, *refs
):
    many, strips = dens_ref.shape[:2]
    *out_refs, scratch, state_a, state_b = refs[:-4]
    coefs = refs[-4:]
    rows = [flat(ref) for ref in (dens_ref, diff_ref, drift_ref)]
    weights = [weight_ref[k] for k in range(4)]
    tiles = middle_tiles(many)

    def load(j, t):
        at = spaced(j * TILE + t, many, strips * TILE)
        return [ref[at, :] for ref in rows]

    def finish(out_ref, j, part, new):
        for t in range(TILE):
            state_ref[j, t] = new[t]
        if out_ref is not None:
            weighted = surpluses(new, roll_rows(new[7], 1), weights)
            before = weighted[7][tiles[0] - 1 : tiles[0]]
            emit_tiles(tiles, per_chunk, scratch, out_ref, j, part, weighted, before)

    def last(source):
        for out_ref, away in zip(out_refs or [None] * SQUARE, partners(dom_ref[0])):
            first = (me_ref[0] ^ away) * per_chunk
            emit = functools.partial(finish, out_ref)
            advance(first, per_chunk, TILE, source, coefs, emit)

    run_steps(strips, TILE, load, (state_a, state_b), coefs, last)


def partners(dom):
    return 0, 1 + dom % 2, 2 - dom % 2, 3


def edge_kernel(
    per_chunk, doms, dom_ref, me_ref, weight_ref, dens_ref, *refs
):
    many, strips = dens_ref.shape[:2]
    dom = dom_ref[0]
    odd = dom % 2 == 1
    diff_ref, drift_ref, state_ref, near_ref, far_ref, *rest = refs
    out_refs, (scratch, slab, state_a, state_b, *coefs) = rest[:-8], rest[-8:]

    def stage(j):
        far, near = far_ref[j], near_ref[j]
        up = jnp.where(dom == 0, 0.0, jnp.where(odd, near, far))
        dn = jnp.where(dom == doms - 1, 0.0, jnp.where(odd, far, near))
        up_mix, dn_mix = up[TILE:], dn[TILE:]
        tiles = (
            (up[:TILE], dens_ref[0, j], dens_ref[many - 1, j], dn[:TILE]),
            (up_mix, diff_ref[0, j], diff_ref[many - 1, j], dn_mix),
            (
                pltpu.roll(up_mix, HALF, 0),
                drift_ref[0, j],
                drift_ref[many - 1, j],
                pltpu.roll(dn_mix, HALF, 0),
            ),
        )
        for k, column in enumerate(tiles):
            for e, tile in enumerate(column):
                slab[k, j, e * TILE : (e + 1) * TILE] = tile

    per_strip(strips, stage, 4)
    slabs = flat(slab)

    def load(j, t):
        return [
            slabs[pl.ds((k * strips + j) * SLAB + t, TILE, stride=HALF), :] for k in range(3)
        ]

    place = lax.broadcasted_iota(jnp.int32, (many, LANES), 0)
    weights = [weight_ref[k] for k in range(4)]

    def finish(out_ref, j, part, new):
        s = [state_ref[j, t] for t in range(TILE)]
        for t in range(HALF):
            s[t] = jnp.where(place == 0, new[t][2:3], s[t])
            s[HALF + t] = jnp.where(place == many - 1, new[t][5:6], s[HALF + t])
        before = new[HALF - 1][1:2]
        weighted = surpluses(s, jnp.where(place == 0, before, roll_rows(s[7], 1)), weights)
        before = weights[3][0:1] * before
        tiles = outer_tiles(many)
        emit_tiles(tiles, per_chunk, scratch, out_ref, j, part, weighted, before)

    def last(source):
        for out_ref, away in zip(out_refs, partners(dom_ref[0])):
            first = (me_ref[0] ^ away) * per_chunk
            emit = functools.partial(finish, out_ref)
            advance(first, per_chunk, HALF, source, coefs, emit)

    run_steps(strips, HALF, load, (state_a, state_b), coefs, last)


def sum_kernel(*refs):
    *parts, out_ref = refs
    total = parts[0][...]
    for part in parts[1:]:
        total = total + part[...]
    out_ref[...] = total


def nodal_kernel(per_chunk, tiles, dom_ref, me_ref, keep_ref, *refs):
    totals, middles, (out_ref, values, sems) = refs[:SQUARE], refs[SQUARE:-3], refs[-3:]
    count = len(tiles)
    fine, mid, low = (keep_ref[k, 0:count] for k in range(3))
    place = lax.broadcasted_iota(jnp.int32, (count, LANES), 0)
    gaps = [k for k in range(1, count) if tiles[k] != tiles[k - 1] + 1]
    copies = []
    for k, (ref, away) in enumerate(zip(totals, partners(dom_ref[0]))):
        first = (me_ref[0] ^ away) * per_chunk
        by_row = flat(values.at[k])

        def body(part, k=k, ref=ref, by_row=by_row):
            w = [
                flat(ref)[spaced(part * count * TILE + t, count, TILE), :] for t in range(TILE)
            ]
            before = ref[per_chunk * count + part // TILE, pl.ds(lax.rem(part, TILE), 1), :]
            prev = jnp.where(place == 0, before, roll_rows(w[7], 1))
            for gap in gaps:
                across = tiles[gap] - tiles[gap - 1] - 1
                before = middles[k][part * across + across - 1, TILE - 1 : TILE, :]
                prev = jnp.where(place == gap, before, prev)
            v3 = 0.5 * (prev + w[7]) + low * w[3]
            v1 = 0.5 * (prev + v3) + mid * w[1]
            v5 = 0.5 * (v3 + w[7]) + mid * w[5]
            rows = (
                0.5 * (prev + v1) + fine * w[0],
                v1,
                0.5 * (v1 + v3) + fine * w[2],
                v3,
                0.5 * (v3 + v5) + fine * w[4],
                v5,
                0.5 * (v5 + w[7]) + fine * w[6],
                w[7],
            )
            for t in range(TILE):
                by_row[spaced(part * TILE + t, count, per_chunk * TILE), :] = rows[t]

        per_strip(per_chunk, body, min(per_chunk, 4))
        for e, m in enumerate(tiles):
            copy = pltpu.make_async_copy(
                values.at[k, e], out_ref.at[m, pl.ds(first, per_chunk)], sems.at[k, e]
            )
            copy.start()
            copies.append(copy)
    for copy in copies:
        copy.wait()


def call(
    kernel, out_shapes, operands, in_smem=0, scratch=(), flops=0, out_space=pltpu.VMEM, onto=None
):
    spaces = [pltpu.SMEM] * in_smem + [pltpu.VMEM] * (len(operands) - in_smem)
    alias = {}
    if onto is not None:
        alias = {len(operands): 0}
        spaces, operands = spaces + [out_space], (*operands, onto)
    specs = [pl.BlockSpec(memory_space=space) for space in spaces]
    moved = 4 * sum(x.size for x in operands)
    return pl.pallas_call(
        kernel,
        out_shape=[jax.ShapeDtypeStruct(shape, jnp.float32) for shape in out_shapes],
        in_specs=specs,
        out_specs=[pl.BlockSpec(memory_space=out_space) for _ in out_shapes],
        input_output_aliases=alias,
        scratch_shapes=list(scratch),
        compiler_params=pltpu.CompilerParams(vmem_limit_bytes=VMEM_LIMIT),
        cost_estimate=pl.CostEstimate(flops=flops, bytes_accessed=moved, transcendentals=0),
    )(*operands)


def on_device(density, diffusion, drift_speed, levels, coefficient):
    rows, cols = density.shape[1:]
    doms, grids = lax.axis_size("dom"), lax.axis_size("grp")
    many, strips = rows // TILE, cols // LANES
    per_chunk = strips // SQUARE
    depth = (rows * doms).bit_length() - 1
    tiles = [tiles_of(x[0]) for x in (density, diffusion, drift_speed)]
    me = (lax.axis_index("grp") % SQUARE).astype(jnp.int32)[None]
    dom = lax.axis_index("dom").astype(jnp.int32)[None]

    def vmem(*shape):
        return pltpu.VMEM(shape, jnp.float32)

    near_pairs = [(d, d ^ 1) for d in range(doms)]
    far_pairs = [(d, min(max((d - 1 ^ 1) + 1, 0), doms - 1)) for d in range(doms)]
    (ones,) = call(ones_kernel, [(many, LANES)], (), flops=LOAD_FLOPS * rows * cols)
    keep, weight = call(
        functools.partial(weights_kernel, depth),
        [(3, many, LANES), (4, many, LANES)],
        (levels, coefficient, ones),
        2,
    )
    near, far = call(
        pack_kernel,
        [(strips, 2 * TILE, LANES)] * 2,
        (dom, weight, *tiles),
        1,
    )
    near = lax.ppermute(near, "dom", near_pairs)
    far = lax.ppermute(far, "dom", far_pairs)
    place = (strips, TILE, many, LANES)
    pieces = (strips, many, TILE, LANES)

    def chunk(tiles):
        return per_chunk * len(tiles) + -(-per_chunk // TILE), TILE, LANES

    middle, outer = middle_tiles(many), outer_tiles(many)
    state, *inside = call(
        functools.partial(inner_kernel, per_chunk),
        [place] + [chunk(middle)] * (SQUARE if middle else 0),
        (dom, me, weight, *tiles),
        2,
        [vmem(*pieces)] + [vmem(strips + 2, *place[1:])] * 2 + [vmem(*place)] * 4,
        flops=40 * rows * cols,
    )
    outside = call(
        functools.partial(edge_kernel, per_chunk, doms),
        [chunk(outer)] * SQUARE,
        (dom, me, weight, *tiles, state, near, far),
        2,
        [vmem(*pieces), vmem(3, strips, SLAB, LANES)]
        + [vmem(strips + 2, HALF, TILE, LANES)] * 2
        + [vmem(strips, HALF, TILE, LANES)] * 4,
        flops=40 * SLAB * cols,
    )

    def swap(array, meet):
        devices = [(g, d) for g in range(grids) for d in range(doms)]
        pairs = [(g * doms + d, (g ^ partners(d % 2)[meet]) * doms + d) for g, d in devices]
        return lax.ppermute(array, ("grp", "dom"), pairs)

    def over_grids(own, *others):
        theirs = [swap(others[meet - 1], meet) for meet in (3, 1, 2)]
        (total,) = call(sum_kernel, [own.shape], (own, *theirs))
        apart = SQUARE
        while apart < grids:
            other = lax.ppermute(total, "grp", [(g, g ^ apart) for g in range(grids)])
            (total,) = call(sum_kernel, [own.shape], (total, other))
            apart *= 2
        return [total] + [swap(total, meet) for meet in range(1, SQUARE)]

    nodal, totals = None, []
    for some, weighted in ((middle, inside), (outer, outside)):
        if not some:
            continue
        totals = over_grids(*weighted) + totals
        (nodal,) = call(
            functools.partial(nodal_kernel, per_chunk, some),
            [(many, strips, TILE, LANES)],
            (dom, me, keep, *totals),
            2,
            [
                vmem(SQUARE, len(some), per_chunk, TILE, LANES),
                pltpu.SemaphoreType.DMA((SQUARE, len(some))),
            ],
            out_space=pl.ANY,
            onto=nodal,
        )
    return block_of(nodal)[None]


def solution(mesh):
    return jax.shard_map(
        on_device,
        mesh=mesh,
        in_specs=(
            P("grp", "dom", None),
            P("grp", "dom", None),
            P("grp", "dom", None),
            P("grp"),
            P("grp"),
        ),
        out_specs=P("grp", "dom", None),
        check_vma=False,
    )
```

```python
import functools

import jax
import jax.numpy as jnp
from jax import lax
from jax.experimental import pallas as pl
from jax.experimental.pallas import tpu as pltpu
from jax.sharding import PartitionSpec as P

STEPS = 4
LANES = 128
TILE = 8
HALF = TILE // 2
SLAB = 4 * TILE
SQUARE = 4
UNROLL = 16
VMEM_LIMIT = 40 * 1024 * 1024
LOAD_FLOPS = 4000


def tiles_of(block):
    rows, cols = block.shape
    return block.reshape(rows // TILE, TILE, cols // LANES, LANES).transpose(0, 2, 1, 3)


def block_of(tiles):
    many, strips = tiles.shape[:2]
    return tiles.transpose(0, 2, 1, 3).reshape(many * TILE, strips * LANES)


def flat(ref):
    return ref.reshape(ref.size // LANES, LANES)


def spaced(first, count, stride):
    return pl.ds(first, count, stride=stride) if count > 1 else pl.ds(first, 1)


def roll_rows(value, shift):
    count = value.shape[0]
    return pltpu.roll(value, shift % count, 0) if count > 1 else value


def per_strip(strips, body, unroll):
    def step(j, carry):
        body(j)
        return carry

    lax.fori_loop(0, strips, step, 0, unroll=unroll)


def advance(first, count, classes, strip, coefs, emit):
    prev, cur = strip(first - 1), strip(first)
    lanes = lax.broadcasted_iota(jnp.int32, cur[0].shape, 1)

    def body(k, carry):
        j = first + k
        cur, right_prev, left_cur = carry
        nxt = strip(j + 1)
        left_next = [pltpu.roll(x, LANES - 1, 1) for x in nxt]
        right_cur = [pltpu.roll(x, 1, 1) for x in cur]
        above = cur[1:] + [roll_rows(cur[0], -1)]
        below = [roll_rows(cur[-1], 1)] + cur[:-1]
        new = []
        for t in range(classes):
            left = jnp.where(lanes == 0, right_prev[t], right_cur[t])
            right = jnp.where(lanes == LANES - 1, left_next[t], left_cur[t])
            center, above_c, below_c, side = coefs(j, t)
            new.append(
                center * cur[t] + above_c * above[t] + below_c * below[t] + side * (left + right)
            )
        emit(j, k, new)
        return nxt, right_cur, left_next

    ends = [pltpu.roll(x, 1, 1) for x in prev], [pltpu.roll(x, LANES - 1, 1) for x in cur]
    lax.fori_loop(0, count, body, (cur, *ends), unroll=min(count, UNROLL))


def run_steps(strips, classes, load, buffers, coefs, last):
    for buf in buffers:
        for edge in (0, strips + 1):
            buf[edge] = jnp.zeros(buf.shape[1:], jnp.float32)

    def first_strip(j):
        if isinstance(j, int) and j < 0:
            return [jnp.zeros(buffers[0].shape[2:], jnp.float32)] * classes
        inside = jnp.minimum(j, strips - 1)
        return [jnp.where(j < strips, load(0, inside, t), 0.0) for t in range(classes)]

    def first_coefs(j, t):
        diffuse, half = load(1, j, t), 0.5 * load(2, j, t)
        made = 1.0 - 4.0 * diffuse, diffuse - half, diffuse + half, diffuse
        for ref, value in zip(coefs, made):
            ref[j, t] = value
        return made

    def kept_strip(buf):
        return lambda j: [buf[j + 1, t] for t in range(classes)]

    def kept_coefs(j, t):
        return [ref[j, t] for ref in coefs]

    strip, now = first_strip, first_coefs
    for step in range(STEPS - 1):
        target = buffers[step % 2]

        def keep(j, _, new, target=target):
            for t in range(classes):
                target[j + 1, t] = new[t]

        advance(0, strips, classes, strip, now, keep)
        strip, now = kept_strip(target), kept_coefs
    last(strip, now)


def surpluses(s, prev, weights):
    fine, mid, low, coef = weights
    return (
        fine * (s[0] - 0.5 * (prev + s[1])),
        mid * (s[1] - 0.5 * (prev + s[3])),
        fine * (s[2] - 0.5 * (s[1] + s[3])),
        low * (s[3] - 0.5 * (prev + s[7])),
        fine * (s[4] - 0.5 * (s[3] + s[5])),
        mid * (s[5] - 0.5 * (s[3] + s[7])),
        fine * (s[6] - 0.5 * (s[5] + s[7])),
        coef * s[7],
    )


def ones_kernel(out_ref):
    out_ref[...] = jnp.ones(out_ref.shape, jnp.float32)


def weights_kernel(depth, level_ref, coef_ref, ones_ref, keep_ref, weight_ref):
    coef = coef_ref[0].astype(jnp.float32)
    for down in range(3):
        keep_ref[down] = jnp.where(level_ref[0] >= depth - down, ones_ref[...], 0.0)
        weight_ref[down] = coef * keep_ref[down]
    weight_ref[3] = coef * ones_ref[...]


def pack_kernel(dom_ref, weight_ref, dens_ref, diff_ref, drift_ref, near_ref, far_ref):
    del weight_ref
    many, strips = dens_ref.shape[:2]
    odd = dom_ref[0] % 2 == 1
    upper = lax.broadcasted_iota(jnp.int32, (TILE, LANES), 0) < HALF

    def body(j):
        drift_last = pltpu.roll(drift_ref[many - 1, j], HALF, 0)
        mix_next = jnp.where(upper, drift_last, diff_ref[many - 1, j])
        mix_prev = jnp.where(upper, diff_ref[0, j], pltpu.roll(drift_ref[0, j], HALF, 0))
        to_next, to_prev = (dens_ref[many - 1, j], mix_next), (dens_ref[0, j], mix_prev)
        for k in range(2):
            at = pl.ds(k * TILE, TILE)
            far_ref[j, at] = jnp.where(odd, to_next[k], to_prev[k])
            near_ref[j, at] = jnp.where(odd, to_prev[k], to_next[k])

    per_strip(strips, body, 4)


def middle_tiles(many):
    return list(range(many // 4, many - many // 4)) if many >= 4 else []


def outer_tiles(many):
    return [m for m in range(many) if m not in middle_tiles(many)]


def emit_tiles(tiles, per_chunk, scratch, out_ref, j, part, weighted, before):
    many = scratch.shape[1]
    by_row = flat(scratch)
    for t in range(TILE):
        by_row[spaced(j * many * TILE + t, many, TILE), :] = weighted[t]
    for k, m in enumerate(tiles):
        out_ref[part * len(tiles) + k] = scratch[j, m]
    last = per_chunk * len(tiles) + part // TILE
    out_ref[last, pl.ds(lax.rem(part, TILE), 1), :] = before


def inner_kernel(
    per_chunk, dom_ref, me_ref, weight_ref, dens_ref, diff_ref, drift_ref, state_ref, *refs
):
    many, strips = dens_ref.shape[:2]
    *out_refs, scratch, state_a, state_b = refs[:-4]
    coefs = refs[-4:]
    rows = [flat(ref) for ref in (dens_ref, diff_ref, drift_ref)]
    weights = [weight_ref[k] for k in range(4)]
    tiles = middle_tiles(many)

    def load(k, j, t):
        return rows[k][spaced(j * TILE + t, many, strips * TILE), :]

    def finish(out_ref, j, part, new):
        for t in range(TILE):
            state_ref[j, t] = new[t]
        if out_ref is not None:
            weighted = surpluses(new, roll_rows(new[7], 1), weights)
            before = weighted[7][tiles[0] - 1 : tiles[0]]
            emit_tiles(tiles, per_chunk, scratch, out_ref, j, part, weighted, before)

    def last(strip, now):
        for out_ref, away in zip(out_refs or [None] * SQUARE, partners(dom_ref[0])):
            first = (me_ref[0] ^ away) * per_chunk
            emit = functools.partial(finish, out_ref)
            advance(first, per_chunk, TILE, strip, now, emit)

    run_steps(strips, TILE, load, (state_a, state_b), coefs, last)


def partners(dom):
    return 0, 1 + dom % 2, 2 - dom % 2, 3


def edge_kernel(
    per_chunk, doms, dom_ref, me_ref, weight_ref, dens_ref, *refs
):
    many, strips = dens_ref.shape[:2]
    dom = dom_ref[0]
    odd = dom % 2 == 1
    diff_ref, drift_ref, state_ref, near_ref, far_ref, *rest = refs
    out_refs, (scratch, slab, state_a, state_b, *coefs) = rest[:-8], rest[-8:]

    def stage(j):
        far, near = far_ref[j], near_ref[j]
        up = jnp.where(dom == 0, 0.0, jnp.where(odd, near, far))
        dn = jnp.where(dom == doms - 1, 0.0, jnp.where(odd, far, near))
        up_mix, dn_mix = up[TILE:], dn[TILE:]
        tiles = (
            (up[:TILE], dens_ref[0, j], dens_ref[many - 1, j], dn[:TILE]),
            (up_mix, diff_ref[0, j], diff_ref[many - 1, j], dn_mix),
            (
                pltpu.roll(up_mix, HALF, 0),
                drift_ref[0, j],
                drift_ref[many - 1, j],
                pltpu.roll(dn_mix, HALF, 0),
            ),
        )
        for k, column in enumerate(tiles):
            for e, tile in enumerate(column):
                slab[k, j, e * TILE : (e + 1) * TILE] = tile

    per_strip(strips, stage, 4)
    slabs = flat(slab)

    def load(k, j, t):
        return slabs[pl.ds((k * strips + j) * SLAB + t, TILE, stride=HALF), :]

    place = lax.broadcasted_iota(jnp.int32, (many, LANES), 0)
    weights = [weight_ref[k] for k in range(4)]

    def finish(out_ref, j, part, new):
        s = [state_ref[j, t] for t in range(TILE)]
        for t in range(HALF):
            s[t] = jnp.where(place == 0, new[t][2:3], s[t])
            s[HALF + t] = jnp.where(place == many - 1, new[t][5:6], s[HALF + t])
        before = new[HALF - 1][1:2]
        weighted = surpluses(s, jnp.where(place == 0, before, roll_rows(s[7], 1)), weights)
        before = weights[3][0:1] * before
        tiles = outer_tiles(many)
        emit_tiles(tiles, per_chunk, scratch, out_ref, j, part, weighted, before)

    def last(strip, now):
        for out_ref, away in zip(out_refs, partners(dom_ref[0])):
            first = (me_ref[0] ^ away) * per_chunk
            emit = functools.partial(finish, out_ref)
            advance(first, per_chunk, HALF, strip, now, emit)

    run_steps(strips, HALF, load, (state_a, state_b), coefs, last)


def sum_kernel(*refs):
    *parts, out_ref = refs
    total = parts[0][...]
    for part in parts[1:]:
        total = total + part[...]
    out_ref[...] = total


def nodal_kernel(per_chunk, tiles, dom_ref, me_ref, keep_ref, *refs):
    totals, middles, (out_ref, values, sems) = refs[:SQUARE], refs[SQUARE:-3], refs[-3:]
    count = len(tiles)
    fine, mid, low = (keep_ref[k, 0:count] for k in range(3))
    place = lax.broadcasted_iota(jnp.int32, (count, LANES), 0)
    gaps = [k for k in range(1, count) if tiles[k] != tiles[k - 1] + 1]
    copies = []
    for k, (ref, away) in enumerate(zip(totals, partners(dom_ref[0]))):
        first = (me_ref[0] ^ away) * per_chunk
        by_row = flat(values.at[k])

        def body(part, k=k, ref=ref, by_row=by_row):
            w = [
                flat(ref)[spaced(part * count * TILE + t, count, TILE), :] for t in range(TILE)
            ]
            before = ref[per_chunk * count + part // TILE, pl.ds(lax.rem(part, TILE), 1), :]
            prev = jnp.where(place == 0, before, roll_rows(w[7], 1))
            for gap in gaps:
                across = tiles[gap] - tiles[gap - 1] - 1
                before = middles[k][part * across + across - 1, TILE - 1 : TILE, :]
                prev = jnp.where(place == gap, before, prev)
            v3 = 0.5 * (prev + w[7]) + low * w[3]
            v1 = 0.5 * (prev + v3) + mid * w[1]
            v5 = 0.5 * (v3 + w[7]) + mid * w[5]
            rows = (
                0.5 * (prev + v1) + fine * w[0],
                v1,
                0.5 * (v1 + v3) + fine * w[2],
                v3,
                0.5 * (v3 + v5) + fine * w[4],
                v5,
                0.5 * (v5 + w[7]) + fine * w[6],
                w[7],
            )
            for t in range(TILE):
                by_row[spaced(part * TILE + t, count, per_chunk * TILE), :] = rows[t]

        per_strip(per_chunk, body, min(per_chunk, 4))
        for e, m in enumerate(tiles):
            copy = pltpu.make_async_copy(
                values.at[k, e], out_ref.at[m, pl.ds(first, per_chunk)], sems.at[k, e]
            )
            copy.start()
            copies.append(copy)
    for copy in copies:
        copy.wait()


def call(
    kernel, out_shapes, operands, in_smem=0, scratch=(), flops=0, out_space=pltpu.VMEM, onto=None
):
    spaces = [pltpu.SMEM] * in_smem + [pltpu.VMEM] * (len(operands) - in_smem)
    alias = {}
    if onto is not None:
        alias = {len(operands): 0}
        spaces, operands = spaces + [out_space], (*operands, onto)
    specs = [pl.BlockSpec(memory_space=space) for space in spaces]
    moved = 4 * sum(x.size for x in operands)
    return pl.pallas_call(
        kernel,
        out_shape=[jax.ShapeDtypeStruct(shape, jnp.float32) for shape in out_shapes],
        in_specs=specs,
        out_specs=[pl.BlockSpec(memory_space=out_space) for _ in out_shapes],
        input_output_aliases=alias,
        scratch_shapes=list(scratch),
        compiler_params=pltpu.CompilerParams(vmem_limit_bytes=VMEM_LIMIT),
        cost_estimate=pl.CostEstimate(flops=flops, bytes_accessed=moved, transcendentals=0),
    )(*operands)


def on_device(density, diffusion, drift_speed, levels, coefficient):
    rows, cols = density.shape[1:]
    doms, grids = lax.axis_size("dom"), lax.axis_size("grp")
    many, strips = rows // TILE, cols // LANES
    per_chunk = strips // SQUARE
    depth = (rows * doms).bit_length() - 1
    tiles = [tiles_of(x[0]) for x in (density, diffusion, drift_speed)]
    me = (lax.axis_index("grp") % SQUARE).astype(jnp.int32)[None]
    dom = lax.axis_index("dom").astype(jnp.int32)[None]

    def vmem(*shape):
        return pltpu.VMEM(shape, jnp.float32)

    near_pairs = [(d, d ^ 1) for d in range(doms)]
    far_pairs = [(d, min(max((d - 1 ^ 1) + 1, 0), doms - 1)) for d in range(doms)]
    (ones,) = call(ones_kernel, [(many, LANES)], (), flops=LOAD_FLOPS * rows * cols)
    keep, weight = call(
        functools.partial(weights_kernel, depth),
        [(3, many, LANES), (4, many, LANES)],
        (levels, coefficient, ones),
        2,
    )
    near, far = call(
        pack_kernel,
        [(strips, 2 * TILE, LANES)] * 2,
        (dom, weight, *tiles),
        1,
    )
    near = lax.ppermute(near, "dom", near_pairs)
    far = lax.ppermute(far, "dom", far_pairs)
    place = (strips, TILE, many, LANES)
    pieces = (strips, many, TILE, LANES)

    def chunk(tiles):
        return per_chunk * len(tiles) + -(-per_chunk // TILE), TILE, LANES

    middle, outer = middle_tiles(many), outer_tiles(many)
    state, *inside = call(
        functools.partial(inner_kernel, per_chunk),
        [place] + [chunk(middle)] * (SQUARE if middle else 0),
        (dom, me, weight, *tiles),
        2,
        [vmem(*pieces)] + [vmem(strips + 2, *place[1:])] * 2 + [vmem(*place)] * 4,
        flops=40 * rows * cols,
    )
    outside = call(
        functools.partial(edge_kernel, per_chunk, doms),
        [chunk(outer)] * SQUARE,
        (dom, me, weight, *tiles, state, near, far),
        2,
        [vmem(*pieces), vmem(3, strips, SLAB, LANES)]
        + [vmem(strips + 2, HALF, TILE, LANES)] * 2
        + [vmem(strips, HALF, TILE, LANES)] * 4,
        flops=40 * SLAB * cols,
    )

    def swap(array, meet):
        devices = [(g, d) for g in range(grids) for d in range(doms)]
        pairs = [(g * doms + d, (g ^ partners(d % 2)[meet]) * doms + d) for g, d in devices]
        return lax.ppermute(array, ("grp", "dom"), pairs)

    def over_grids(own, *others):
        theirs = [swap(others[meet - 1], meet) for meet in (3, 1, 2)]
        (total,) = call(sum_kernel, [own.shape], (own, *theirs))
        apart = SQUARE
        while apart < grids:
            other = lax.ppermute(total, "grp", [(g, g ^ apart) for g in range(grids)])
            (total,) = call(sum_kernel, [own.shape], (total, other))
            apart *= 2
        return [total] + [swap(total, meet) for meet in range(1, SQUARE)]

    nodal, totals = None, []
    for some, weighted in ((middle, inside), (outer, outside)):
        if not some:
            continue
        totals = over_grids(*weighted) + totals
        (nodal,) = call(
            functools.partial(nodal_kernel, per_chunk, some),
            [(many, strips, TILE, LANES)],
            (dom, me, keep, *totals),
            2,
            [
                vmem(SQUARE, len(some), per_chunk, TILE, LANES),
                pltpu.SemaphoreType.DMA((SQUARE, len(some))),
            ],
            out_space=pl.ANY,
            onto=nodal,
        )
    return block_of(nodal)[None]


def solution(mesh):
    return jax.shard_map(
        on_device,
        mesh=mesh,
        in_specs=(
            P("grp", "dom", None),
            P("grp", "dom", None),
            P("grp", "dom", None),
            P("grp"),
            P("grp"),
        ),
        out_specs=P("grp", "dom", None),
        check_vma=False,
    )
```

```python
import functools

import jax
import jax.numpy as jnp
from jax import lax
from jax.experimental import pallas as pl
from jax.experimental.pallas import tpu as pltpu
from jax.sharding import PartitionSpec as P

STEPS = 4
LANES = 128
TILE = 8
HALF = TILE // 2
SLAB = 4 * TILE
SQUARE = 4
UNROLL = 16
VMEM_LIMIT = 40 * 1024 * 1024
LOAD_FLOPS = 4000


def tiles_of(block):
    rows, cols = block.shape
    return block.reshape(rows // TILE, TILE, cols // LANES, LANES).transpose(0, 2, 1, 3)


def block_of(tiles):
    many, strips = tiles.shape[:2]
    return tiles.transpose(0, 2, 1, 3).reshape(many * TILE, strips * LANES)


def flat(ref):
    return ref.reshape(ref.size // LANES, LANES)


def spaced(first, count, stride):
    return pl.ds(first, count, stride=stride) if count > 1 else pl.ds(first, 1)


def roll_rows(value, shift):
    count = value.shape[0]
    return pltpu.roll(value, shift % count, 0) if count > 1 else value


def per_strip(strips, body, unroll):
    def step(j, carry):
        body(j)
        return carry

    lax.fori_loop(0, strips, step, 0, unroll=unroll)


def advance(first, count, classes, strip, coefs, emit):
    prev, cur = strip(first - 1), strip(first)
    lanes = lax.broadcasted_iota(jnp.int32, cur[0].shape, 1)

    def body(k, carry):
        j = first + k
        cur, right_prev, left_cur = carry
        nxt = strip(j + 1)
        left_next = [pltpu.roll(x, LANES - 1, 1) for x in nxt]
        right_cur = [pltpu.roll(x, 1, 1) for x in cur]
        above = cur[1:] + [roll_rows(cur[0], -1)]
        below = [roll_rows(cur[-1], 1)] + cur[:-1]
        new = []
        for t in range(classes):
            left = jnp.where(lanes == 0, right_prev[t], right_cur[t])
            right = jnp.where(lanes == LANES - 1, left_next[t], left_cur[t])
            center, above_c, below_c, side = coefs(j, t)
            new.append(
                center * cur[t] + above_c * above[t] + below_c * below[t] + side * (left + right)
            )
        emit(j, k, new)
        return nxt, right_cur, left_next

    ends = [pltpu.roll(x, 1, 1) for x in prev], [pltpu.roll(x, LANES - 1, 1) for x in cur]
    lax.fori_loop(0, count, body, (cur, *ends), unroll=min(count, UNROLL))


def run_steps(strips, classes, load, buffers, coefs, last):
    for buf in buffers:
        for edge in (0, strips + 1):
            buf[edge] = jnp.zeros(buf.shape[1:], jnp.float32)

    def first_strip(j):
        if isinstance(j, int) and j < 0:
            return [jnp.zeros(buffers[0].shape[2:], jnp.float32)] * classes
        inside = jnp.minimum(j, strips - 1)
        return [jnp.where(j < strips, load(0, inside, t), 0.0) for t in range(classes)]

    def first_coefs(j, t):
        diffuse, half = load(1, j, t), 0.5 * load(2, j, t)
        made = 1.0 - 4.0 * diffuse, diffuse - half, diffuse + half, diffuse
        for ref, value in zip(coefs, made):
            ref[j, t] = value
        return made

    def kept_strip(buf):
        return lambda j: [buf[j + 1, t] for t in range(classes)]

    def kept_coefs(j, t):
        return [ref[j, t] for ref in coefs]

    strip, now = first_strip, first_coefs
    for step in range(STEPS - 1):
        target = buffers[step % 2]

        def keep(j, _, new, target=target):
            for t in range(classes):
                target[j + 1, t] = new[t]

        advance(0, strips, classes, strip, now, keep)
        strip, now = kept_strip(target), kept_coefs
    last(strip, now)


def surpluses(s, prev, weights):
    fine, mid, low, coef = weights
    return (
        fine * (s[0] - 0.5 * (prev + s[1])),
        mid * (s[1] - 0.5 * (prev + s[3])),
        fine * (s[2] - 0.5 * (s[1] + s[3])),
        low * (s[3] - 0.5 * (prev + s[7])),
        fine * (s[4] - 0.5 * (s[3] + s[5])),
        mid * (s[5] - 0.5 * (s[3] + s[7])),
        fine * (s[6] - 0.5 * (s[5] + s[7])),
        coef * s[7],
    )


def ones_kernel(out_ref):
    out_ref[...] = jnp.ones(out_ref.shape, jnp.float32)


def weights_kernel(depth, level_ref, coef_ref, ones_ref, keep_ref, weight_ref):
    coef = coef_ref[0].astype(jnp.float32)
    for down in range(3):
        keep_ref[down] = jnp.where(level_ref[0] >= depth - down, ones_ref[...], 0.0)
        weight_ref[down] = coef * keep_ref[down]
    weight_ref[3] = coef * ones_ref[...]


def pack_kernel(dom_ref, weight_ref, dens_ref, diff_ref, drift_ref, near_ref, far_ref):
    del weight_ref
    many, strips = dens_ref.shape[:2]
    odd = dom_ref[0] % 2 == 1
    upper = lax.broadcasted_iota(jnp.int32, (TILE, LANES), 0) < HALF

    def body(j):
        drift_last = pltpu.roll(drift_ref[many - 1, j], HALF, 0)
        mix_next = jnp.where(upper, drift_last, diff_ref[many - 1, j])
        mix_prev = jnp.where(upper, diff_ref[0, j], pltpu.roll(drift_ref[0, j], HALF, 0))
        to_next, to_prev = (dens_ref[many - 1, j], mix_next), (dens_ref[0, j], mix_prev)
        for k in range(2):
            at = pl.ds(k * TILE, TILE)
            far_ref[j, at] = jnp.where(odd, to_next[k], to_prev[k])
            near_ref[j, at] = jnp.where(odd, to_prev[k], to_next[k])

    per_strip(strips, body, 4)


def middle_tiles(many):
    return list(range(many // 4, many - many // 4)) if many >= 4 else []


def outer_tiles(many):
    return [m for m in range(many) if m not in middle_tiles(many)]


def emit_tiles(tiles, per_chunk, scratch, out_ref, j, part, weighted, before):
    many = scratch.shape[1]
    by_row = flat(scratch)
    for t in range(TILE):
        by_row[spaced(j * many * TILE + t, many, TILE), :] = weighted[t]
    for k, m in enumerate(tiles):
        out_ref[part * len(tiles) + k] = scratch[j, m]
    last = per_chunk * len(tiles) + part // TILE
    out_ref[last, pl.ds(lax.rem(part, TILE), 1), :] = before


def inner_kernel(
    per_chunk, dom_ref, me_ref, weight_ref, dens_ref, diff_ref, drift_ref, state_ref, *refs
):
    many, strips = dens_ref.shape[:2]
    *out_refs, scratch, state_a, state_b = refs[:-4]
    coefs = refs[-4:]
    rows = [flat(ref) for ref in (dens_ref, diff_ref, drift_ref)]
    weights = [weight_ref[k] for k in range(4)]
    tiles = middle_tiles(many)

    def load(k, j, t):
        return rows[k][spaced(j * TILE + t, many, strips * TILE), :]

    def finish(out_ref, j, part, new):
        for t in range(TILE):
            state_ref[j, t] = new[t]
        if out_ref is not None:
            weighted = surpluses(new, roll_rows(new[7], 1), weights)
            before = weighted[7][tiles[0] - 1 : tiles[0]]
            emit_tiles(tiles, per_chunk, scratch, out_ref, j, part, weighted, before)

    def last(strip, now):
        for out_ref, away in zip(out_refs or [None] * SQUARE, partners(dom_ref[0])):
            first = (me_ref[0] ^ away) * per_chunk
            emit = functools.partial(finish, out_ref)
            advance(first, per_chunk, TILE, strip, now, emit)

    run_steps(strips, TILE, load, (state_a, state_b), coefs, last)


def partners(dom):
    return 0, 1 + dom % 2, 2 - dom % 2, 3


def edge_kernel(
    per_chunk, doms, dom_ref, me_ref, weight_ref, dens_ref, *refs
):
    many, strips = dens_ref.shape[:2]
    dom = dom_ref[0]
    odd = dom % 2 == 1
    diff_ref, drift_ref, state_ref, near_ref, far_ref, *rest = refs
    out_refs, (scratch, slab, state_a, state_b, *coefs) = rest[:-8], rest[-8:]

    def stage(j):
        far, near = far_ref[j], near_ref[j]
        up = jnp.where(dom == 0, 0.0, jnp.where(odd, near, far))
        dn = jnp.where(dom == doms - 1, 0.0, jnp.where(odd, far, near))
        up_mix, dn_mix = up[TILE:], dn[TILE:]
        tiles = (
            (up[:TILE], dens_ref[0, j], dens_ref[many - 1, j], dn[:TILE]),
            (up_mix, diff_ref[0, j], diff_ref[many - 1, j], dn_mix),
            (
                pltpu.roll(up_mix, HALF, 0),
                drift_ref[0, j],
                drift_ref[many - 1, j],
                pltpu.roll(dn_mix, HALF, 0),
            ),
        )
        for k, column in enumerate(tiles):
            for e, tile in enumerate(column):
                slab[k, j, e * TILE : (e + 1) * TILE] = tile

    per_strip(strips, stage, 4)
    slabs = flat(slab)

    def load(k, j, t):
        return slabs[pl.ds((k * strips + j) * SLAB + t, TILE, stride=HALF), :]

    place = lax.broadcasted_iota(jnp.int32, (many, LANES), 0)
    weights = [weight_ref[k] for k in range(4)]

    def finish(out_ref, j, part, new):
        s = [state_ref[j, t] for t in range(TILE)]
        for t in range(HALF):
            s[t] = jnp.where(place == 0, new[t][2:3], s[t])
            s[HALF + t] = jnp.where(place == many - 1, new[t][5:6], s[HALF + t])
        before = new[HALF - 1][1:2]
        weighted = surpluses(s, jnp.where(place == 0, before, roll_rows(s[7], 1)), weights)
        before = weights[3][0:1] * before
        tiles = outer_tiles(many)
        emit_tiles(tiles, per_chunk, scratch, out_ref, j, part, weighted, before)

    def last(strip, now):
        for out_ref, away in zip(out_refs, partners(dom_ref[0])):
            first = (me_ref[0] ^ away) * per_chunk
            emit = functools.partial(finish, out_ref)
            advance(first, per_chunk, HALF, strip, now, emit)

    run_steps(strips, HALF, load, (state_a, state_b), coefs, last)


def sum_kernel(*refs):
    *parts, out_ref = refs
    total = parts[0][...]
    for part in parts[1:]:
        total = total + part[...]
    out_ref[...] = total


def nodal_kernel(per_chunk, tiles, dom_ref, me_ref, keep_ref, *refs):
    totals, middles, (out_ref, values, sems) = refs[:SQUARE], refs[SQUARE:-3], refs[-3:]
    count = len(tiles)
    fine, mid, low = (keep_ref[k, 0:count] for k in range(3))
    place = lax.broadcasted_iota(jnp.int32, (count, LANES), 0)
    gaps = [k for k in range(1, count) if tiles[k] != tiles[k - 1] + 1]
    starts = [0, *gaps]
    runs = [end - start for start, end in zip(starts, [*gaps, count])]
    copies = []
    for k, (ref, away) in enumerate(zip(totals, partners(dom_ref[0]))):
        first = (me_ref[0] ^ away) * per_chunk
        by_row = flat(values.at[k])

        def body(part, k=k, ref=ref, by_row=by_row):
            w = [
                flat(ref)[spaced(part * count * TILE + t, count, TILE), :] for t in range(TILE)
            ]
            before = ref[per_chunk * count + part // TILE, pl.ds(lax.rem(part, TILE), 1), :]
            prev = jnp.where(place == 0, before, roll_rows(w[7], 1))
            for gap in gaps:
                across = tiles[gap] - tiles[gap - 1] - 1
                before = middles[k][part * across + across - 1, TILE - 1 : TILE, :]
                prev = jnp.where(place == gap, before, prev)
            v3 = 0.5 * (prev + w[7]) + low * w[3]
            v1 = 0.5 * (prev + v3) + mid * w[1]
            v5 = 0.5 * (v3 + w[7]) + mid * w[5]
            rows = (
                0.5 * (prev + v1) + fine * w[0],
                v1,
                0.5 * (v1 + v3) + fine * w[2],
                v3,
                0.5 * (v3 + v5) + fine * w[4],
                v5,
                0.5 * (v5 + w[7]) + fine * w[6],
                w[7],
            )
            for t in range(TILE):
                by_row[spaced(part * TILE + t, count, per_chunk * TILE), :] = rows[t]

        per_strip(per_chunk, body, min(per_chunk, 4))
        for e, run in zip(starts, runs):
            copy = pltpu.make_async_copy(
                values.at[k, pl.ds(e, run)],
                out_ref.at[pl.ds(tiles[e], run), pl.ds(first, per_chunk)],
                sems.at[k, e],
            )
            copy.start()
            copies.append(copy)
    for copy in copies:
        copy.wait()


def call(
    kernel, out_shapes, operands, in_smem=0, scratch=(), flops=0, out_space=pltpu.VMEM, onto=None
):
    spaces = [pltpu.SMEM] * in_smem + [pltpu.VMEM] * (len(operands) - in_smem)
    alias = {}
    if onto is not None:
        alias = {len(operands): 0}
        spaces, operands = spaces + [out_space], (*operands, onto)
    specs = [pl.BlockSpec(memory_space=space) for space in spaces]
    moved = 4 * sum(x.size for x in operands)
    return pl.pallas_call(
        kernel,
        out_shape=[jax.ShapeDtypeStruct(shape, jnp.float32) for shape in out_shapes],
        in_specs=specs,
        out_specs=[pl.BlockSpec(memory_space=out_space) for _ in out_shapes],
        input_output_aliases=alias,
        scratch_shapes=list(scratch),
        compiler_params=pltpu.CompilerParams(vmem_limit_bytes=VMEM_LIMIT),
        cost_estimate=pl.CostEstimate(flops=flops, bytes_accessed=moved, transcendentals=0),
    )(*operands)


def on_device(density, diffusion, drift_speed, levels, coefficient):
    rows, cols = density.shape[1:]
    doms, grids = lax.axis_size("dom"), lax.axis_size("grp")
    many, strips = rows // TILE, cols // LANES
    per_chunk = strips // SQUARE
    depth = (rows * doms).bit_length() - 1
    tiles = [tiles_of(x[0]) for x in (density, diffusion, drift_speed)]
    me = (lax.axis_index("grp") % SQUARE).astype(jnp.int32)[None]
    dom = lax.axis_index("dom").astype(jnp.int32)[None]

    def vmem(*shape):
        return pltpu.VMEM(shape, jnp.float32)

    near_pairs = [(d, d ^ 1) for d in range(doms)]
    far_pairs = [(d, min(max((d - 1 ^ 1) + 1, 0), doms - 1)) for d in range(doms)]
    (ones,) = call(ones_kernel, [(many, LANES)], (), flops=LOAD_FLOPS * rows * cols)
    keep, weight = call(
        functools.partial(weights_kernel, depth),
        [(3, many, LANES), (4, many, LANES)],
        (levels, coefficient, ones),
        2,
    )
    near, far = call(
        pack_kernel,
        [(strips, 2 * TILE, LANES)] * 2,
        (dom, weight, *tiles),
        1,
    )
    near = lax.ppermute(near, "dom", near_pairs)
    far = lax.ppermute(far, "dom", far_pairs)
    place = (strips, TILE, many, LANES)
    pieces = (strips, many, TILE, LANES)

    def chunk(tiles):
        return per_chunk * len(tiles) + -(-per_chunk // TILE), TILE, LANES

    middle, outer = middle_tiles(many), outer_tiles(many)
    state, *inside = call(
        functools.partial(inner_kernel, per_chunk),
        [place] + [chunk(middle)] * (SQUARE if middle else 0),
        (dom, me, weight, *tiles),
        2,
        [vmem(*pieces)] + [vmem(strips + 2, *place[1:])] * 2 + [vmem(*place)] * 4,
        flops=40 * rows * cols,
    )
    outside = call(
        functools.partial(edge_kernel, per_chunk, doms),
        [chunk(outer)] * SQUARE,
        (dom, me, weight, *tiles, state, near, far),
        2,
        [vmem(*pieces), vmem(3, strips, SLAB, LANES)]
        + [vmem(strips + 2, HALF, TILE, LANES)] * 2
        + [vmem(strips, HALF, TILE, LANES)] * 4,
        flops=40 * SLAB * cols,
    )

    def swap(array, meet):
        devices = [(g, d) for g in range(grids) for d in range(doms)]
        pairs = [(g * doms + d, (g ^ partners(d % 2)[meet]) * doms + d) for g, d in devices]
        return lax.ppermute(array, ("grp", "dom"), pairs)

    def over_grids(own, *others):
        theirs = [swap(others[meet - 1], meet) for meet in (3, 1, 2)]
        (total,) = call(sum_kernel, [own.shape], (own, *theirs))
        apart = SQUARE
        while apart < grids:
            other = lax.ppermute(total, "grp", [(g, g ^ apart) for g in range(grids)])
            (total,) = call(sum_kernel, [own.shape], (total, other))
            apart *= 2
        return [total] + [swap(total, meet) for meet in range(1, SQUARE)]

    nodal, totals = None, []
    for some, weighted in ((middle, inside), (outer, outside)):
        if not some:
            continue
        totals = over_grids(*weighted) + totals
        (nodal,) = call(
            functools.partial(nodal_kernel, per_chunk, some),
            [(many, strips, TILE, LANES)],
            (dom, me, keep, *totals),
            2,
            [
                vmem(SQUARE, len(some), per_chunk, TILE, LANES),
                pltpu.SemaphoreType.DMA((SQUARE, len(some))),
            ],
            out_space=pl.ANY,
            onto=nodal,
        )
    return block_of(nodal)[None]


def solution(mesh):
    return jax.shard_map(
        on_device,
        mesh=mesh,
        in_specs=(
            P("grp", "dom", None),
            P("grp", "dom", None),
            P("grp", "dom", None),
            P("grp"),
            P("grp"),
        ),
        out_specs=P("grp", "dom", None),
        check_vma=False,
    )
```

```python
import functools

import jax
import jax.numpy as jnp
from jax import lax
from jax.experimental import pallas as pl
from jax.experimental.pallas import tpu as pltpu
from jax.sharding import PartitionSpec as P

STEPS = 4
LANES = 128
TILE = 8
HALF = TILE // 2
SLAB = 4 * TILE
SQUARE = 4
UNROLL = 16
VMEM_LIMIT = 40 * 1024 * 1024
LOAD_FLOPS = 4000


def tiles_of(block):
    rows, cols = block.shape
    return block.reshape(rows // TILE, TILE, cols // LANES, LANES).transpose(0, 2, 1, 3)


def block_of(tiles):
    many, strips = tiles.shape[:2]
    return tiles.transpose(0, 2, 1, 3).reshape(many * TILE, strips * LANES)


def flat(ref):
    return ref.reshape(ref.size // LANES, LANES)


def spaced(first, count, stride):
    return pl.ds(first, count, stride=stride) if count > 1 else pl.ds(first, 1)


def roll_rows(value, shift):
    count = value.shape[0]
    return pltpu.roll(value, shift % count, 0) if count > 1 else value


def per_strip(strips, body, unroll):
    def step(j, carry):
        body(j)
        return carry

    lax.fori_loop(0, strips, step, 0, unroll=unroll)


def advance(first, count, classes, strip, coefs, emit):
    prev, cur = strip(first - 1), strip(first)
    lanes = lax.broadcasted_iota(jnp.int32, cur[0].shape, 1)

    def body(k, carry):
        j = first + k
        cur, right_prev, left_cur = carry
        nxt = strip(j + 1)
        left_next = [pltpu.roll(x, LANES - 1, 1) for x in nxt]
        right_cur = [pltpu.roll(x, 1, 1) for x in cur]
        above = cur[1:] + [roll_rows(cur[0], -1)]
        below = [roll_rows(cur[-1], 1)] + cur[:-1]
        new = []
        for t in range(classes):
            left = jnp.where(lanes == 0, right_prev[t], right_cur[t])
            right = jnp.where(lanes == LANES - 1, left_next[t], left_cur[t])
            center, above_c, below_c, side = coefs(j, t)
            new.append(
                center * cur[t] + above_c * above[t] + below_c * below[t] + side * (left + right)
            )
        emit(j, k, new)
        return nxt, right_cur, left_next

    ends = [pltpu.roll(x, 1, 1) for x in prev], [pltpu.roll(x, LANES - 1, 1) for x in cur]
    lax.fori_loop(0, count, body, (cur, *ends), unroll=min(count, UNROLL))


def run_steps(strips, classes, load, buffers, coefs, last):
    for buf in buffers:
        for edge in (0, strips + 1):
            buf[edge] = jnp.zeros(buf.shape[1:], jnp.float32)

    def first_strip(j):
        if isinstance(j, int) and j < 0:
            return [jnp.zeros(buffers[0].shape[2:], jnp.float32)] * classes
        inside = jnp.minimum(j, strips - 1)
        return [jnp.where(j < strips, load(0, inside, t), 0.0) for t in range(classes)]

    def first_coefs(j, t):
        diffuse, half = load(1, j, t), 0.5 * load(2, j, t)
        made = 1.0 - 4.0 * diffuse, diffuse - half, diffuse + half, diffuse
        for ref, value in zip(coefs, made):
            ref[j, t] = value
        return made

    def kept_strip(buf):
        return lambda j: [buf[j + 1, t] for t in range(classes)]

    def kept_coefs(j, t):
        return [ref[j, t] for ref in coefs]

    strip, now = first_strip, first_coefs
    for step in range(STEPS - 1):
        target = buffers[step % 2]

        def keep(j, _, new, target=target):
            for t in range(classes):
                target[j + 1, t] = new[t]

        advance(0, strips, classes, strip, now, keep)
        strip, now = kept_strip(target), kept_coefs
    last(strip, now)


def surpluses(s, prev, weights):
    fine, mid, low, coef = weights
    return (
        fine * (s[0] - 0.5 * (prev + s[1])),
        mid * (s[1] - 0.5 * (prev + s[3])),
        fine * (s[2] - 0.5 * (s[1] + s[3])),
        low * (s[3] - 0.5 * (prev + s[7])),
        fine * (s[4] - 0.5 * (s[3] + s[5])),
        mid * (s[5] - 0.5 * (s[3] + s[7])),
        fine * (s[6] - 0.5 * (s[5] + s[7])),
        coef * s[7],
    )


def ones_kernel(out_ref):
    out_ref[...] = jnp.ones(out_ref.shape, jnp.float32)


def weights_kernel(depth, level_ref, coef_ref, ones_ref, keep_ref, weight_ref):
    coef = coef_ref[0].astype(jnp.float32)
    for down in range(3):
        keep_ref[down] = jnp.where(level_ref[0] >= depth - down, ones_ref[...], 0.0)
        weight_ref[down] = coef * keep_ref[down]
    weight_ref[3] = coef * ones_ref[...]


def pack_kernel(dom_ref, weight_ref, dens_ref, diff_ref, drift_ref, near_ref, far_ref):
    del weight_ref
    many, strips = dens_ref.shape[:2]
    odd = dom_ref[0] % 2 == 1
    upper = lax.broadcasted_iota(jnp.int32, (TILE, LANES), 0) < HALF

    def body(j):
        drift_last = pltpu.roll(drift_ref[many - 1, j], HALF, 0)
        mix_next = jnp.where(upper, drift_last, diff_ref[many - 1, j])
        mix_prev = jnp.where(upper, diff_ref[0, j], pltpu.roll(drift_ref[0, j], HALF, 0))
        to_next, to_prev = (dens_ref[many - 1, j], mix_next), (dens_ref[0, j], mix_prev)
        for k in range(2):
            at = pl.ds(k * TILE, TILE)
            far_ref[j, at] = jnp.where(odd, to_next[k], to_prev[k])
            near_ref[j, at] = jnp.where(odd, to_prev[k], to_next[k])

    per_strip(strips, body, 4)


def middle_tiles(many):
    return list(range(many // 4, many - many // 4)) if many >= 4 else []


def outer_tiles(many):
    return [m for m in range(many) if m not in middle_tiles(many)]


def emit_tiles(tiles, per_chunk, scratch, out_ref, j, part, weighted, before):
    many = scratch.shape[1]
    by_row = flat(scratch)
    for t in range(TILE):
        by_row[spaced(j * many * TILE + t, many, TILE), :] = weighted[t]
    for k, m in enumerate(tiles):
        out_ref[part * len(tiles) + k] = scratch[j, m]
    last = per_chunk * len(tiles) + part // TILE
    out_ref[last, pl.ds(lax.rem(part, TILE), 1), :] = before


def inner_kernel(
    per_chunk, dom_ref, me_ref, weight_ref, dens_ref, diff_ref, drift_ref, state_ref, *refs
):
    many, strips = dens_ref.shape[:2]
    *out_refs, scratch, state_a, state_b = refs[:-4]
    coefs = refs[-4:]
    rows = [flat(ref) for ref in (dens_ref, diff_ref, drift_ref)]
    weights = [weight_ref[k] for k in range(4)]
    tiles = middle_tiles(many)

    def load(k, j, t):
        return rows[k][spaced(j * TILE + t, many, strips * TILE), :]

    def finish(out_ref, j, part, new):
        for t in range(TILE):
            state_ref[j, t] = new[t]
        if out_ref is not None:
            weighted = surpluses(new, roll_rows(new[7], 1), weights)
            before = weighted[7][tiles[0] - 1 : tiles[0]]
            emit_tiles(tiles, per_chunk, scratch, out_ref, j, part, weighted, before)

    def last(strip, now):
        for out_ref, away in zip(out_refs or [None] * SQUARE, partners(dom_ref[0])):
            first = (me_ref[0] ^ away) * per_chunk
            emit = functools.partial(finish, out_ref)
            advance(first, per_chunk, TILE, strip, now, emit)

    run_steps(strips, TILE, load, (state_a, state_b), coefs, last)


def partners(dom):
    return 0, 1 + dom % 2, 2 - dom % 2, 3


def edge_kernel(
    per_chunk, doms, dom_ref, me_ref, weight_ref, dens_ref, *refs
):
    many, strips = dens_ref.shape[:2]
    dom = dom_ref[0]
    odd = dom % 2 == 1
    diff_ref, drift_ref, state_ref, near_ref, far_ref, *rest = refs
    out_refs, (scratch, slab, state_a, state_b, *coefs) = rest[:-8], rest[-8:]

    def stage(j):
        far, near = far_ref[j], near_ref[j]
        up = jnp.where(dom == 0, 0.0, jnp.where(odd, near, far))
        dn = jnp.where(dom == doms - 1, 0.0, jnp.where(odd, far, near))
        up_mix, dn_mix = up[TILE:], dn[TILE:]
        tiles = (
            (up[:TILE], dens_ref[0, j], dens_ref[many - 1, j], dn[:TILE]),
            (up_mix, diff_ref[0, j], diff_ref[many - 1, j], dn_mix),
            (
                pltpu.roll(up_mix, HALF, 0),
                drift_ref[0, j],
                drift_ref[many - 1, j],
                pltpu.roll(dn_mix, HALF, 0),
            ),
        )
        for k, column in enumerate(tiles):
            for e, tile in enumerate(column):
                slab[k, j, e * TILE : (e + 1) * TILE] = tile

    per_strip(strips, stage, 4)
    slabs = flat(slab)

    def load(k, j, t):
        return slabs[pl.ds((k * strips + j) * SLAB + t, TILE, stride=HALF), :]

    place = lax.broadcasted_iota(jnp.int32, (many, LANES), 0)
    weights = [weight_ref[k] for k in range(4)]

    def finish(out_ref, j, part, new):
        s = [state_ref[j, t] for t in range(TILE)]
        for t in range(HALF):
            s[t] = jnp.where(place == 0, new[t][2:3], s[t])
            s[HALF + t] = jnp.where(place == many - 1, new[t][5:6], s[HALF + t])
        before = new[HALF - 1][1:2]
        weighted = surpluses(s, jnp.where(place == 0, before, roll_rows(s[7], 1)), weights)
        before = weights[3][0:1] * before
        tiles = outer_tiles(many)
        emit_tiles(tiles, per_chunk, scratch, out_ref, j, part, weighted, before)

    def last(strip, now):
        for out_ref, away in zip(out_refs, partners(dom_ref[0])):
            first = (me_ref[0] ^ away) * per_chunk
            emit = functools.partial(finish, out_ref)
            advance(first, per_chunk, HALF, strip, now, emit)

    run_steps(strips, HALF, load, (state_a, state_b), coefs, last)


def sum_kernel(*refs):
    *parts, out_ref = refs
    total = parts[0][...]
    for part in parts[1:]:
        total = total + part[...]
    out_ref[...] = total


def nodal_kernel(per_chunk, tiles, dom_ref, me_ref, keep_ref, *refs):
    out_ref, values, sems = refs[-3:]
    own, second, first, diagonal = refs[:SQUARE]
    totals = own, first, second, diagonal
    count = len(tiles)
    fine, mid, low = (keep_ref[k, 0:count] for k in range(3))
    place = lax.broadcasted_iota(jnp.int32, (count, LANES), 0)
    gaps = [k for k in range(1, count) if tiles[k] != tiles[k - 1] + 1]
    copies = []
    for k, (ref, away) in enumerate(zip(totals, partners(dom_ref[0]))):
        first = (me_ref[0] ^ away) * per_chunk
        by_row = flat(values.at[k])

        def body(part, k=k, ref=ref, by_row=by_row):
            w = [
                flat(ref)[spaced(part * count * TILE + t, count, TILE), :] for t in range(TILE)
            ]
            before = ref[per_chunk * count + part // TILE, pl.ds(lax.rem(part, TILE), 1), :]
            prev = jnp.where(place == 0, before, roll_rows(w[7], 1))
            for gap in gaps:
                across = tiles[gap] - tiles[gap - 1] - 1
                middle_ref = refs[SQUARE + (0, 2, 1, 3)[k]]
                before = middle_ref[part * across + across - 1, TILE - 1 : TILE, :]
                prev = jnp.where(place == gap, before, prev)
            v3 = 0.5 * (prev + w[7]) + low * w[3]
            v1 = 0.5 * (prev + v3) + mid * w[1]
            v5 = 0.5 * (v3 + w[7]) + mid * w[5]
            rows = (
                0.5 * (prev + v1) + fine * w[0],
                v1,
                0.5 * (v1 + v3) + fine * w[2],
                v3,
                0.5 * (v3 + v5) + fine * w[4],
                v5,
                0.5 * (v5 + w[7]) + fine * w[6],
                w[7],
            )
            for t in range(TILE):
                by_row[spaced(part * TILE + t, count, per_chunk * TILE), :] = rows[t]

        per_strip(per_chunk, body, min(per_chunk, 4))
        for e, m in enumerate(tiles):
            copy = pltpu.make_async_copy(
                values.at[k, e], out_ref.at[m, pl.ds(first, per_chunk)], sems.at[k, e]
            )
            copy.start()
            copies.append(copy)
    for copy in copies:
        copy.wait()


def call(
    kernel, out_shapes, operands, in_smem=0, scratch=(), flops=0, out_space=pltpu.VMEM, onto=None
):
    spaces = [pltpu.SMEM] * in_smem + [pltpu.VMEM] * (len(operands) - in_smem)
    alias = {}
    if onto is not None:
        alias = {len(operands): 0}
        spaces, operands = spaces + [out_space], (*operands, onto)
    specs = [pl.BlockSpec(memory_space=space) for space in spaces]
    moved = 4 * sum(x.size for x in operands)
    return pl.pallas_call(
        kernel,
        out_shape=[jax.ShapeDtypeStruct(shape, jnp.float32) for shape in out_shapes],
        in_specs=specs,
        out_specs=[pl.BlockSpec(memory_space=out_space) for _ in out_shapes],
        input_output_aliases=alias,
        scratch_shapes=list(scratch),
        compiler_params=pltpu.CompilerParams(vmem_limit_bytes=VMEM_LIMIT),
        cost_estimate=pl.CostEstimate(flops=flops, bytes_accessed=moved, transcendentals=0),
    )(*operands)


def on_device(density, diffusion, drift_speed, levels, coefficient):
    rows, cols = density.shape[1:]
    doms, grids = lax.axis_size("dom"), lax.axis_size("grp")
    many, strips = rows // TILE, cols // LANES
    per_chunk = strips // SQUARE
    depth = (rows * doms).bit_length() - 1
    tiles = [tiles_of(x[0]) for x in (density, diffusion, drift_speed)]
    me = (lax.axis_index("grp") % SQUARE).astype(jnp.int32)[None]
    dom = lax.axis_index("dom").astype(jnp.int32)[None]

    def vmem(*shape):
        return pltpu.VMEM(shape, jnp.float32)

    near_pairs = [(d, d ^ 1) for d in range(doms)]
    far_pairs = [(d, min(max((d - 1 ^ 1) + 1, 0), doms - 1)) for d in range(doms)]
    (ones,) = call(ones_kernel, [(many, LANES)], (), flops=LOAD_FLOPS * rows * cols)
    keep, weight = call(
        functools.partial(weights_kernel, depth),
        [(3, many, LANES), (4, many, LANES)],
        (levels, coefficient, ones),
        2,
    )
    near, far = call(
        pack_kernel,
        [(strips, 2 * TILE, LANES)] * 2,
        (dom, weight, *tiles),
        1,
    )
    near = lax.ppermute(near, "dom", near_pairs)
    far = lax.ppermute(far, "dom", far_pairs)
    place = (strips, TILE, many, LANES)
    pieces = (strips, many, TILE, LANES)

    def chunk(tiles):
        return per_chunk * len(tiles) + -(-per_chunk // TILE), TILE, LANES

    middle, outer = middle_tiles(many), outer_tiles(many)
    state, *inside = call(
        functools.partial(inner_kernel, per_chunk),
        [place] + [chunk(middle)] * (SQUARE if middle else 0),
        (dom, me, weight, *tiles),
        2,
        [vmem(*pieces)] + [vmem(strips + 2, *place[1:])] * 2 + [vmem(*place)] * 4,
        flops=40 * rows * cols,
    )
    outside = call(
        functools.partial(edge_kernel, per_chunk, doms),
        [chunk(outer)] * SQUARE,
        (dom, me, weight, *tiles, state, near, far),
        2,
        [vmem(*pieces), vmem(3, strips, SLAB, LANES)]
        + [vmem(strips + 2, HALF, TILE, LANES)] * 2
        + [vmem(strips, HALF, TILE, LANES)] * 4,
        flops=40 * SLAB * cols,
    )

    def swap(array, meet):
        devices = [(g, d) for g in range(grids) for d in range(doms)]
        pairs = [(g * doms + d, (g ^ partners(d % 2)[meet]) * doms + d) for g, d in devices]
        return lax.ppermute(array, ("grp", "dom"), pairs)

    def over_grids(own, *others):
        theirs = [swap(others[meet - 1], meet) for meet in (3, 1, 2)]
        (total,) = call(sum_kernel, [own.shape], (own, *theirs))
        apart = SQUARE
        while apart < grids:
            other = lax.ppermute(total, "grp", [(g, g ^ apart) for g in range(grids)])
            (total,) = call(sum_kernel, [own.shape], (total, other))
            apart *= 2
        return [total] + [swap(total, meet) for meet in (2, 1, 3)]

    nodal, totals = None, []
    for some, weighted in ((middle, inside), (outer, outside)):
        if not some:
            continue
        totals = over_grids(*weighted) + totals
        (nodal,) = call(
            functools.partial(nodal_kernel, per_chunk, some),
            [(many, strips, TILE, LANES)],
            (dom, me, keep, *totals),
            2,
            [
                vmem(SQUARE, len(some), per_chunk, TILE, LANES),
                pltpu.SemaphoreType.DMA((SQUARE, len(some))),
            ],
            out_space=pl.ANY,
            onto=nodal,
        )
    return block_of(nodal)[None]


def solution(mesh):
    return jax.shard_map(
        on_device,
        mesh=mesh,
        in_specs=(
            P("grp", "dom", None),
            P("grp", "dom", None),
            P("grp", "dom", None),
            P("grp"),
            P("grp"),
        ),
        out_specs=P("grp", "dom", None),
        check_vma=False,
    )
```

```python
import functools

import jax
import jax.numpy as jnp
from jax import lax
from jax.experimental import pallas as pl
from jax.experimental.pallas import tpu as pltpu
from jax.sharding import PartitionSpec as P

STEPS = 4
LANES = 128
TILE = 8
HALF = TILE // 2
SLAB = 4 * TILE
SQUARE = 4
UNROLL = 16
VMEM_LIMIT = 40 * 1024 * 1024
LOAD_FLOPS = 4000


def tiles_of(block):
    rows, cols = block.shape
    return block.reshape(rows // TILE, TILE, cols // LANES, LANES).transpose(0, 2, 1, 3)


def block_of(tiles):
    many, strips = tiles.shape[:2]
    return tiles.transpose(0, 2, 1, 3).reshape(many * TILE, strips * LANES)


def flat(ref):
    return ref.reshape(ref.size // LANES, LANES)


def spaced(first, count, stride):
    return pl.ds(first, count, stride=stride) if count > 1 else pl.ds(first, 1)


def roll_rows(value, shift):
    count = value.shape[0]
    return pltpu.roll(value, shift % count, 0) if count > 1 else value


def per_strip(strips, body, unroll):
    def step(j, carry):
        body(j)
        return carry

    lax.fori_loop(0, strips, step, 0, unroll=unroll)


def advance(first, count, classes, strip, coefs, emit):
    prev, cur = strip(first - 1), strip(first)
    lanes = lax.broadcasted_iota(jnp.int32, cur[0].shape, 1)

    def body(k, carry):
        j = first + k
        cur, right_prev, left_cur = carry
        nxt = strip(j + 1)
        left_next = [pltpu.roll(x, LANES - 1, 1) for x in nxt]
        right_cur = [pltpu.roll(x, 1, 1) for x in cur]
        above = cur[1:] + [roll_rows(cur[0], -1)]
        below = [roll_rows(cur[-1], 1)] + cur[:-1]
        new = []
        for t in range(classes):
            left = jnp.where(lanes == 0, right_prev[t], right_cur[t])
            right = jnp.where(lanes == LANES - 1, left_next[t], left_cur[t])
            center, above_c, below_c, side = coefs(j, t)
            new.append(
                center * cur[t] + above_c * above[t] + below_c * below[t] + side * (left + right)
            )
        emit(j, k, new)
        return nxt, right_cur, left_next

    ends = [pltpu.roll(x, 1, 1) for x in prev], [pltpu.roll(x, LANES - 1, 1) for x in cur]
    lax.fori_loop(0, count, body, (cur, *ends), unroll=min(count, UNROLL))


def run_steps(strips, classes, load, buffers, coefs, last):
    for buf in buffers:
        for edge in (0, strips + 1):
            buf[edge] = jnp.zeros(buf.shape[1:], jnp.float32)

    def first_strip(j):
        if isinstance(j, int) and j < 0:
            return [jnp.zeros(buffers[0].shape[2:], jnp.float32)] * classes
        inside = jnp.minimum(j, strips - 1)
        return [jnp.where(j < strips, load(0, inside, t), 0.0) for t in range(classes)]

    def first_coefs(j, t):
        diffuse, half = load(1, j, t), 0.5 * load(2, j, t)
        made = 1.0 - 4.0 * diffuse, diffuse - half, diffuse + half, diffuse
        for ref, value in zip(coefs, made):
            ref[j, t] = value
        return made

    def kept_strip(buf):
        return lambda j: [buf[j + 1, t] for t in range(classes)]

    def kept_coefs(j, t):
        return [ref[j, t] for ref in coefs]

    strip, now = first_strip, first_coefs
    for step in range(STEPS - 1):
        target = buffers[step % 2]

        def keep(j, _, new, target=target):
            for t in range(classes):
                target[j + 1, t] = new[t]

        advance(0, strips, classes, strip, now, keep)
        strip, now = kept_strip(target), kept_coefs
    last(strip, now)


def surpluses(s, prev, weights):
    fine, mid, low, coef = weights
    return (
        fine * (s[0] - 0.5 * (prev + s[1])),
        mid * (s[1] - 0.5 * (prev + s[3])),
        fine * (s[2] - 0.5 * (s[1] + s[3])),
        low * (s[3] - 0.5 * (prev + s[7])),
        fine * (s[4] - 0.5 * (s[3] + s[5])),
        mid * (s[5] - 0.5 * (s[3] + s[7])),
        fine * (s[6] - 0.5 * (s[5] + s[7])),
        coef * s[7],
    )


def ones_kernel(out_ref):
    out_ref[...] = jnp.ones(out_ref.shape, jnp.float32)


def weights_kernel(depth, level_ref, coef_ref, ones_ref, keep_ref, weight_ref):
    coef = coef_ref[0].astype(jnp.float32)
    for down in range(3):
        keep_ref[down] = jnp.where(level_ref[0] >= depth - down, ones_ref[...], 0.0)
        weight_ref[down] = coef * keep_ref[down]
    weight_ref[3] = coef * ones_ref[...]


def pack_kernel(dom_ref, weight_ref, dens_ref, diff_ref, drift_ref, near_ref, far_ref):
    del weight_ref
    many, strips = dens_ref.shape[:2]
    odd = dom_ref[0] % 2 == 1
    upper = lax.broadcasted_iota(jnp.int32, (TILE, LANES), 0) < HALF

    def body(j):
        drift_last = pltpu.roll(drift_ref[many - 1, j], HALF, 0)
        mix_next = jnp.where(upper, drift_last, diff_ref[many - 1, j])
        mix_prev = jnp.where(upper, diff_ref[0, j], pltpu.roll(drift_ref[0, j], HALF, 0))
        to_next, to_prev = (dens_ref[many - 1, j], mix_next), (dens_ref[0, j], mix_prev)
        for k in range(2):
            at = pl.ds(k * TILE, TILE)
            far_ref[j, at] = jnp.where(odd, to_next[k], to_prev[k])
            near_ref[j, at] = jnp.where(odd, to_prev[k], to_next[k])

    per_strip(strips, body, 4)


def middle_tiles(many):
    return list(range(many // 4, many - many // 4)) if many >= 4 else []


def outer_tiles(many):
    return [m for m in range(many) if m not in middle_tiles(many)]


def emit_tiles(tiles, per_chunk, scratch, out_ref, j, part, weighted, before):
    many = scratch.shape[1]
    by_row = flat(scratch)
    for t in range(TILE):
        by_row[spaced(j * many * TILE + t, many, TILE), :] = weighted[t]
    for k, m in enumerate(tiles):
        out_ref[part * len(tiles) + k] = scratch[j, m]
    last = per_chunk * len(tiles) + part // TILE
    out_ref[last, pl.ds(lax.rem(part, TILE), 1), :] = before


def inner_kernel(
    per_chunk, dom_ref, me_ref, weight_ref, dens_ref, diff_ref, drift_ref, state_ref, *refs
):
    many, strips = dens_ref.shape[:2]
    *out_refs, scratch, state_a, state_b = refs[:-4]
    coefs = refs[-4:]
    rows = [flat(ref) for ref in (dens_ref, diff_ref, drift_ref)]
    weights = [weight_ref[k] for k in range(4)]
    tiles = middle_tiles(many)

    def load(k, j, t):
        return rows[k][spaced(j * TILE + t, many, strips * TILE), :]

    def finish(out_ref, j, part, new):
        for t in range(TILE):
            state_ref[j, t] = new[t]
        if out_ref is not None:
            weighted = surpluses(new, roll_rows(new[7], 1), weights)
            before = weighted[7][tiles[0] - 1 : tiles[0]]
            emit_tiles(tiles, per_chunk, scratch, out_ref, j, part, weighted, before)

    def last(strip, now):
        for out_ref, away in zip(out_refs or [None] * SQUARE, partners(dom_ref[0])):
            first = (me_ref[0] ^ away) * per_chunk
            emit = functools.partial(finish, out_ref)
            advance(first, per_chunk, TILE, strip, now, emit)

    run_steps(strips, TILE, load, (state_a, state_b), coefs, last)


def partners(dom):
    return 0, 2 - dom % 2, 1 + dom % 2, 3


def edge_kernel(
    per_chunk, doms, dom_ref, me_ref, weight_ref, dens_ref, *refs
):
    many, strips = dens_ref.shape[:2]
    dom = dom_ref[0]
    odd = dom % 2 == 1
    diff_ref, drift_ref, state_ref, near_ref, far_ref, *rest = refs
    out_refs, (scratch, slab, state_a, state_b, *coefs) = rest[:-8], rest[-8:]

    def stage(j):
        far, near = far_ref[j], near_ref[j]
        up = jnp.where(dom == 0, 0.0, jnp.where(odd, near, far))
        dn = jnp.where(dom == doms - 1, 0.0, jnp.where(odd, far, near))
        up_mix, dn_mix = up[TILE:], dn[TILE:]
        tiles = (
            (up[:TILE], dens_ref[0, j], dens_ref[many - 1, j], dn[:TILE]),
            (up_mix, diff_ref[0, j], diff_ref[many - 1, j], dn_mix),
            (
                pltpu.roll(up_mix, HALF, 0),
                drift_ref[0, j],
                drift_ref[many - 1, j],
                pltpu.roll(dn_mix, HALF, 0),
            ),
        )
        for k, column in enumerate(tiles):
            for e, tile in enumerate(column):
                slab[k, j, e * TILE : (e + 1) * TILE] = tile

    per_strip(strips, stage, 4)
    slabs = flat(slab)

    def load(k, j, t):
        return slabs[pl.ds((k * strips + j) * SLAB + t, TILE, stride=HALF), :]

    place = lax.broadcasted_iota(jnp.int32, (many, LANES), 0)
    weights = [weight_ref[k] for k in range(4)]

    def finish(out_ref, j, part, new):
        s = [state_ref[j, t] for t in range(TILE)]
        for t in range(HALF):
            s[t] = jnp.where(place == 0, new[t][2:3], s[t])
            s[HALF + t] = jnp.where(place == many - 1, new[t][5:6], s[HALF + t])
        before = new[HALF - 1][1:2]
        weighted = surpluses(s, jnp.where(place == 0, before, roll_rows(s[7], 1)), weights)
        before = weights[3][0:1] * before
        tiles = outer_tiles(many)
        emit_tiles(tiles, per_chunk, scratch, out_ref, j, part, weighted, before)

    def last(strip, now):
        for out_ref, away in zip(out_refs, partners(dom_ref[0])):
            first = (me_ref[0] ^ away) * per_chunk
            emit = functools.partial(finish, out_ref)
            advance(first, per_chunk, HALF, strip, now, emit)

    run_steps(strips, HALF, load, (state_a, state_b), coefs, last)


def sum_kernel(*refs):
    *parts, out_ref = refs
    total = parts[0][...]
    for part in parts[1:]:
        total = total + part[...]
    out_ref[...] = total


def nodal_kernel(per_chunk, tiles, dom_ref, me_ref, keep_ref, *refs):
    totals, middles, (out_ref, values, sems) = refs[:SQUARE], refs[SQUARE:-3], refs[-3:]
    count = len(tiles)
    fine, mid, low = (keep_ref[k, 0:count] for k in range(3))
    place = lax.broadcasted_iota(jnp.int32, (count, LANES), 0)
    gaps = [k for k in range(1, count) if tiles[k] != tiles[k - 1] + 1]
    copies = []
    for k, (ref, away) in enumerate(zip(totals, partners(dom_ref[0]))):
        first = (me_ref[0] ^ away) * per_chunk
        by_row = flat(values.at[k])

        def body(part, k=k, ref=ref, by_row=by_row):
            w = [
                flat(ref)[spaced(part * count * TILE + t, count, TILE), :] for t in range(TILE)
            ]
            before = ref[per_chunk * count + part // TILE, pl.ds(lax.rem(part, TILE), 1), :]
            prev = jnp.where(place == 0, before, roll_rows(w[7], 1))
            for gap in gaps:
                across = tiles[gap] - tiles[gap - 1] - 1
                before = middles[k][part * across + across - 1, TILE - 1 : TILE, :]
                prev = jnp.where(place == gap, before, prev)
            v3 = 0.5 * (prev + w[7]) + low * w[3]
            v1 = 0.5 * (prev + v3) + mid * w[1]
            v5 = 0.5 * (v3 + w[7]) + mid * w[5]
            rows = (
                0.5 * (prev + v1) + fine * w[0],
                v1,
                0.5 * (v1 + v3) + fine * w[2],
                v3,
                0.5 * (v3 + v5) + fine * w[4],
                v5,
                0.5 * (v5 + w[7]) + fine * w[6],
                w[7],
            )
            for t in range(TILE):
                by_row[spaced(part * TILE + t, count, per_chunk * TILE), :] = rows[t]

        per_strip(per_chunk, body, min(per_chunk, 4))
        for e, m in enumerate(tiles):
            copy = pltpu.make_async_copy(
                values.at[k, e], out_ref.at[m, pl.ds(first, per_chunk)], sems.at[k, e]
            )
            copy.start()
            copies.append(copy)
    for copy in copies:
        copy.wait()


def call(
    kernel, out_shapes, operands, in_smem=0, scratch=(), flops=0, out_space=pltpu.VMEM, onto=None
):
    spaces = [pltpu.SMEM] * in_smem + [pltpu.VMEM] * (len(operands) - in_smem)
    alias = {}
    if onto is not None:
        alias = {len(operands): 0}
        spaces, operands = spaces + [out_space], (*operands, onto)
    specs = [pl.BlockSpec(memory_space=space) for space in spaces]
    moved = 4 * sum(x.size for x in operands)
    return pl.pallas_call(
        kernel,
        out_shape=[jax.ShapeDtypeStruct(shape, jnp.float32) for shape in out_shapes],
        in_specs=specs,
        out_specs=[pl.BlockSpec(memory_space=out_space) for _ in out_shapes],
        input_output_aliases=alias,
        scratch_shapes=list(scratch),
        compiler_params=pltpu.CompilerParams(vmem_limit_bytes=VMEM_LIMIT),
        cost_estimate=pl.CostEstimate(flops=flops, bytes_accessed=moved, transcendentals=0),
    )(*operands)


def on_device(density, diffusion, drift_speed, levels, coefficient):
    rows, cols = density.shape[1:]
    doms, grids = lax.axis_size("dom"), lax.axis_size("grp")
    many, strips = rows // TILE, cols // LANES
    per_chunk = strips // SQUARE
    depth = (rows * doms).bit_length() - 1
    tiles = [tiles_of(x[0]) for x in (density, diffusion, drift_speed)]
    me = (lax.axis_index("grp") % SQUARE).astype(jnp.int32)[None]
    dom = lax.axis_index("dom").astype(jnp.int32)[None]

    def vmem(*shape):
        return pltpu.VMEM(shape, jnp.float32)

    near_pairs = [(d, d ^ 1) for d in range(doms)]
    far_pairs = [(d, min(max((d - 1 ^ 1) + 1, 0), doms - 1)) for d in range(doms)]
    (ones,) = call(ones_kernel, [(many, LANES)], (), flops=LOAD_FLOPS * rows * cols)
    keep, weight = call(
        functools.partial(weights_kernel, depth),
        [(3, many, LANES), (4, many, LANES)],
        (levels, coefficient, ones),
        2,
    )
    near, far = call(
        pack_kernel,
        [(strips, 2 * TILE, LANES)] * 2,
        (dom, weight, *tiles),
        1,
    )
    near = lax.ppermute(near, "dom", near_pairs)
    far = lax.ppermute(far, "dom", far_pairs)
    place = (strips, TILE, many, LANES)
    pieces = (strips, many, TILE, LANES)

    def chunk(tiles):
        return per_chunk * len(tiles) + -(-per_chunk // TILE), TILE, LANES

    middle, outer = middle_tiles(many), outer_tiles(many)
    state, *inside = call(
        functools.partial(inner_kernel, per_chunk),
        [place] + [chunk(middle)] * (SQUARE if middle else 0),
        (dom, me, weight, *tiles),
        2,
        [vmem(*pieces)] + [vmem(strips + 2, *place[1:])] * 2 + [vmem(*place)] * 4,
        flops=40 * rows * cols,
    )
    outside = call(
        functools.partial(edge_kernel, per_chunk, doms),
        [chunk(outer)] * SQUARE,
        (dom, me, weight, *tiles, state, near, far),
        2,
        [vmem(*pieces), vmem(3, strips, SLAB, LANES)]
        + [vmem(strips + 2, HALF, TILE, LANES)] * 2
        + [vmem(strips, HALF, TILE, LANES)] * 4,
        flops=40 * SLAB * cols,
    )

    def swap(array, meet):
        devices = [(g, d) for g in range(grids) for d in range(doms)]
        pairs = [(g * doms + d, (g ^ partners(d % 2)[meet]) * doms + d) for g, d in devices]
        return lax.ppermute(array, ("grp", "dom"), pairs)

    def over_grids(own, *others):
        theirs = [swap(others[meet - 1], meet) for meet in (3, 1, 2)]
        (total,) = call(sum_kernel, [own.shape], (own, *theirs))
        apart = SQUARE
        while apart < grids:
            other = lax.ppermute(total, "grp", [(g, g ^ apart) for g in range(grids)])
            (total,) = call(sum_kernel, [own.shape], (total, other))
            apart *= 2
        return [total] + [swap(total, meet) for meet in range(1, SQUARE)]

    nodal, totals = None, []
    for some, weighted in ((middle, inside), (outer, outside)):
        if not some:
            continue
        totals = over_grids(*weighted) + totals
        (nodal,) = call(
            functools.partial(nodal_kernel, per_chunk, some),
            [(many, strips, TILE, LANES)],
            (dom, me, keep, *totals),
            2,
            [
                vmem(SQUARE, len(some), per_chunk, TILE, LANES),
                pltpu.SemaphoreType.DMA((SQUARE, len(some))),
            ],
            out_space=pl.ANY,
            onto=nodal,
        )
    return block_of(nodal)[None]


def solution(mesh):
    return jax.shard_map(
        on_device,
        mesh=mesh,
        in_specs=(
            P("grp", "dom", None),
            P("grp", "dom", None),
            P("grp", "dom", None),
            P("grp"),
            P("grp"),
        ),
        out_specs=P("grp", "dom", None),
        check_vma=False,
    )
```

```python
import functools

import jax
import jax.numpy as jnp
from jax import lax
from jax.experimental import pallas as pl
from jax.experimental.pallas import tpu as pltpu
from jax.sharding import PartitionSpec as P

STEPS = 4
LANES = 128
TILE = 8
HALF = TILE // 2
SLAB = 4 * TILE
SQUARE = 4
UNROLL = 16
VMEM_LIMIT = 40 * 1024 * 1024
LOAD_FLOPS = 4000


def tiles_of(block):
    rows, cols = block.shape
    return block.reshape(rows // TILE, TILE, cols // LANES, LANES).transpose(0, 2, 1, 3)


def block_of(tiles):
    many, strips = tiles.shape[:2]
    return tiles.transpose(0, 2, 1, 3).reshape(many * TILE, strips * LANES)


def flat(ref):
    return ref.reshape(ref.size // LANES, LANES)


def spaced(first, count, stride):
    return pl.ds(first, count, stride=stride) if count > 1 else pl.ds(first, 1)


def roll_rows(value, shift):
    count = value.shape[0]
    return pltpu.roll(value, shift % count, 0) if count > 1 else value


def per_strip(strips, body, unroll):
    def step(j, carry):
        body(j)
        return carry

    lax.fori_loop(0, strips, step, 0, unroll=unroll)


def advance(first, count, classes, strip, coefs, emit):
    prev, cur = strip(first - 1), strip(first)
    lanes = lax.broadcasted_iota(jnp.int32, cur[0].shape, 1)

    def body(k, carry):
        j = first + k
        cur, right_prev, left_cur = carry
        nxt = strip(j + 1)
        left_next = [pltpu.roll(x, LANES - 1, 1) for x in nxt]
        right_cur = [pltpu.roll(x, 1, 1) for x in cur]
        above = cur[1:] + [roll_rows(cur[0], -1)]
        below = [roll_rows(cur[-1], 1)] + cur[:-1]
        new = []
        for t in range(classes):
            left = jnp.where(lanes == 0, right_prev[t], right_cur[t])
            right = jnp.where(lanes == LANES - 1, left_next[t], left_cur[t])
            center, above_c, below_c, side = coefs(j, t)
            new.append(
                center * cur[t] + above_c * above[t] + below_c * below[t] + side * (left + right)
            )
        emit(j, k, new)
        return nxt, right_cur, left_next

    ends = [pltpu.roll(x, 1, 1) for x in prev], [pltpu.roll(x, LANES - 1, 1) for x in cur]
    lax.fori_loop(0, count, body, (cur, *ends), unroll=min(count, UNROLL))


def run_steps(strips, classes, load, buffers, coefs, last):
    for buf in buffers:
        for edge in (0, strips + 1):
            buf[edge] = jnp.zeros(buf.shape[1:], jnp.float32)

    def first_strip(j):
        if isinstance(j, int) and j < 0:
            return [jnp.zeros(buffers[0].shape[2:], jnp.float32)] * classes
        inside = jnp.minimum(j, strips - 1)
        return [jnp.where(j < strips, load(0, inside, t), 0.0) for t in range(classes)]

    def first_coefs(j, t):
        diffuse, half = load(1, j, t), 0.5 * load(2, j, t)
        made = 1.0 - 4.0 * diffuse, diffuse - half, diffuse + half, diffuse
        for ref, value in zip(coefs, made):
            ref[j, t] = value
        return made

    def kept_strip(buf):
        return lambda j: [buf[j + 1, t] for t in range(classes)]

    def kept_coefs(j, t):
        return [ref[j, t] for ref in coefs]

    strip, now = first_strip, first_coefs
    for step in range(STEPS - 1):
        target = buffers[step % 2]

        def keep(j, _, new, target=target):
            for t in range(classes):
                target[j + 1, t] = new[t]

        advance(0, strips, classes, strip, now, keep)
        strip, now = kept_strip(target), kept_coefs
    last(strip, now)


def surpluses(s, prev, weights):
    fine, mid, low, coef = weights
    return (
        fine * (s[0] - 0.5 * (prev + s[1])),
        mid * (s[1] - 0.5 * (prev + s[3])),
        fine * (s[2] - 0.5 * (s[1] + s[3])),
        low * (s[3] - 0.5 * (prev + s[7])),
        fine * (s[4] - 0.5 * (s[3] + s[5])),
        mid * (s[5] - 0.5 * (s[3] + s[7])),
        fine * (s[6] - 0.5 * (s[5] + s[7])),
        coef * s[7],
    )


def ones_kernel(out_ref):
    out_ref[...] = jnp.ones(out_ref.shape, jnp.float32)


def weights_kernel(depth, level_ref, coef_ref, ones_ref, keep_ref, weight_ref):
    coef = coef_ref[0].astype(jnp.float32)
    for down in range(3):
        keep_ref[down] = jnp.where(level_ref[0] >= depth - down, ones_ref[...], 0.0)
        weight_ref[down] = coef * keep_ref[down]
    weight_ref[3] = coef * ones_ref[...]


def pack_kernel(dom_ref, weight_ref, dens_ref, diff_ref, drift_ref, near_ref, far_ref):
    del weight_ref
    many, strips = dens_ref.shape[:2]
    odd = dom_ref[0] % 2 == 1
    upper = lax.broadcasted_iota(jnp.int32, (TILE, LANES), 0) < HALF

    def body(j):
        drift_last = pltpu.roll(drift_ref[many - 1, j], HALF, 0)
        mix_next = jnp.where(upper, drift_last, diff_ref[many - 1, j])
        mix_prev = jnp.where(upper, diff_ref[0, j], pltpu.roll(drift_ref[0, j], HALF, 0))
        to_next, to_prev = (dens_ref[many - 1, j], mix_next), (dens_ref[0, j], mix_prev)
        for k in range(2):
            at = pl.ds(k * TILE, TILE)
            far_ref[j, at] = jnp.where(odd, to_next[k], to_prev[k])
            near_ref[j, at] = jnp.where(odd, to_prev[k], to_next[k])

    per_strip(strips, body, min(strips, UNROLL))


def middle_tiles(many):
    return list(range(many // 4, many - many // 4)) if many >= 4 else []


def outer_tiles(many):
    return [m for m in range(many) if m not in middle_tiles(many)]


def emit_tiles(tiles, per_chunk, scratch, out_ref, j, part, weighted, before):
    many = scratch.shape[1]
    by_row = flat(scratch)
    for t in range(TILE):
        by_row[spaced(j * many * TILE + t, many, TILE), :] = weighted[t]
    for k, m in enumerate(tiles):
        out_ref[part * len(tiles) + k] = scratch[j, m]
    last = per_chunk * len(tiles) + part // TILE
    out_ref[last, pl.ds(lax.rem(part, TILE), 1), :] = before


def inner_kernel(
    per_chunk, dom_ref, me_ref, weight_ref, dens_ref, diff_ref, drift_ref, state_ref, *refs
):
    many, strips = dens_ref.shape[:2]
    *out_refs, scratch, state_a, state_b = refs[:-4]
    coefs = refs[-4:]
    rows = [flat(ref) for ref in (dens_ref, diff_ref, drift_ref)]
    weights = [weight_ref[k] for k in range(4)]
    tiles = middle_tiles(many)

    def load(k, j, t):
        return rows[k][spaced(j * TILE + t, many, strips * TILE), :]

    def finish(out_ref, j, part, new):
        for t in range(TILE):
            state_ref[j, t] = new[t]
        if out_ref is not None:
            weighted = surpluses(new, roll_rows(new[7], 1), weights)
            before = weighted[7][tiles[0] - 1 : tiles[0]]
            emit_tiles(tiles, per_chunk, scratch, out_ref, j, part, weighted, before)

    def last(strip, now):
        for out_ref, away in zip(out_refs or [None] * SQUARE, partners(dom_ref[0])):
            first = (me_ref[0] ^ away) * per_chunk
            emit = functools.partial(finish, out_ref)
            advance(first, per_chunk, TILE, strip, now, emit)

    run_steps(strips, TILE, load, (state_a, state_b), coefs, last)


def partners(dom):
    return 0, 1 + dom % 2, 2 - dom % 2, 3


def edge_kernel(
    per_chunk, doms, dom_ref, me_ref, weight_ref, dens_ref, *refs
):
    many, strips = dens_ref.shape[:2]
    dom = dom_ref[0]
    odd = dom % 2 == 1
    diff_ref, drift_ref, state_ref, near_ref, far_ref, *rest = refs
    out_refs, (scratch, slab, state_a, state_b, *coefs) = rest[:-8], rest[-8:]

    def stage(j):
        far, near = far_ref[j], near_ref[j]
        up = jnp.where(dom == 0, 0.0, jnp.where(odd, near, far))
        dn = jnp.where(dom == doms - 1, 0.0, jnp.where(odd, far, near))
        up_mix, dn_mix = up[TILE:], dn[TILE:]
        tiles = (
            (up[:TILE], dens_ref[0, j], dens_ref[many - 1, j], dn[:TILE]),
            (up_mix, diff_ref[0, j], diff_ref[many - 1, j], dn_mix),
            (
                pltpu.roll(up_mix, HALF, 0),
                drift_ref[0, j],
                drift_ref[many - 1, j],
                pltpu.roll(dn_mix, HALF, 0),
            ),
        )
        for k, column in enumerate(tiles):
            for e, tile in enumerate(column):
                slab[k, j, e * TILE : (e + 1) * TILE] = tile

    per_strip(strips, stage, min(strips, UNROLL))
    slabs = flat(slab)

    def load(k, j, t):
        return slabs[pl.ds((k * strips + j) * SLAB + t, TILE, stride=HALF), :]

    place = lax.broadcasted_iota(jnp.int32, (many, LANES), 0)
    weights = [weight_ref[k] for k in range(4)]

    def finish(out_ref, j, part, new):
        s = [state_ref[j, t] for t in range(TILE)]
        for t in range(HALF):
            s[t] = jnp.where(place == 0, new[t][2:3], s[t])
            s[HALF + t] = jnp.where(place == many - 1, new[t][5:6], s[HALF + t])
        before = new[HALF - 1][1:2]
        weighted = surpluses(s, jnp.where(place == 0, before, roll_rows(s[7], 1)), weights)
        before = weights[3][0:1] * before
        tiles = outer_tiles(many)
        emit_tiles(tiles, per_chunk, scratch, out_ref, j, part, weighted, before)

    def last(strip, now):
        for out_ref, away in zip(out_refs, partners(dom_ref[0])):
            first = (me_ref[0] ^ away) * per_chunk
            emit = functools.partial(finish, out_ref)
            advance(first, per_chunk, HALF, strip, now, emit)

    run_steps(strips, HALF, load, (state_a, state_b), coefs, last)


def sum_kernel(*refs):
    *parts, out_ref = refs
    total = parts[0][...]
    for part in parts[1:]:
        total = total + part[...]
    out_ref[...] = total


def nodal_kernel(per_chunk, tiles, dom_ref, me_ref, keep_ref, *refs):
    totals, middles, (out_ref, values, sems) = refs[:SQUARE], refs[SQUARE:-3], refs[-3:]
    count = len(tiles)
    fine, mid, low = (keep_ref[k, 0:count] for k in range(3))
    place = lax.broadcasted_iota(jnp.int32, (count, LANES), 0)
    gaps = [k for k in range(1, count) if tiles[k] != tiles[k - 1] + 1]
    copies = []
    for k, (ref, away) in enumerate(zip(totals, partners(dom_ref[0]))):
        first = (me_ref[0] ^ away) * per_chunk
        by_row = flat(values.at[k])

        def body(part, k=k, ref=ref, by_row=by_row):
            w = [
                flat(ref)[spaced(part * count * TILE + t, count, TILE), :] for t in range(TILE)
            ]
            before = ref[per_chunk * count + part // TILE, pl.ds(lax.rem(part, TILE), 1), :]
            prev = jnp.where(place == 0, before, roll_rows(w[7], 1))
            for gap in gaps:
                across = tiles[gap] - tiles[gap - 1] - 1
                before = middles[k][part * across + across - 1, TILE - 1 : TILE, :]
                prev = jnp.where(place == gap, before, prev)
            v3 = 0.5 * (prev + w[7]) + low * w[3]
            v1 = 0.5 * (prev + v3) + mid * w[1]
            v5 = 0.5 * (v3 + w[7]) + mid * w[5]
            rows = (
                0.5 * (prev + v1) + fine * w[0],
                v1,
                0.5 * (v1 + v3) + fine * w[2],
                v3,
                0.5 * (v3 + v5) + fine * w[4],
                v5,
                0.5 * (v5 + w[7]) + fine * w[6],
                w[7],
            )
            for t in range(TILE):
                by_row[spaced(part * TILE + t, count, per_chunk * TILE), :] = rows[t]

        per_strip(per_chunk, body, min(per_chunk, 4))
        for e, m in enumerate(tiles):
            copy = pltpu.make_async_copy(
                values.at[k, e], out_ref.at[m, pl.ds(first, per_chunk)], sems.at[k, e]
            )
            copy.start()
            copies.append(copy)
    for copy in copies:
        copy.wait()


def call(
    kernel, out_shapes, operands, in_smem=0, scratch=(), flops=0, out_space=pltpu.VMEM, onto=None
):
    spaces = [pltpu.SMEM] * in_smem + [pltpu.VMEM] * (len(operands) - in_smem)
    alias = {}
    if onto is not None:
        alias = {len(operands): 0}
        spaces, operands = spaces + [out_space], (*operands, onto)
    specs = [pl.BlockSpec(memory_space=space) for space in spaces]
    moved = 4 * sum(x.size for x in operands)
    return pl.pallas_call(
        kernel,
        out_shape=[jax.ShapeDtypeStruct(shape, jnp.float32) for shape in out_shapes],
        in_specs=specs,
        out_specs=[pl.BlockSpec(memory_space=out_space) for _ in out_shapes],
        input_output_aliases=alias,
        scratch_shapes=list(scratch),
        compiler_params=pltpu.CompilerParams(vmem_limit_bytes=VMEM_LIMIT),
        cost_estimate=pl.CostEstimate(flops=flops, bytes_accessed=moved, transcendentals=0),
    )(*operands)


def on_device(density, diffusion, drift_speed, levels, coefficient):
    rows, cols = density.shape[1:]
    doms, grids = lax.axis_size("dom"), lax.axis_size("grp")
    many, strips = rows // TILE, cols // LANES
    per_chunk = strips // SQUARE
    depth = (rows * doms).bit_length() - 1
    tiles = [tiles_of(x[0]) for x in (density, diffusion, drift_speed)]
    me = (lax.axis_index("grp") % SQUARE).astype(jnp.int32)[None]
    dom = lax.axis_index("dom").astype(jnp.int32)[None]

    def vmem(*shape):
        return pltpu.VMEM(shape, jnp.float32)

    near_pairs = [(d, d ^ 1) for d in range(doms)]
    far_pairs = [(d, min(max((d - 1 ^ 1) + 1, 0), doms - 1)) for d in range(doms)]
    (ones,) = call(ones_kernel, [(many, LANES)], (), flops=LOAD_FLOPS * rows * cols)
    keep, weight = call(
        functools.partial(weights_kernel, depth),
        [(3, many, LANES), (4, many, LANES)],
        (levels, coefficient, ones),
        2,
    )
    near, far = call(
        pack_kernel,
        [(strips, 2 * TILE, LANES)] * 2,
        (dom, weight, *tiles),
        1,
    )
    near = lax.ppermute(near, "dom", near_pairs)
    far = lax.ppermute(far, "dom", far_pairs)
    place = (strips, TILE, many, LANES)
    pieces = (strips, many, TILE, LANES)

    def chunk(tiles):
        return per_chunk * len(tiles) + -(-per_chunk // TILE), TILE, LANES

    middle, outer = middle_tiles(many), outer_tiles(many)
    state, *inside = call(
        functools.partial(inner_kernel, per_chunk),
        [place] + [chunk(middle)] * (SQUARE if middle else 0),
        (dom, me, weight, *tiles),
        2,
        [vmem(*pieces)] + [vmem(strips + 2, *place[1:])] * 2 + [vmem(*place)] * 4,
        flops=40 * rows * cols,
    )
    outside = call(
        functools.partial(edge_kernel, per_chunk, doms),
        [chunk(outer)] * SQUARE,
        (dom, me, weight, *tiles, state, near, far),
        2,
        [vmem(*pieces), vmem(3, strips, SLAB, LANES)]
        + [vmem(strips + 2, HALF, TILE, LANES)] * 2
        + [vmem(strips, HALF, TILE, LANES)] * 4,
        flops=40 * SLAB * cols,
    )

    def swap(array, meet):
        devices = [(g, d) for g in range(grids) for d in range(doms)]
        pairs = [(g * doms + d, (g ^ partners(d % 2)[meet]) * doms + d) for g, d in devices]
        return lax.ppermute(array, ("grp", "dom"), pairs)

    def over_grids(own, *others):
        theirs = [swap(others[meet - 1], meet) for meet in (3, 1, 2)]
        (total,) = call(sum_kernel, [own.shape], (own, *theirs))
        apart = SQUARE
        while apart < grids:
            other = lax.ppermute(total, "grp", [(g, g ^ apart) for g in range(grids)])
            (total,) = call(sum_kernel, [own.shape], (total, other))
            apart *= 2
        return [total] + [swap(total, meet) for meet in range(1, SQUARE)]

    nodal, totals = None, []
    for some, weighted in ((middle, inside), (outer, outside)):
        if not some:
            continue
        totals = over_grids(*weighted) + totals
        (nodal,) = call(
            functools.partial(nodal_kernel, per_chunk, some),
            [(many, strips, TILE, LANES)],
            (dom, me, keep, *totals),
            2,
            [
                vmem(SQUARE, len(some), per_chunk, TILE, LANES),
                pltpu.SemaphoreType.DMA((SQUARE, len(some))),
            ],
            out_space=pl.ANY,
            onto=nodal,
        )
    return block_of(nodal)[None]


def solution(mesh):
    return jax.shard_map(
        on_device,
        mesh=mesh,
        in_specs=(
            P("grp", "dom", None),
            P("grp", "dom", None),
            P("grp", "dom", None),
            P("grp"),
            P("grp"),
        ),
        out_specs=P("grp", "dom", None),
        check_vma=False,
    )
```
